32 devices in a mesh: gx: 2 (over y), gy: 8 (over z, core), gz: 2 (over x).
Axes of the slice: x: 2, y: 2, z: 4, core: 2. Of those that a mesh axis runs over, the one named last changes fastest.
Arguments:
- velocity: float32 [3, 256, 256, 256], P(None, 'gx', 'gy', 'gz'), may hold values from -6 to 6
- adjoint_seed: float32 [3, 256, 256, 256], P(None, 'gx', 'gy', 'gz'), may hold values from -6 to 6
- susceptibility: float32 [256, 256, 256], P('gx', 'gy', 'gz'), may hold values from 0.5 to 4
- remanence: float32 [256, 256, 256], P('gx', 'gy', 'gz'), may hold values from 0.2 to 1.5
- region_bounds: int32 [2, 3], replicated, may hold values from 0 to 128, as said below
- step_id: int32 [1], replicated, may hold values from 0 to 999
Outputs:
- next_velocity: float32 [3, 256, 256, 256], P(None, 'gx', 'gy', 'gz')
- velocity_adjoint: float32 [3, 256, 256, 256], P(None, 'gx', 'gy', 'gz')
- design_gradient: float32 [256, 256, 256], P('gx', 'gy', 'gz')
The draws below stay inside these ranges and needn't reach their ends.
Inputs may be any that keep to these rules, and one draw needn't show every extreme that they name: Along every dimension the design region is nonempty and lies in the lower half of the box: region_bounds[0, d] < region_bounds[1, d] <= half the cells along d.
All inputs are finite; a program needn't handle non-finite values.
Results may differ from the reference program's by a relative error of at most 0.000096.
Values sent between devices are 32-bit elements; how exact they have to be, the bound alone decides.
No kernel may reach another device: no remote copies, remote signals or barrier semaphores. Data moves between devices by JAX's collectives and lax.ppermute only.
A program may use at most 320 MiB of HBM per device.

```python
import math
import jax
import jax.numpy as jnp

NX = 256
NY = 256
NZ = 256


def draw_region_bounds(key, part):
    first_key, second_key = jax.random.split(jax.random.fold_in(key, 11))
    lengths = jnp.array([NX, NY, NZ], dtype=jnp.int32)
    lower = jax.random.randint(first_key, (3,), 0, lengths // 8 + 1)
    upper = jax.random.randint(second_key, (3,), 3 * lengths // 8, lengths // 2 + 1)
    lower = lower.at[0].set(0)
    upper = upper.at[0].set(NX // 2)
    return jnp.stack([lower, upper]).astype(jnp.int32)


def levels(stream_key, extent, pieces, low, high):
    def one(position, shards_of):
        heights = jax.random.uniform(jax.random.fold_in(jax.random.fold_in(stream_key, 6), position), (shards_of,), jnp.float32, low / len(pieces), high / len(pieces))
        return jnp.repeat(jnp.exp(heights), extent[position] // shards_of).reshape((-1,) + (1,) * (len(extent) - position - 1))

    level = one(*pieces[0])
    for cut in pieces[1:]:
        level = level * one(*cut)
    return level


def noise(stream_key, extent, scale, bound, pieces=(), held_as=jnp.bfloat16):
    loudness = levels(stream_key, extent, pieces, -0.22, 0.18) if pieces else 1.0
    values = jax.random.normal(stream_key, extent, jnp.float32) * scale * loudness
    return jnp.minimum(jnp.maximum(values, -bound), bound).astype(held_as)


def setup_inputs(seed: int = 0) -> dict:
    key_list = jax.random.split(jax.random.key(seed), 7)
    velocity = noise(key_list[0], (3, NX, NY, NZ), 1.0, 6.0, ((1, 2), (2, 8), (3, 2)), jnp.float32)
    adjoint_seed = noise(key_list[1], (3, NX, NY, NZ), 1.0, 6.0, ((1, 2), (2, 8), (3, 2)), jnp.float32)
    susceptibility = jnp.clip(jnp.exp(math.log(4.0) - 2.0794415 * jax.random.uniform(key_list[2], (NX, NY, NZ), jnp.float32) ** levels(key_list[2], (NX, NY, NZ), ((0, 2), (1, 8), (2, 2)), -0.2, 0.2)), 0.5, 4.0)
    remanence = jnp.clip(0.2 + 1.3 * jax.random.uniform(key_list[3], (NX, NY, NZ), jnp.float32) ** levels(key_list[3], (NX, NY, NZ), ((0, 2), (1, 8), (2, 2)), -0.2, 0.2), 0.2, 1.5)
    region_bounds = draw_region_bounds(jax.random.fold_in(key_list[6], 71), 0)
    step_id = jax.random.randint(key_list[5], (1,), 0, 1000).astype(jnp.int32)
    return dict(velocity=velocity, adjoint_seed=adjoint_seed, susceptibility=susceptibility, remanence=remanence, region_bounds=region_bounds, step_id=step_id)


time_step = 0.5
viscosity = 0.2
field_period = 24
full_turn = 6.283185307179586


def folded_wave(length):
    cell_index = jnp.arange(length, dtype=jnp.int32)
    folded = jnp.where(cell_index < length // 2, cell_index, cell_index - length)
    return folded, full_turn * folded.astype(jnp.float32) / length


def kernel_set():
    fold_first, wave_first = folded_wave(NX)
    fold_second, wave_second = folded_wave(NY)
    fold_third, wave_third = folded_wave(NZ)
    fold_first, wave_first = fold_first[:, None, None], wave_first[:, None, None]
    fold_second, wave_second = fold_second[None, :, None], wave_second[None, :, None]
    fold_third, wave_third = fold_third[None, None, :], wave_third[None, None, :]
    anchor = (fold_first == 0) & (fold_second == 0) & (fold_third == 0)
    square = wave_first * wave_first + wave_second * wave_second + wave_third * wave_third
    safe_square = jnp.where(anchor, 1.0, square)
    return [jnp.where(anchor, 0.0, -(component_wave * wave_third) / safe_square) for component_wave in (wave_first, wave_second, wave_third)]


def region_mask_of(region_bounds):
    masks = []
    for axis_number, length in enumerate((NX, NY, NZ)):
        positions = jnp.arange(length, dtype=jnp.int32)
        masks.append((positions >= region_bounds[0, axis_number]) & (positions < region_bounds[1, axis_number]))
    joined = masks[0][:, None, None] & masks[1][None, :, None] & masks[2][None, None, :]
    return joined.astype(jnp.float32)


def central_slope(padded, axis_number):
    if axis_number == 0:
        return (padded[..., 2:, 1:-1, 1:-1] - padded[..., :-2, 1:-1, 1:-1]) * 0.5
    if axis_number == 1:
        return (padded[..., 1:-1, 2:, 1:-1] - padded[..., 1:-1, :-2, 1:-1]) * 0.5
    return (padded[..., 1:-1, 1:-1, 2:] - padded[..., 1:-1, 1:-1, :-2]) * 0.5


def laplace(padded):
    beside = padded[..., 2:, 1:-1, 1:-1] + padded[..., :-2, 1:-1, 1:-1]
    beside = beside + padded[..., 1:-1, 2:, 1:-1] + padded[..., 1:-1, :-2, 1:-1]
    beside = beside + padded[..., 1:-1, 1:-1, 2:] + padded[..., 1:-1, 1:-1, :-2]
    return beside - 6.0 * padded[..., 1:-1, 1:-1, 1:-1]


def pad_cells(field):
    widths = [(0, 0)] * (field.ndim - 3) + [(1, 1), (1, 1), (1, 1)]
    return jnp.pad(field, widths)


def reference(velocity, adjoint_seed, susceptibility, remanence, region_bounds, step_id):
    region_mask = region_mask_of(region_bounds)
    magnet = remanence * region_mask
    kernels = kernel_set()
    spectrum = jnp.fft.fftn(magnet)
    demag_field = jnp.stack([jnp.real(jnp.fft.ifftn(kernel * spectrum)) for kernel in kernels])
    phase_angle = full_turn * (step_id[0] % field_period).astype(jnp.float32) / field_period
    applied = jnp.stack([jnp.cos(phase_angle), jnp.sin(phase_angle), jnp.zeros((), jnp.float32)])
    total_field = demag_field + applied[:, None, None, None]
    energy = 0.5 * jnp.sum(total_field * total_field, axis=0)
    padded_energy = pad_cells(energy)
    padded_velocity = pad_cells(velocity)
    padded_seed = pad_cells(adjoint_seed)
    padded_suscept = pad_cells(susceptibility)
    advect = jnp.stack([velocity[0] * central_slope(padded_velocity[comp], 0) + velocity[1] * central_slope(padded_velocity[comp], 1) + velocity[2] * central_slope(padded_velocity[comp], 2) for comp in range(3)])
    pushed = jnp.stack([susceptibility * central_slope(padded_energy, axis_number) for axis_number in range(3)])
    next_velocity = velocity + time_step * (viscosity * laplace(padded_velocity) - advect + pushed)
    flux_terms = padded_suscept[None] * padded_seed
    source = central_slope(flux_terms[0], 0) + central_slope(flux_terms[1], 1) + central_slope(flux_terms[2], 2)
    source = -time_step * source
    field_adjoint = source[None] * total_field
    combined = kernels[0] * jnp.fft.fftn(field_adjoint[0]) + kernels[1] * jnp.fft.fftn(field_adjoint[1]) + kernels[2] * jnp.fft.fftn(field_adjoint[2])
    magnet_adjoint = jnp.real(jnp.fft.ifftn(combined))
    design_gradient = region_mask * magnet_adjoint
    shear_terms = jnp.stack([adjoint_seed[0] * central_slope(padded_velocity[0], comp) + adjoint_seed[1] * central_slope(padded_velocity[1], comp) + adjoint_seed[2] * central_slope(padded_velocity[2], comp) for comp in range(3)])
    carried = jnp.stack([central_slope(padded_velocity[0] * padded_seed[comp], 0) + central_slope(padded_velocity[1] * padded_seed[comp], 1) + central_slope(padded_velocity[2] * padded_seed[comp], 2) for comp in range(3)])
    velocity_adjoint = adjoint_seed + time_step * (viscosity * laplace(padded_seed) - shear_terms + carried)
    return next_velocity, velocity_adjoint, design_gradient
```

```python
import functools
import math

import jax
import jax.numpy as jnp
import ml_dtypes
import numpy as np
from jax import lax
from jax.experimental import pallas as pl
from jax.experimental.pallas import tpu as pltpu
from jax.sharding import PartitionSpec as P

time_step = 0.5
viscosity = 0.2
field_period = 24
full_turn = 2.0 * math.pi
bf16 = ml_dtypes.bfloat16
axes = ("gx", "gy", "gz")


def wave_tables(length):
    half = length // 2
    slot = np.arange(length)
    wave = np.where(slot <= half, slot, slot - half)
    angle = full_turn * (wave[:, None] * np.arange(length)[None, :] % length) / length
    weight = np.sqrt(np.where(slot % half == 0, 1.0, 2.0) / length)[:, None]
    odd = (slot > half)[:, None]
    kappa = full_turn * wave / length
    basis = np.where(odd, np.sin(angle), np.cos(angle)) * weight
    slope = np.where(odd, np.cos(angle), -np.sin(angle)) * weight * kappa[:, None]
    slope[half] = 0.0
    return basis, slope, kappa


def two_parts(table):
    high = table.astype(bf16)
    low = (table - high.astype(np.float64)).astype(bf16)
    return high, low


def split(value):
    high = value.astype(jnp.bfloat16)
    low = (value - high.astype(jnp.float32)).astype(jnp.bfloat16)
    return high, low


def dot(left, right):
    return jnp.dot(left, right, preferred_element_type=jnp.float32)


def own_rows(table, axis, count):
    return lax.dynamic_slice_in_dim(jnp.asarray(table), lax.axis_index(axis) * count, count, 0)


def own_cols(table, axis, count):
    return lax.dynamic_slice_in_dim(jnp.asarray(table), lax.axis_index(axis) * count, count, 1)


class Plan:
    def __init__(self, mesh, local):
        self.gx, self.gy, self.gz = (mesh.shape[a] for a in axes)
        self.xl, self.yl, self.zl = local
        self.nx, self.ny, self.nz = self.xl * self.gx, self.yl * self.gy, self.zl * self.gz
        self.x2, self.y2, self.z2 = self.nx // 2, self.ny // 2, self.nz // 2
        self.px, self.py = self.xl // 4, self.yl // 2

    def piece_rows(self, y):
        across, inside = lax.div(y, self.py), lax.rem(y, self.py)
        runs = []
        for depth in range(self.gz // 2):
            runs.append([])
            for first in range(self.gx):
                for side in range(2):
                    piece = (first * self.gy + across) * self.gz + 2 * depth + side
                    runs[-1].append(piece * (self.px * self.py) + inside)
        return runs


def forward_tables(plan):
    bx, dx, wx = wave_tables(plan.nx)
    by, dy, wy = wave_tables(plan.ny)
    bz, dz, wz = wave_tables(plan.nz)
    hx, hy, hz = plan.nx // 2, plan.ny // 2, plan.nz // 2
    ez = bz.copy()
    ez[0] = bz[hz]
    z1 = dz.copy()
    z1[0] = 0.0
    z2 = dz.copy()
    z2[0] = -(np.pi**2) * bz[hz]
    z3 = -(wz**2)[:, None] * bz
    z3[0] = 0.0
    z1n = np.zeros_like(z1)
    z1n[hz] = -np.pi * bz[hz]
    xs = dx.copy()
    xs[hx] = np.pi * bx[hx]
    w3 = wz.copy()
    w3[0] = np.pi
    base = wy[:, None] ** 2 + w3[None, :] ** 2
    keep = np.ones_like(base, bool)
    keep[:, 0] = False
    keep[hy, 0] = True
    base = np.where(keep, base, 1e30).astype(np.float32)
    return dict(
        fx=bx[:, : plan.x2],
        ez=ez[:, : plan.z2],
        fy=by[:, : plan.y2],
        by=by,
        dy=dy,
        bx=bx,
        xs=xs,
        z1=z1,
        z2=z2,
        z3=z3,
        z1n=z1n,
        base=base,
        w1=(wx**2).astype(np.float32),
    )


def pair_lanes(a, b):
    return jnp.concatenate([a, b], axis=1)


def pair_rows(a, b):
    return jnp.concatenate([a, b], axis=0)


def load_plane(ref, plan, y):
    blocks = [
        [ref[pl.ds(start, plan.px, stride=plan.py), :] for start in runs]
        for runs in plan.piece_rows(y)
    ]
    blocks = [jnp.concatenate(rows, axis=0) for rows in blocks]
    return blocks[0] if len(blocks) == 1 else jnp.concatenate(blocks, axis=1)


def store_plane(ref, plan, y, value):
    for depth, runs in enumerate(plan.piece_rows(y)):
        for place, start in enumerate(runs):
            ref[pl.ds(start, plan.px, stride=plan.py), :] = value[
                place * plan.px : (place + 1) * plan.px, depth * plan.zl : (depth + 1) * plan.zl
            ]


def field_body(
    plan, w1_ref, app_ref, m_ref, src_ref, fx_ref, fxl_ref, ez_ref, ezl_ref, fy_ref, fyl_ref,
    g_ref, z13_ref, z13l_ref, z2_ref, z1n_ref, xs_ref, xb_ref, base_ref,
    f_ref, e_ref, s_ref, r_ref, kern_ref,
):
    nx, hx, y2, z2, xl, yl, zl = plan.nx, plan.nx // 2, plan.y2, plan.z2, plan.xl, plan.yl, plan.zl
    span, block = yl * nx, xl * yl

    def along_x(pair, carry):
        plane = pair_lanes(load_plane(m_ref, plan, 2 * pair), load_plane(m_ref, plan, 2 * pair + 1))
        high, low = split(plane)
        out = dot(fx_ref[...], pair_rows(high, low)) + dot(fxl_ref[...], high)
        s_ref[pl.ds(2 * pair * nx, nx), :] = out[:, :z2]
        s_ref[pl.ds((2 * pair + 1) * nx, nx), :] = out[:, z2:]
        return carry

    lax.fori_loop(0, y2 // 2, along_x, 0)

    def one_slab(plane, kern):
        high, low = split(plane)
        spectrum = dot(fy_ref[...], pair_rows(high, low)) + dot(fyl_ref[...], high)
        high, low = split(spectrum * kern)
        both = dot(g_ref[...], high)
        return both[: 2 * yl] + both[2 * yl :] + dot(g_ref[: 2 * yl], low)

    def slabs(i, edge):
        rows = pair_rows(
            s_ref[pl.ds(i, y2, stride=nx), :], s_ref[pl.ds(i + hx, y2, stride=nx), :]
        )
        high, low = split(rows)
        planes = dot(pair_lanes(high, low), ez_ref[...]) + dot(high, ezl_ref[...])
        kern_ref[...] = 1.0 / (base_ref[...] + w1_ref[i])
        even = one_slab(planes[:y2], kern_ref[...])
        if edge:
            kern_ref[...] = 1.0 / (base_ref[...] + w1_ref[hx])
        odd = one_slab(planes[y2:], kern_ref[...])
        q1 = pair_rows(even[:yl], odd[:yl])
        q2 = pair_rows(even[yl:], odd[yl:])
        lane = lax.broadcasted_iota(jnp.int32, q1.shape, 1)
        q2 = jnp.where(lane == 0, q1, q2)
        high, low = split(q1)
        r13 = dot(high, z13_ref[...]) + dot(low, z13_ref[...]) + dot(high, z13l_ref[...])
        high2, low2 = split(q2)
        r2 = dot(high2, z2_ref[...])
        r2 = r2[:, :zl] + r2[:, zl:] + dot(low2, z2_ref[:, :zl])
        for part, slot in ((0, i), (1, i + hx)):
            take = slice(part * yl, (part + 1) * yl)
            r1 = r13[take, :zl]
            if edge and part == 1:
                r1 = dot(high[yl:], z1n_ref[...])
                r1 = r1[:, :zl] + r1[:, zl:] + dot(low[yl:], z1n_ref[:, :zl])
            r_ref[pl.ds(slot, yl, stride=nx), :] = r1
            r_ref[pl.ds(span + slot, yl, stride=nx), :] = r2[take]
            r_ref[pl.ds(2 * span + slot, yl, stride=nx), :] = r13[take, zl:]

    def later_slabs(i, carry):
        slabs(i, False)
        return carry

    slabs(0, True)
    lax.fori_loop(1, hx, later_slabs, 0)

    def back_x(mat_ref, values):
        high, low = split(values)
        both = dot(mat_ref[...], high)
        return both[:xl] + both[xl:] + dot(mat_ref[:xl], low)

    def cells(pair, carry):
        here = [[pl.ds(j * span + (2 * pair + k) * nx, nx) for k in range(2)] for j in range(3)]
        h1 = back_x(xs_ref, pair_lanes(r_ref[here[0][0], :], r_ref[here[0][1], :]))
        for k in range(2):
            h23 = back_x(xb_ref, pair_lanes(r_ref[here[1][k], :], r_ref[here[2][k], :]))
            t1 = h1[:, k * zl : (k + 1) * zl] + app_ref[0]
            t2 = h23[:, :zl] + app_ref[1]
            t3 = h23[:, zl:]
            out = pl.ds(2 * pair + k, xl, stride=yl)
            source = src_ref[out, :]
            e_ref[out, :] = 0.5 * (t1 * t1 + t2 * t2 + t3 * t3)
            f_ref[pl.ds(2 * pair + k, xl, stride=yl), :] = source * t1
            f_ref[pl.ds(block + 2 * pair + k, xl, stride=yl), :] = source * t2
            f_ref[pl.ds(2 * block + 2 * pair + k, xl, stride=yl), :] = source * t3
        return carry

    lax.fori_loop(0, yl // 2, cells, 0)


def adjoint_body(
    plan, w1_ref, f_ref, xs_ref, xsl_ref, xb_ref, xbl_ref, z13_ref, z13l_ref, z2_ref, z2l_ref, z1n_ref, z1nl_ref,
    g_ref, fy_ref, ez_ref, fx_ref, base_ref,
    m_ref, s_ref, r_ref, kern_ref,
):
    nx, hx, y2, z2, xl, yl, zl = plan.nx, plan.nx // 2, plan.y2, plan.z2, plan.xl, plan.yl, plan.zl
    span, block = yl * nx, xl * yl

    def along_x(mat_ref, low_ref, values):
        high, low = split(values)
        return dot(mat_ref[...], pair_rows(high, low)) + dot(low_ref[...], high)

    def cells(pair, carry):
        here = [[pl.ds(j * block + 2 * pair + k, xl, stride=yl) for k in range(2)] for j in range(3)]
        u1 = along_x(xs_ref, xsl_ref, pair_lanes(f_ref[here[0][0], :], f_ref[here[0][1], :]))
        for k in range(2):
            u23 = along_x(xb_ref, xbl_ref, pair_lanes(f_ref[here[1][k], :], f_ref[here[2][k], :]))
            row = (2 * pair + k) * nx
            r_ref[pl.ds(row, nx), :] = u1[:, k * zl : (k + 1) * zl]
            r_ref[pl.ds(span + row, nx), :] = u23[:, :zl]
            r_ref[pl.ds(2 * span + row, nx), :] = u23[:, zl:]
        return carry

    lax.fori_loop(0, yl // 2, cells, 0)

    def one_slab(q, kern):
        high, low = split(q)
        spectrum = dot(g_ref[...], jnp.concatenate([high, high, low], axis=0))
        high, low = split(spectrum * kern)
        both = dot(fy_ref[...], high)
        return both[:y2] + both[y2:] + dot(fy_ref[:y2], low)

    def slabs(i, edge):
        u = [
            pair_rows(
                r_ref[pl.ds(j * span + i, yl, stride=nx), :],
                r_ref[pl.ds(j * span + i + hx, yl, stride=nx), :],
            )
            for j in range(3)
        ]
        high1, low1 = split(u[0])
        high3, low3 = split(u[2])
        high, low = pair_lanes(high1, high3), pair_lanes(low1, low3)
        q1 = dot(high, z13_ref[...]) + dot(low, z13_ref[...]) + dot(high, z13l_ref[...])
        if edge:
            mid = dot(pair_lanes(high1, low1), z1n_ref[...]) + dot(high1, z1nl_ref[...])
            q1 = pair_rows(q1[:yl], q1[yl:] + mid[yl:])
        high2, low2 = split(u[1])
        q2 = dot(pair_lanes(high2, low2), z2_ref[...]) + dot(high2, z2l_ref[...])
        first = lax.broadcasted_iota(jnp.int32, q1.shape, 1) == 0
        q1, q2 = jnp.where(first, q2, q1), jnp.where(first, 0.0, q2)
        kern_ref[...] = 1.0 / (base_ref[...] + w1_ref[i])
        even = one_slab(pair_rows(q1[:yl], q2[:yl]), kern_ref[...])
        if edge:
            kern_ref[...] = 1.0 / (base_ref[...] + w1_ref[hx])
        odd = one_slab(pair_rows(q1[yl:], q2[yl:]), kern_ref[...])
        high, low = split(pair_rows(even, odd))
        out = dot(high, ez_ref[...])
        out = out[:, :z2] + out[:, z2:] + dot(low, ez_ref[:, :z2])
        s_ref[pl.ds(i, y2, stride=nx), :] = out[:y2]
        s_ref[pl.ds(i + hx, y2, stride=nx), :] = out[y2:]

    def later_slabs(i, carry):
        slabs(i, False)
        return carry

    slabs(0, True)
    lax.fori_loop(1, hx, later_slabs, 0)

    def back_x(pair, carry):
        planes = pair_lanes(
            s_ref[pl.ds(2 * pair * nx, nx), :], s_ref[pl.ds((2 * pair + 1) * nx, nx), :]
        )
        high, low = split(planes)
        both = dot(fx_ref[...], high)
        out = both[: plan.x2] + both[plan.x2 :] + dot(fx_ref[: plan.x2], low)
        store_plane(m_ref, plan, 2 * pair, out[:, :z2])
        store_plane(m_ref, plan, 2 * pair + 1, out[:, z2:])
        return carry

    lax.fori_loop(0, y2 // 2, back_x, 0)


def spread(block, axis, dim):
    count = lax.axis_size(axis)
    halves = jnp.split(block, 2, axis=dim)
    moved = [
        lax.ppermute(half, axis, [(s, 2 * s + k) for s in range(count // 2)])
        for k, half in enumerate(halves)
    ]
    return moved[0] + moved[1]


def unspread(piece, axis, dim):
    count = lax.axis_size(axis)
    moved = [
        lax.ppermute(piece, axis, [(2 * s + k, s) for s in range(count // 2)]) for k in range(2)
    ]
    return jnp.concatenate(moved, axis=dim)


def halves_of(high_low, axis=0):
    return np.concatenate(high_low, axis=axis)


vmem = pl.BlockSpec(memory_space=pltpu.VMEM)
smem = pl.BlockSpec(memory_space=pltpu.SMEM)
kernel_params = pltpu.CompilerParams(vmem_limit_bytes=60 * 2**20)


def scratch_of(plan):
    return [
        pltpu.VMEM((plan.y2 * plan.nx, plan.z2), jnp.float32),
        pltpu.VMEM((3 * plan.yl * plan.nx, plan.zl), jnp.float32),
        pltpu.VMEM((plan.ny, plan.nz), jnp.float32),
    ]


def field_call(plan, tables, magnet, source, applied):
    t = tables
    xl, yl, zl = plan.xl, plan.yl, plan.zl

    def cat(*arrays):
        return jnp.concatenate(arrays, axis=0)

    fx, fxl = two_parts(t["fx"])
    ez, ezl = two_parts(t["ez"].T)
    fy, fyl = two_parts(t["fy"])
    g1, g1l = [own_rows(p, "gy", yl) for p in two_parts(t["by"].T)]
    g2, g2l = [own_rows(p, "gy", yl) for p in two_parts(t["dy"].T)]
    z1, z1l = [own_cols(p, "gz", zl) for p in two_parts(t["z1"])]
    z2, z2l = [own_cols(p, "gz", zl) for p in two_parts(t["z2"])]
    z3, z3l = [own_cols(p, "gz", zl) for p in two_parts(t["z3"])]
    z1n, z1nl = [own_cols(p, "gz", zl) for p in two_parts(t["z1n"])]
    xs, xsl = [own_rows(p, "gx", xl) for p in two_parts(t["xs"].T)]
    xb, xbl = [own_rows(p, "gx", xl) for p in two_parts(t["bx"].T)]
    rows = xl * yl
    return pl.pallas_call(
        functools.partial(field_body, plan),
        out_shape=[
            jax.ShapeDtypeStruct((3 * rows, zl), jnp.float32),
            jax.ShapeDtypeStruct((rows, zl), jnp.float32),
        ],
        in_specs=[smem, smem] + [vmem] * 16,
        out_specs=[vmem, vmem],
        scratch_shapes=scratch_of(plan),
        compiler_params=kernel_params,
    )(
        jnp.asarray(t["w1"]), applied, magnet.reshape(-1, zl), source.reshape(rows, zl),
        np.concatenate([fx, fx], axis=1), fxl, np.concatenate([ez, ez]), ezl, np.concatenate([fy, fy], axis=1), fyl,
        cat(g1, g2, g1l, g2l), pair_lanes(z1, z3), pair_lanes(z1l, z3l), pair_lanes(z2, z2l),
        pair_lanes(z1n, z1nl), cat(xs, xsl), cat(xb, xbl), jnp.asarray(t["base"]),
    )


def adjoint_call(plan, tables, field):
    t = tables
    xl, yl, zl = plan.xl, plan.yl, plan.zl

    def cat(*arrays):
        return jnp.concatenate(arrays, axis=0)

    xs, xsl = [own_cols(p, "gx", xl) for p in two_parts(t["xs"])]
    xb, xbl = [own_cols(p, "gx", xl) for p in two_parts(t["bx"])]
    z1, z1l = [own_rows(p, "gz", zl) for p in two_parts(t["z1"].T)]
    z2, z2l = [own_rows(p, "gz", zl) for p in two_parts(t["z2"].T)]
    z3, z3l = [own_rows(p, "gz", zl) for p in two_parts(t["z3"].T)]
    z1n, z1nl = [own_rows(p, "gz", zl) for p in two_parts((t["z1n"] - t["z1"]).T)]
    g1, g1l = [own_cols(p, "gy", yl) for p in two_parts(t["by"])]
    g2, g2l = [own_cols(p, "gy", yl) for p in two_parts(t["dy"])]
    fy, fyl = two_parts(t["fy"].T)
    ez, ezl = two_parts(t["ez"])
    fx, fxl = two_parts(t["fx"].T)
    return pl.pallas_call(
        functools.partial(adjoint_body, plan),
        out_shape=jax.ShapeDtypeStruct((plan.x2 * plan.y2 * plan.z2 // zl, zl), jnp.float32),
        in_specs=[smem] + [vmem] * 16,
        out_specs=vmem,
        scratch_shapes=scratch_of(plan),
        compiler_params=kernel_params,
    )(
        jnp.asarray(t["w1"]), field,
        pair_lanes(xs, xs), xsl, pair_lanes(xb, xb), xbl, cat(z1, z3), cat(z1l, z3l), cat(z2, z2), z2l, cat(z1n, z1n), z1nl,
        jnp.concatenate([g1, g2, g1l, g2l, g1, g2], axis=1), np.concatenate([fy, fyl]),
        np.concatenate([ez, ezl], axis=1), np.concatenate([fx, fxl]), jnp.asarray(t["base"]),
    )


def lanes_of(count):
    return -(-count // 128) * 128


def faces_body(chunk, v_ref, a_ref, c_ref, ylo_ref, yhi_ref, zlo_ref, zhi_ref):
    yl, zl = v_ref.shape[2:]
    step = pl.program_id(0)

    @pl.when(step == 0)
    def _():
        zlo_ref[...] = jnp.zeros_like(zlo_ref)
        zhi_ref[...] = jnp.zeros_like(zhi_ref)

    lane = lax.broadcasted_iota(jnp.int32, zlo_ref.shape[1:], 1)
    for field in range(7):
        low, high = zlo_ref[field], zhi_ref[field]
        for k in range(chunk):
            plane = v_ref[field, k] if field < 3 else a_ref[field - 3, k] if field < 6 else c_ref[k]
            ylo_ref[field, k : k + 1, :] = plane[:1]
            yhi_ref[field, k : k + 1, :] = plane[yl - 1 :]
            here = lane == step * chunk + k
            low = jnp.where(here, plane[:, :1], low)
            high = jnp.where(here, plane[:, zl - 1 :], high)
        zlo_ref[field] = low
        zhi_ref[field] = high


def faces_call(velocity, adjoint_seed, susceptibility):
    xl, yl, zl = susceptibility.shape
    chunk = 8
    three = pl.BlockSpec((3, chunk, yl, zl), lambda i: (0, i, 0, 0))
    y_spec = pl.BlockSpec((7, chunk, zl), lambda i: (0, i, 0))
    z_spec = pl.BlockSpec((7, yl, lanes_of(max(xl, zl))), lambda i: (0, 0, 0))
    y_shape = jax.ShapeDtypeStruct((7, xl, zl), jnp.float32)
    z_shape = jax.ShapeDtypeStruct((7, yl, lanes_of(max(xl, zl))), jnp.float32)
    return pl.pallas_call(
        functools.partial(faces_body, chunk),
        grid=(xl // chunk,),
        in_specs=[three, three, pl.BlockSpec((chunk, yl, zl), lambda i: (i, 0, 0))],
        out_specs=[y_spec, y_spec, z_spec, z_spec],
        out_shape=[y_shape, y_shape, z_shape, z_shape],
        compiler_params=kernel_params,
    )(velocity, adjoint_seed, susceptibility)


def to_neighbours(low_face, high_face, axis):
    count = lax.axis_size(axis)
    below = lax.ppermute(high_face, axis, [(i, i + 1) for i in range(count - 1)])
    above = lax.ppermute(low_face, axis, [(i + 1, i) for i in range(count - 1)])
    return below, above


class Around:
    def __init__(self, ref, k, x, y_below, y_above, z_below, z_above):
        mid = ref[k + 1]
        yl, zl = mid.shape
        row = lax.broadcasted_iota(jnp.int32, mid.shape, 0)
        lane = lax.broadcasted_iota(jnp.int32, mid.shape, 1)
        width = z_below.shape[1]
        left = pltpu.roll(z_below, lax.rem(width - x, width), 1)[:, :zl]
        right = pltpu.roll(z_above, lax.rem(width + zl - 1 - x, width), 1)[:, :zl]
        self.mid = mid
        self.less = [
            ref[k],
            jnp.where(row == 0, y_below, pltpu.roll(mid, 1, 0)),
            jnp.where(lane == 0, left, pltpu.roll(mid, 1, 1)),
        ]
        self.more = [
            ref[k + 2],
            jnp.where(row == yl - 1, y_above, pltpu.roll(mid, yl - 1, 0)),
            jnp.where(lane == zl - 1, right, pltpu.roll(mid, zl - 1, 1)),
        ]

    def slope(self, d):
        return (self.more[d] - self.less[d]) * 0.5

    def laplace(self):
        beside = self.more[0] + self.less[0] + self.more[1] + self.less[1]
        return beside + self.more[2] + self.less[2] - 6.0 * self.mid


def fill_window(window, chunk, field, before, block, after, x_below, x_above):
    step, last = pl.program_id(0), pl.num_programs(0) - 1
    for k in range(chunk):
        window[field, k + 1] = block(k)
    window[field, 0] = jnp.where(step == 0, x_below, before)
    window[field, chunk + 1] = jnp.where(step == last, x_above, after)


def adjoint_cells_body(
    chunk, v_ref, vb_ref, va_ref, a_ref, ab_ref, aa_ref, c_ref, cb_ref, ca_ref,
    xlo_ref, xhi_ref, ylo_ref, yhi_ref, zlo_ref, zhi_ref, out_ref, source_ref, window,
):
    for j in range(3):
        fill_window(window, chunk, j, vb_ref[j, 0], lambda k: v_ref[j, k], va_ref[j, 0], xlo_ref[j], xhi_ref[j])
        fill_window(window, chunk, 3 + j, ab_ref[j, 0], lambda k: a_ref[j, k], aa_ref[j, 0], xlo_ref[3 + j], xhi_ref[3 + j])
    fill_window(window, chunk, 6, cb_ref[0], lambda k: c_ref[k], ca_ref[0], xlo_ref[6], xhi_ref[6])
    start = pl.program_id(0) * chunk

    def plane(k, carry):
        at = [
            Around(
                window.at[f], k, start + k,
                ylo_ref[f, pl.ds(k, 1), :], yhi_ref[f, pl.ds(k, 1), :], zlo_ref[f], zhi_ref[f],
            )
            for f in range(7)
        ]
        v, a, c = at[:3], at[3:6], at[6]
        flux = [c.more[i] * a[i].more[i] - c.less[i] * a[i].less[i] for i in range(3)]
        source_ref[k] = (-0.5 * time_step) * (flux[0] + flux[1] + flux[2])
        for j in range(3):
            shear = sum(a[i].mid * (v[i].more[j] - v[i].less[j]) for i in range(3))
            carried = sum(v[i].more[i] * a[j].more[i] - v[i].less[i] * a[j].less[i] for i in range(3))
            out_ref[j, k] = a[j].mid + time_step * (
                viscosity * a[j].laplace() + 0.5 * (carried - shear)
            )
        return carry

    lax.fori_loop(0, chunk, plane, 0)


def next_cells_body(
    chunk, v_ref, vb_ref, va_ref, e_ref, eb_ref, ea_ref, c_ref,
    xlo_ref, xhi_ref, ylo_ref, yhi_ref, zlo_ref, zhi_ref,
    exlo_ref, exhi_ref, eylo_ref, eyhi_ref, ezlo_ref, ezhi_ref, out_ref, window,
):
    for j in range(3):
        fill_window(window, chunk, j, vb_ref[j, 0], lambda k: v_ref[j, k], va_ref[j, 0], xlo_ref[j], xhi_ref[j])
    fill_window(window, chunk, 3, eb_ref[0], lambda k: e_ref[k], ea_ref[0], exlo_ref[...], exhi_ref[...])
    start = pl.program_id(0) * chunk

    def plane(k, carry):
        v = [
            Around(
                window.at[f], k, start + k,
                ylo_ref[f, pl.ds(k, 1), :], yhi_ref[f, pl.ds(k, 1), :], zlo_ref[f], zhi_ref[f],
            )
            for f in range(3)
        ]
        e = Around(
            window.at[3], k, start + k,
            eylo_ref[pl.ds(k, 1), :], eyhi_ref[pl.ds(k, 1), :], ezlo_ref[...], ezhi_ref[...],
        )
        for j in range(3):
            advect = sum(v[i].mid * (v[j].more[i] - v[j].less[i]) for i in range(3))
            pushed = c_ref[k] * (e.more[j] - e.less[j])
            out_ref[j, k] = v[j].mid + time_step * (
                viscosity * v[j].laplace() + 0.5 * (pushed - advect)
            )
        return carry

    lax.fori_loop(0, chunk, plane, 0)


def cell_specs(chunk, xl, yl, zl, lead):
    def at(block, place):
        if lead:
            return pl.BlockSpec((3, block, yl, zl), lambda i: (0, place(i), 0, 0))
        return pl.BlockSpec((block, yl, zl), lambda i: (place(i), 0, 0))

    return [
        at(chunk, lambda i: i),
        at(1, lambda i: jnp.maximum(i * chunk - 1, 0)),
        at(1, lambda i: jnp.minimum((i + 1) * chunk, xl - 1)),
    ]


def face_specs(chunk, yl, zl, width, fields):
    def spec(shape, index):
        return pl.BlockSpec((fields, *shape), lambda i: (0, *index(i)))

    x_spec = spec((yl, zl), lambda i: (0, 0))
    y_spec = spec((chunk, zl), lambda i: (i, 0))
    z_spec = spec((yl, width), lambda i: (0, 0))
    return [x_spec, x_spec, y_spec, y_spec, z_spec, z_spec]


def adjoint_cells_call(velocity, adjoint_seed, susceptibility, faces):
    xl, yl, zl = susceptibility.shape
    chunk = 8
    three = cell_specs(chunk, xl, yl, zl, True)
    one = cell_specs(chunk, xl, yl, zl, False)
    v, a, c = velocity, adjoint_seed, susceptibility
    return pl.pallas_call(
        functools.partial(adjoint_cells_body, chunk),
        grid=(xl // chunk,),
        in_specs=three + three + one + face_specs(chunk, yl, zl, lanes_of(max(xl, zl)), 7),
        out_specs=[three[0], one[0]],
        out_shape=[
            jax.ShapeDtypeStruct(v.shape, jnp.float32),
            jax.ShapeDtypeStruct(c.shape, jnp.float32),
        ],
        scratch_shapes=[pltpu.VMEM((7, chunk + 2, yl, zl), jnp.float32)],
        compiler_params=kernel_params,
    )(v, v, v, a, a, a, c, c, c, *faces)


def next_cells_call(velocity, energy, susceptibility, faces, energy_faces):
    xl, yl, zl = susceptibility.shape
    chunk = 8
    three = cell_specs(chunk, xl, yl, zl, True)
    one = cell_specs(chunk, xl, yl, zl, False)
    width = lanes_of(max(xl, zl))
    energy_specs = [
        pl.BlockSpec((yl, zl), lambda i: (0, 0)),
        pl.BlockSpec((chunk, zl), lambda i: (i, 0)),
        pl.BlockSpec((yl, width), lambda i: (0, 0)),
    ]
    energy_specs = [spec for spec in energy_specs for _ in range(2)]
    v, e, c = velocity, energy, susceptibility
    return pl.pallas_call(
        functools.partial(next_cells_body, chunk),
        grid=(xl // chunk,),
        in_specs=three + one + one[:1] + face_specs(chunk, yl, zl, width, 3) + energy_specs,
        out_specs=three[0],
        out_shape=jax.ShapeDtypeStruct(v.shape, jnp.float32),
        scratch_shapes=[pltpu.VMEM((4, chunk + 2, yl, zl), jnp.float32)],
        compiler_params=kernel_params,
    )(v, v, v, e, e, e, c, *faces, *energy_faces)


def on_device(mesh, velocity, adjoint_seed, susceptibility, remanence, region_bounds, step_id):
    plan = Plan(mesh, susceptibility.shape)
    tables = forward_tables(plan)
    places = [
        lax.axis_index(a) * n + jnp.arange(n, dtype=jnp.int32)
        for a, n in zip(axes, susceptibility.shape)
    ]
    inside = [
        (place >= region_bounds[0, d]) & (place < region_bounds[1, d])
        for d, place in enumerate(places)
    ]
    region_mask = (
        inside[0][:, None, None] & inside[1][None, :, None] & inside[2][None, None, :]
    ).astype(jnp.float32)
    magnet = spread(spread(spread(remanence * region_mask, "gx", 0), "gz", 0), "gy", 1)
    magnet = lax.all_gather(magnet, axes)
    stacked = [
        jnp.concatenate([velocity[:, x], adjoint_seed[:, x], susceptibility[None, x]], axis=0)
        for x in (0, plan.xl - 1)
    ]
    ylo, yhi, zlo, zhi = faces_call(velocity, adjoint_seed, susceptibility)
    faces = [
        *to_neighbours(*stacked, "gx"), *to_neighbours(ylo, yhi, "gy"), *to_neighbours(zlo, zhi, "gz"),
    ]
    velocity_adjoint, source = adjoint_cells_call(velocity, adjoint_seed, susceptibility, faces)
    phase_angle = full_turn * (step_id[0] % field_period).astype(jnp.float32) / field_period
    applied = jnp.stack([jnp.cos(phase_angle), jnp.sin(phase_angle)])
    field_adjoint, energy = field_call(plan, tables, magnet, source, applied)
    partial_sums = adjoint_call(plan, tables, field_adjoint)
    piece = lax.psum_scatter(
        partial_sums.reshape(-1, plan.px, plan.py, plan.zl), axes, scatter_dimension=0
    )
    magnet_adjoint = unspread(unspread(unspread(piece, "gy", 1), "gz", 0), "gx", 0)
    design_gradient = region_mask * magnet_adjoint
    energy = energy.reshape(susceptibility.shape)
    ends = [energy[..., z].T for z in (0, plan.zl - 1)]
    ends = [jnp.pad(end, ((0, 0), (0, lanes_of(max(plan.xl, plan.zl)) - plan.xl))) for end in ends]
    energy_faces = [
        *to_neighbours(energy[0], energy[-1], "gx"),
        *to_neighbours(energy[:, 0], energy[:, -1], "gy"),
        *to_neighbours(*ends, "gz"),
    ]
    next_velocity = next_cells_call(velocity, energy, susceptibility, faces, energy_faces)
    return (next_velocity, velocity_adjoint, design_gradient)


def solution(mesh):
    cells = P(*axes)
    vectors = P(None, *axes)
    return jax.shard_map(
        functools.partial(on_device, mesh),
        mesh=mesh,
        in_specs=(vectors, vectors, cells, cells, P(), P()),
        out_specs=(vectors, vectors, cells),
        check_vma=False,
    )
```

```python
import functools
import math

import jax
import jax.numpy as jnp
import ml_dtypes
import numpy as np
from jax import lax
from jax.experimental import pallas as pl
from jax.experimental.pallas import tpu as pltpu
from jax.sharding import PartitionSpec as P

time_step = 0.5
viscosity = 0.2
field_period = 24
full_turn = 2.0 * math.pi
bf16 = ml_dtypes.bfloat16
axes = ("gx", "gy", "gz")


def wave_tables(length):
    half = length // 2
    slot = np.arange(length)
    wave = np.where(slot <= half, slot, slot - half)
    angle = full_turn * (wave[:, None] * np.arange(length)[None, :] % length) / length
    weight = np.sqrt(np.where(slot % half == 0, 1.0, 2.0) / length)[:, None]
    odd = (slot > half)[:, None]
    kappa = full_turn * wave / length
    basis = np.where(odd, np.sin(angle), np.cos(angle)) * weight
    slope = np.where(odd, np.cos(angle), -np.sin(angle)) * weight * kappa[:, None]
    slope[half] = 0.0
    return basis, slope, kappa


def two_parts(table):
    high = table.astype(bf16)
    low = (table - high.astype(np.float64)).astype(bf16)
    return high, low


def split(value):
    high = value.astype(jnp.bfloat16)
    low = (value - high.astype(jnp.float32)).astype(jnp.bfloat16)
    return high, low


def dot(left, right):
    return jnp.dot(left, right, preferred_element_type=jnp.float32)


class Plan:
    def __init__(self, mesh, local):
        self.gx, self.gy, self.gz = (mesh.shape[a] for a in axes)
        self.xl, self.yl, self.zl = local
        self.nx, self.ny, self.nz = self.xl * self.gx, self.yl * self.gy, self.zl * self.gz
        self.x2, self.y2, self.z2 = self.nx // 2, self.ny // 2, self.nz // 2
        self.kx, self.kh = self.nx // 2, self.nx // 4
        self.yc = 2 * self.yl
        self.pitch = self.kx + 8
        self.px, self.py = self.xl // 4, self.yl // 2
        self.relay = (self.gx, self.gy, self.gz) == (2, 8, 2)
        self.arrays = 16 if self.relay else 1
        self.segments = self.relay_segments() if self.relay else self.gathered_segments()

    def gathered_segments(self):
        size = self.py * self.px
        return [
            [
                [
                    (0, ((first * self.gy + across) * self.gz + 2 * depth + side) * size)
                    for first in range(self.gx)
                    for side in range(2)
                ]
                for depth in range(self.gz // 2)
            ]
            for across in range(self.gy)
        ]

    def relay_segments(self):
        size = self.py * self.px
        segments = []
        for at in range(0, 16, 4):
            segments.append([[(at, 0), (at, size), (at + 1, 0), (at + 1, size)]])
            segments.append([[(at + 2, 0), (at + 3, 0), (at + 2, size), (at + 3, size)]])
        return segments

    def orders(self):
        x_orders = [
            np.concatenate([np.arange(self.px) + (column ^ r) * self.px for r in range(4)])
            for column in range(4)
        ]
        y_orders = []
        for side in range(2):
            for later in range(2):
                blocks = [2 * (half ^ later) + (side ^ far) for far in range(2) for half in range(2)]
                y_orders.append(np.concatenate([np.arange(self.yl) + block * self.yl for block in blocks]))
        return x_orders, y_orders


def make_tables(plan):
    bx, dx, wx = wave_tables(plan.nx)
    by, dy, wy = wave_tables(plan.ny)
    bz, dz, wz = wave_tables(plan.nz)
    hx, hy, hz = plan.nx // 2, plan.ny // 2, plan.nz // 2
    ez = bz.copy()
    ez[0] = bz[hz]
    z1 = dz.copy()
    z1[0] = 0.0
    z2 = dz.copy()
    z2[0] = -(np.pi**2) * bz[hz]
    z3 = -(wz**2)[:, None] * bz
    z3[0] = 0.0
    z1n = np.zeros_like(z1)
    z1n[hz] = -np.pi * bz[hz]
    xs = dx.copy()
    xs[hx] = np.pi * bx[hx]
    w3 = wz.copy()
    w3[0] = np.pi
    base = wy[:, None] ** 2 + w3[None, :] ** 2
    keep = np.ones_like(base, bool)
    keep[:, 0] = False
    keep[hy, 0] = True
    base = np.where(keep, base, 1e30).astype(np.float32)
    own = [np.arange(c * plan.kh, (c + 1) * plan.kh) for c in range(2)]
    own = [np.concatenate([cosines, hx + cosines]) for cosines in own]

    def by_side(table):
        return np.stack([table[slots] for slots in own])

    fx, fy = by_side(bx[:, : plan.x2]), by[None, :, : plan.y2]
    if plan.relay:
        x_orders, y_orders = plan.orders()
        fx = np.stack([part[:, order] for part in fx for order in x_orders])
        fy = np.stack([fy[0][:, order] for order in y_orders])
    return dict(
        fx=fx,
        fy=fy,
        xb=by_side(bx),
        xs=by_side(xs),
        w1=by_side((wx**2).astype(np.float32)),
        z1n=np.stack([z1n, z1]),
        ez=ez[:, : plan.z2],
        by=by,
        dy=dy,
        z1=z1,
        z2=z2,
        z3=z3,
        base=base,
    )


def pair_lanes(*arrays):
    return jnp.concatenate(arrays, axis=1)


def pair_rows(*arrays):
    return jnp.concatenate(arrays, axis=0)


def load_plane(refs, plan, segment, i):
    blocks = [
        pair_rows(*[refs[array][pl.ds(start + i * plan.px, plan.px), :] for array, start in runs])
        for runs in segment
    ]
    return blocks[0] if len(blocks) == 1 else pair_lanes(*blocks)


def store_plane(refs, plan, segment, i, value):
    for depth, runs in enumerate(segment):
        for place, (array, start) in enumerate(runs):
            refs[array][pl.ds(start + i * plan.px, plan.px), :] = value[
                place * plan.px : (place + 1) * plan.px, depth * plan.zl : (depth + 1) * plan.zl
            ]


def field_body(
    plan, group, w1_ref, fx_ref, ez_ref, fy_ref, g_ref, z13_ref, z2_ref, z1n_ref, xs_ref, xb_ref, base_ref, *refs,
):
    kx, kh, pitch = plan.kx, plan.kh, plan.pitch
    y2, z2, xl, yl, yc, zl = plan.y2, plan.z2, plan.xl, plan.yl, plan.yc, plan.zl
    span = yc * pitch
    m_refs, (own_ref, other_ref, s_ref, r_ref) = refs[: plan.arrays], refs[plan.arrays :]

    def along_x(number, segment):
        def body(pair, carry):
            planes = [load_plane(m_refs, plan, segment, 2 * pair + k) for k in range(2)]
            high, low = split(pair_lanes(*planes))
            out = dot(fx_ref[...], pair_rows(high, low, high))
            row = (number * plan.py + 2 * pair) * pitch
            s_ref[pl.ds(row, kx), :] = out[:, :z2]
            s_ref[pl.ds(row + pitch, kx), :] = out[:, z2:]
            return carry

        lax.fori_loop(0, plan.py // 2, body, 0)

    for number, segment in enumerate(plan.segments):
        along_x(number, segment)

    def depth_waves(slots):
        rows = pair_rows(*[s_ref[pl.ds(slot, y2, stride=pitch), :] for slot in slots])
        high, low = split(rows)
        return dot(pair_lanes(high, low, high), ez_ref[...])

    def one_slab(plane, kern):
        high, low = split(plane)
        high, low = split(dot(fy_ref[...], pair_rows(high, low, high)) * kern)
        both = dot(g_ref[...], high)
        return both[: 2 * yc] + both[2 * yc :] + dot(g_ref[: 2 * yc], low)

    def two_products(high, low, table_ref):
        both = dot(high, table_ref[...])
        return both[:, :zl] + both[:, zl:] + dot(low, table_ref[:, :zl])

    def store(slots, cells, j):
        for place, slot in enumerate(slots):
            r_ref[pl.ds(j * span + slot, yc, stride=pitch), :] = cells[place * yc : (place + 1) * yc]

    def depth_cells(slots, slabs, edge):
        q1 = pair_rows(*[slab[:yc] for slab in slabs])
        q2 = pair_rows(*[slab[yc:] for slab in slabs])
        lane = lax.broadcasted_iota(jnp.int32, q1.shape, 1)
        q2 = jnp.where(lane == 0, q1, q2)
        high, low = split(q1)
        r13 = dot(pair_lanes(high, low, high), z13_ref[...])
        store(slots, two_products(high, low, z1n_ref) if edge else r13[:, :zl], 0)
        store(slots, r13[:, zl:], 2)
        store(slots, two_products(*split(q2), z2_ref), 1)

    def waves(step, carry):
        first = step * group
        slots = [first + k + part for k in range(group) for part in (0, kh)]
        planes = depth_waves(slots)
        slabs = []
        for k in range(group):
            kern = 1.0 / (base_ref[...] + w1_ref[first + k])
            for part in range(2):
                at = (2 * k + part) * y2
                slabs.append(one_slab(planes[at : at + y2], kern))
        depth_cells(slots, slabs, False)
        return carry

    lax.fori_loop(0, kh // group, waves, 0)

    slab = one_slab(depth_waves([kh]), 1.0 / (base_ref[...] + w1_ref[kh]))
    depth_cells([kh], [slab], True)

    def back_x(mat_ref, values):
        high, low = split(values)
        return dot(mat_ref[...], pair_rows(high, low, high))

    def cells(out_ref, shift):
        def body(pair, carry):
            here = [
                [pl.ds(j * span + (shift + 2 * pair + k) * pitch, kx) for k in range(2)]
                for j in range(3)
            ]
            h1 = back_x(xs_ref, pair_lanes(r_ref[here[0][0], :], r_ref[here[0][1], :]))
            for k in range(2):
                h23 = back_x(xb_ref, pair_lanes(r_ref[here[1][k], :], r_ref[here[2][k], :]))
                at = (2 * pair + k) * xl
                out_ref[pl.ds(at, xl), :] = h1[:, k * zl : (k + 1) * zl]
                out_ref[pl.ds(yl * xl + at, xl), :] = h23[:, :zl]
                out_ref[pl.ds(2 * yl * xl + at, xl), :] = h23[:, zl:]
            return carry

        lax.fori_loop(0, yl // 2, body, 0)

    cells(other_ref, yl)
    cells(own_ref, 0)


def adjoint_body(
    plan, group, w1_ref, own_ref, other_ref, xs_ref, xb_ref, z13_ref, z2_ref, z1n_ref, g_ref, fy_ref, ez_ref, fx_ref, base_ref, *refs,
):
    kx, kh, pitch = plan.kx, plan.kh, plan.pitch
    y2, z2, xl, yl, yc, zl = plan.y2, plan.z2, plan.xl, plan.yl, plan.yc, plan.zl
    span = yc * pitch
    m_refs, (s_ref, r_ref) = refs[: plan.arrays], refs[plan.arrays :]

    def along_x(mat_ref, values):
        high, low = split(values)
        return dot(mat_ref[...], pair_rows(high, low, high))

    def cells(f_ref, shift):
        def body(pair, carry):
            here = [
                [pl.ds((j * yl + 2 * pair + k) * xl, xl) for k in range(2)] for j in range(3)
            ]
            u1 = along_x(xs_ref, pair_lanes(f_ref[here[0][0], :], f_ref[here[0][1], :]))
            for k in range(2):
                u23 = along_x(xb_ref, pair_lanes(f_ref[here[1][k], :], f_ref[here[2][k], :]))
                row = (shift + 2 * pair + k) * pitch
                r_ref[pl.ds(row, kx), :] = u1[:, k * zl : (k + 1) * zl]
                r_ref[pl.ds(span + row, kx), :] = u23[:, :zl]
                r_ref[pl.ds(2 * span + row, kx), :] = u23[:, zl:]
            return carry

        lax.fori_loop(0, yl // 2, body, 0)

    cells(own_ref, 0)
    cells(other_ref, yl)

    def depth_waves(slots, edge):
        u = [
            pair_rows(*[r_ref[pl.ds(j * span + slot, yc, stride=pitch), :] for slot in slots])
            for j in range(3)
        ]
        high1, low1 = split(u[0])
        high2, low2 = split(u[1])
        high3, low3 = split(u[2])
        high = pair_lanes(high1, high3)
        q1 = dot(pair_lanes(high, low1, low3, high), z13_ref[...])
        if edge:
            q1 = q1 + dot(pair_lanes(high1, low1, high1), z1n_ref[...])
        q2 = dot(pair_lanes(high2, low2, high2), z2_ref[...])
        first = lax.broadcasted_iota(jnp.int32, q1.shape, 1) == 0
        return jnp.where(first, q2, q1), jnp.where(first, 0.0, q2)

    def one_slab(q1, q2, kern):
        high, low = split(pair_rows(q1, q2))
        high, low = split(dot(g_ref[...], pair_rows(high, low, high)) * kern)
        both = dot(fy_ref[...], high)
        return both[:y2] + both[y2:] + dot(fy_ref[:y2], low)

    def depth_cells(slots, slabs):
        high, low = split(pair_rows(*slabs))
        out = dot(high, ez_ref[...])
        out = out[:, :z2] + out[:, z2:] + dot(low, ez_ref[:, :z2])
        for place, slot in enumerate(slots):
            s_ref[pl.ds(slot, y2, stride=pitch), :] = out[place * y2 : (place + 1) * y2]

    def waves(step, carry):
        first = step * group
        slots = [first + k + part for k in range(group) for part in (0, kh)]
        q1, q2 = depth_waves(slots, False)
        slabs = []
        for k in range(group):
            kern = 1.0 / (base_ref[...] + w1_ref[first + k])
            for part in range(2):
                take = slice((2 * k + part) * yc, (2 * k + part + 1) * yc)
                slabs.append(one_slab(q1[take], q2[take], kern))
        depth_cells(slots, slabs)
        return carry

    lax.fori_loop(0, kh // group, waves, 0)

    q1, q2 = depth_waves([kh], True)
    depth_cells([kh], [one_slab(q1, q2, 1.0 / (base_ref[...] + w1_ref[kh]))])

    def back_x(number, segment):
        def body(pair, carry):
            row = (number * plan.py + 2 * pair) * pitch
            planes = [s_ref[pl.ds(row + k * pitch, kx), :] for k in range(2)]
            high, low = split(pair_lanes(*planes))
            out = dot(fx_ref[...], pair_rows(high, low, high))
            store_plane(m_refs, plan, segment, 2 * pair, out[:, :z2])
            store_plane(m_refs, plan, segment, 2 * pair + 1, out[:, z2:])
            return carry

        lax.fori_loop(0, plan.py // 2, body, 0)

    for number, segment in enumerate(plan.segments):
        back_x(number, segment)


vmem = pl.BlockSpec(memory_space=pltpu.VMEM)
smem = pl.BlockSpec(memory_space=pltpu.SMEM)
kernel_params = pltpu.CompilerParams(vmem_limit_bytes=60 * 2**20)


def scratch_of(plan):
    return [
        pltpu.VMEM((plan.y2 * plan.pitch, plan.z2), jnp.float32),
        pltpu.VMEM((3 * plan.yc * plan.pitch, plan.zl), jnp.float32),
    ]


def side_of(plan):
    return lax.rem(lax.axis_index("gy"), 2)


def of_side(plan, stack):
    return lax.dynamic_index_in_dim(jnp.asarray(stack), side_of(plan), 0, keepdims=False)


def of_place(plan, stack, name):
    side, place = side_of(plan), 0
    if plan.relay and name == "fx":
        side, place = 4 * side, 2 * lax.axis_index("gx") + lax.axis_index("gz")
    elif plan.relay:
        side, place = 2 * side, jnp.minimum(lax.axis_index("gy") // 2, 1)
    elif name == "fy":
        side = 0
    return lax.dynamic_index_in_dim(jnp.asarray(stack), side + place, 0, keepdims=False)


def own_block(plan, table, axis, count, dim):
    table = jnp.asarray(table)
    place = lax.axis_index(axis)
    if axis != "gy":
        return lax.dynamic_slice_in_dim(table, place * count, count, dim)
    partner = place + 1 - 2 * lax.rem(place, 2)
    both = [lax.dynamic_slice_in_dim(table, p * count, count, dim) for p in (place, partner)]
    return jnp.concatenate(both, axis=dim)


def thrice_lanes(table):
    high, low = two_parts(table)
    return np.concatenate([high, high, low], axis=-1)


def thrice_rows(table):
    high, low = two_parts(table)
    return np.concatenate([high, high, low], axis=-2)


def field_tables(plan, t):
    xl, yl, zl = plan.xl, plan.yl, plan.zl

    def y_cells(part):
        return own_block(plan, part, "gy", yl, 0)

    def z_cells(part):
        return own_block(plan, part, "gz", zl, 1)

    def x_table(name):
        high, low = [
            own_block(plan, of_side(plan, part.swapaxes(1, 2)), "gx", xl, 0) for part in two_parts(t[name])
        ]
        return pair_lanes(high, high, low)

    b, bl = [y_cells(part) for part in two_parts(t["by"].T)]
    d, dl = [y_cells(part) for part in two_parts(t["dy"].T)]
    z1, z1l = [z_cells(part) for part in two_parts(t["z1"])]
    z2, z2l = [z_cells(part) for part in two_parts(t["z2"])]
    z3, z3l = [z_cells(part) for part in two_parts(t["z3"])]
    z1n, z1nl = [z_cells(of_side(plan, part)) for part in two_parts(t["z1n"])]
    z13, z13l = pair_lanes(z1, z3), pair_lanes(z1l, z3l)
    return [
        of_side(plan, t["w1"]), of_place(plan, thrice_lanes(t["fx"]), "fx"), jnp.asarray(thrice_rows(t["ez"].T)),
        of_place(plan, thrice_lanes(t["fy"]), "fy"), pair_rows(b, d, bl, dl), pair_rows(z13, z13, z13l), pair_lanes(z2, z2l),
        pair_lanes(z1n, z1nl), x_table("xs"), x_table("xb"), jnp.asarray(t["base"]),
    ]


def field_call(plan, tables, octant):
    xl, yl, zl = plan.xl, plan.yl, plan.zl
    group = 4
    shape = jax.ShapeDtypeStruct((3 * yl * xl, zl), jnp.float32)
    own, other = pl.pallas_call(
        functools.partial(field_body, plan, group),
        out_shape=[shape, shape],
        in_specs=[smem] + [vmem] * (10 + plan.arrays),
        out_specs=[vmem, vmem],
        scratch_shapes=scratch_of(plan),
        compiler_params=kernel_params,
    )(*tables, *octant)
    return own.reshape(3, yl, xl, zl), other.reshape(3, yl, xl, zl)


def adjoint_tables(plan, t):
    xl, yl, zl = plan.xl, plan.yl, plan.zl

    def y_cells(part):
        return own_block(plan, part, "gy", yl, 1)

    def z_cells(part):
        return own_block(plan, part, "gz", zl, 0)

    def x_table(name):
        high, low = [
            own_block(plan, of_side(plan, part), "gx", xl, 1) for part in two_parts(t[name])
        ]
        return pair_lanes(high, high, low)

    b, bl = [y_cells(part) for part in two_parts(t["by"])]
    d, dl = [y_cells(part) for part in two_parts(t["dy"])]
    z1, z1l = [z_cells(part) for part in two_parts(t["z1"].T)]
    z2, z2l = [z_cells(part) for part in two_parts(t["z2"].T)]
    z3, z3l = [z_cells(part) for part in two_parts(t["z3"].T)]
    z1n, z1nl = [
        z_cells(of_side(plan, part)) for part in two_parts((t["z1n"] - t["z1"]).swapaxes(1, 2))
    ]
    fy, fyl = two_parts(t["fy"].swapaxes(1, 2))
    ez, ezl = two_parts(t["ez"])
    return [
        of_side(plan, t["w1"]), x_table("xs"), x_table("xb"),
        pair_rows(z1, z3, z1, z3, z1l, z3l), pair_rows(z2, z2, z2l), pair_rows(z1n, z1n, z1nl),
        pair_lanes(b, d, b, d, bl, dl), of_place(plan, np.concatenate([fy, fyl], axis=1), "fy"), jnp.concatenate([ez, ezl], axis=1),
        of_place(plan, thrice_lanes(t["fx"].swapaxes(1, 2)), "fx"), jnp.asarray(t["base"]),
    ]


def adjoint_call(plan, tables, own, other):
    zl = plan.zl
    group = 4
    return pl.pallas_call(
        functools.partial(adjoint_body, plan, group),
        out_shape=[
            jax.ShapeDtypeStruct((plan.x2 * plan.y2 * plan.z2 // zl // plan.arrays, zl), jnp.float32)
        ] * plan.arrays,
        in_specs=[smem] + [vmem] * 12,
        out_specs=[vmem] * plan.arrays,
        scratch_shapes=scratch_of(plan),
        compiler_params=kernel_params,
    )(tables[0], own.reshape(-1, zl), other.reshape(-1, zl), *tables[1:])


def swapped(array):
    count = lax.axis_size("gy")
    return lax.ppermute(array, "gy", [(i, i + 1 - 2 * (i % 2)) for i in range(count)])


def spread(block, axis, dim):
    count = lax.axis_size(axis)
    halves = jnp.split(block, 2, axis=dim)
    moved = [
        lax.ppermute(half, axis, [(s, 2 * s + k) for s in range(count // 2)])
        for k, half in enumerate(halves)
    ]
    return moved[0] + moved[1]


def unspread(piece, axis, dim):
    count = lax.axis_size(axis)
    moved = [
        lax.ppermute(piece, axis, [(2 * s + k, s) for s in range(count // 2)]) for k in range(2)
    ]
    return jnp.concatenate(moved, axis=dim)


def gather_octant(plan, block, work):
    if plan.relay:
        return relay_octant(plan, block, work)
    done = []
    for step in work:
        done.append(step(done))
    piece = block
    for axis, dim in (("gx", 1), ("gz", 1), ("gy", 0)):
        piece = spread(piece, axis, dim)
    return [lax.all_gather(piece.reshape(plan.py * plan.px, plan.zl), axes, tiled=True)], done


def owners_sum(plan, sums, work):
    if plan.relay:
        return relay_sums(plan, sums, work)
    done = [step() for step in work]
    piece = lax.psum_scatter(sums[0], axes, scatter_dimension=0, tiled=True)
    piece = piece.reshape(plan.py, plan.px, plan.zl)
    return unspread(unspread(unspread(piece, "gy", 0), "gz", 1), "gx", 1), done


flip = [(0, 1), (1, 0)]


def along(array, pairs):
    return lax.ppermute(array, "gy", [(2 * a + c, 2 * b + c) for a, b in pairs for c in range(2)])


def together(*values):
    return lax.optimization_barrier(values)


def relay_octant(plan, block, work):
    z = lax.axis_index("gy") // 2
    done = []
    quarters = [block[:, r * plan.px : (r + 1) * plan.px].reshape(-1, plan.zl) for r in range(4)]
    moved = [lax.ppermute(quarters[r], ("gx", "gz"), [(0, r)]) for r in range(1, 4)]
    moved, result = together(moved, work[0](done))
    done.append(result)
    piece = quarters[0] + moved[0] + moved[1] + moved[2]
    up = along(piece, [(0, 1), (1, 2)])
    down = along(piece, [(1, 0)])
    up, result = together(up, work[1](done))
    done.append(result)
    up2 = along(up, [(1, 2), (2, 3)])
    up2, result = together(up2, work[2](done))
    done.append(result)
    up3 = along(up2, [(2, 3)])
    first = across(plan, jnp.where(z < 2, piece, jnp.where(z == 2, up, up2)))
    up3, result = together(up3, work[3](done))
    done.append(result)
    second = jnp.where(z == 0, down, jnp.where(z == 1, up, jnp.where(z == 2, up2, up3)))
    own = first + across(plan, second)
    return own + [swapped(array) for array in own], done


def across(plan, piece):
    half = plan.py * plan.px
    low, high = piece[:half], piece[half:]
    a = pair_rows(low, lax.ppermute(low, "gz", flip))
    b = pair_rows(high, lax.ppermute(high, "gx", flip))
    return [a, lax.ppermute(a, "gx", flip), b, lax.ppermute(b, "gz", flip)]


def across_sums(plan, arrays):
    half = plan.py * plan.px
    a, ay, b, bx = arrays
    a = a + lax.ppermute(ay, "gx", flip)
    b = b + lax.ppermute(bx, "gz", flip)
    low = a[:half] + lax.ppermute(a[half:], "gz", flip)
    high = b[:half] + lax.ppermute(b[half:], "gx", flip)
    return pair_rows(low, high)


def relay_sums(plan, sums, work):
    z = lax.axis_index("gy") // 2
    own = [sums[i] + swapped(sums[i + 8]) for i in range(8)]
    second = across_sums(plan, own[4:])
    moved = along(second, [(3, 2)])
    moved, result0 = together(moved, work[0]())
    first = across_sums(plan, own[:4])
    second = second + moved
    moved = along(jnp.where(z == 3, first, second), [(3, 2), (2, 1)])
    moved, result1 = together(moved, work[1]())
    first = first + jnp.where(z == 2, moved, 0.0)
    second = second + jnp.where(z == 1, moved, 0.0)
    first = first + along(second, [(0, 1)]) + along(jnp.where(z == 2, first, second), [(2, 1), (1, 0)])
    quarters = [first] + [lax.ppermute(first, ("gx", "gz"), [(r, 0)]) for r in range(1, 4)]
    block = jnp.concatenate([q.reshape(plan.yl, plan.px, plan.zl) for q in quarters], axis=1)
    return block, [result0, result1]


def lanes_of(count):
    return -(-count // 128) * 128


def faces_body(chunk, v_ref, a_ref, c_ref, ylo_ref, yhi_ref, zlo_ref, zhi_ref):
    yl, zl = v_ref.shape[2:]
    step = pl.program_id(0)

    @pl.when(step == 0)
    def _():
        zlo_ref[...] = jnp.zeros_like(zlo_ref)
        zhi_ref[...] = jnp.zeros_like(zhi_ref)

    lane = lax.broadcasted_iota(jnp.int32, zlo_ref.shape[1:], 1)
    for field in range(7):
        low, high = zlo_ref[field], zhi_ref[field]
        for k in range(chunk):
            plane = v_ref[field, k] if field < 3 else a_ref[field - 3, k] if field < 6 else c_ref[k]
            ylo_ref[field, k : k + 1, :] = plane[:1]
            yhi_ref[field, k : k + 1, :] = plane[yl - 1 :]
            here = lane == step * chunk + k
            low = jnp.where(here, plane[:, :1], low)
            high = jnp.where(here, plane[:, zl - 1 :], high)
        zlo_ref[field] = low
        zhi_ref[field] = high


def faces_call(velocity, adjoint_seed, susceptibility):
    xl, yl, zl = susceptibility.shape
    chunk = 8
    three = pl.BlockSpec((3, chunk, yl, zl), lambda i: (0, i, 0, 0))
    y_spec = pl.BlockSpec((7, chunk, zl), lambda i: (0, i, 0))
    z_spec = pl.BlockSpec((7, yl, lanes_of(max(xl, zl))), lambda i: (0, 0, 0))
    y_shape = jax.ShapeDtypeStruct((7, xl, zl), jnp.float32)
    z_shape = jax.ShapeDtypeStruct((7, yl, lanes_of(max(xl, zl))), jnp.float32)
    return pl.pallas_call(
        functools.partial(faces_body, chunk),
        grid=(xl // chunk,),
        in_specs=[three, three, pl.BlockSpec((chunk, yl, zl), lambda i: (i, 0, 0))],
        out_specs=[y_spec, y_spec, z_spec, z_spec],
        out_shape=[y_shape, y_shape, z_shape, z_shape],
        compiler_params=kernel_params,
    )(velocity, adjoint_seed, susceptibility)


def to_neighbours(low_face, high_face, axis):
    count = lax.axis_size(axis)
    below = lax.ppermute(high_face, axis, [(i, i + 1) for i in range(count - 1)])
    above = lax.ppermute(low_face, axis, [(i + 1, i) for i in range(count - 1)])
    return below, above


def combine_body(chunk, app_ref, own_ref, arrived_ref, source_ref, f_ref, e_ref, ylo_ref, yhi_ref, zlo_ref, zhi_ref):
    yl, _, zl = source_ref.shape
    step = pl.program_id(0)

    @pl.when(step == 0)
    def _():
        zlo_ref[...] = jnp.zeros_like(zlo_ref)
        zhi_ref[...] = jnp.zeros_like(zhi_ref)

    energy = 0.0
    for j in range(3):
        total = own_ref[j] + arrived_ref[j] + app_ref[j]
        f_ref[j] = source_ref[...] * total
        energy = energy + total * total
    energy = 0.5 * energy
    lane = lax.broadcasted_iota(jnp.int32, zlo_ref.shape, 1)
    low, high = zlo_ref[...], zhi_ref[...]
    for k in range(chunk):
        plane = energy[:, k, :]
        e_ref[k] = plane
        ylo_ref[k : k + 1, :] = plane[:1]
        yhi_ref[k : k + 1, :] = plane[yl - 1 :]
        here = lane == step * chunk + k
        low = jnp.where(here, plane[:, :1], low)
        high = jnp.where(here, plane[:, zl - 1 :], high)
    zlo_ref[...] = low
    zhi_ref[...] = high


def combine_call(applied, own, arrived, source):
    _, yl, xl, zl = own.shape
    chunk = 8
    width = lanes_of(max(xl, zl))
    three = pl.BlockSpec((3, yl, chunk, zl), lambda i: (0, 0, i, 0))
    y_spec = pl.BlockSpec((chunk, zl), lambda i: (i, 0))
    z_spec = pl.BlockSpec((yl, width), lambda i: (0, 0))
    shapes = [(3, yl, xl, zl), (xl, yl, zl), (xl, zl), (xl, zl), (yl, width), (yl, width)]
    return pl.pallas_call(
        functools.partial(combine_body, chunk),
        grid=(xl // chunk,),
        in_specs=[smem, three, three, pl.BlockSpec((yl, chunk, zl), lambda i: (0, i, 0))],
        out_specs=[
            three, pl.BlockSpec((chunk, yl, zl), lambda i: (i, 0, 0)), y_spec, y_spec, z_spec, z_spec,
        ],
        out_shape=[jax.ShapeDtypeStruct(shape, jnp.float32) for shape in shapes],
        compiler_params=kernel_params,
    )(applied, own, arrived, source)


class Around:
    def __init__(self, ref, k, x, y_below, y_above, z_below, z_above):
        mid = ref[k + 1]
        yl, zl = mid.shape
        row = lax.broadcasted_iota(jnp.int32, mid.shape, 0)
        lane = lax.broadcasted_iota(jnp.int32, mid.shape, 1)
        width = z_below.shape[1]
        left = pltpu.roll(z_below, lax.rem(width - x, width), 1)[:, :zl]
        right = pltpu.roll(z_above, lax.rem(width + zl - 1 - x, width), 1)[:, :zl]
        self.mid = mid
        self.less = [
            ref[k],
            jnp.where(row == 0, y_below, pltpu.roll(mid, 1, 0)),
            jnp.where(lane == 0, left, pltpu.roll(mid, 1, 1)),
        ]
        self.more = [
            ref[k + 2],
            jnp.where(row == yl - 1, y_above, pltpu.roll(mid, yl - 1, 0)),
            jnp.where(lane == zl - 1, right, pltpu.roll(mid, zl - 1, 1)),
        ]

    def slope(self, d):
        return (self.more[d] - self.less[d]) * 0.5

    def laplace(self):
        beside = self.more[0] + self.less[0] + self.more[1] + self.less[1]
        return beside + self.more[2] + self.less[2] - 6.0 * self.mid


def fill_window(window, chunk, field, before, block, after, x_below, x_above):
    step, last = pl.program_id(0), pl.num_programs(0) - 1
    for k in range(chunk):
        window[field, k + 1] = block(k)
    window[field, 0] = jnp.where(step == 0, x_below, before)
    window[field, chunk + 1] = jnp.where(step == last, x_above, after)


def source_body(
    chunk, a_ref, ab_ref, aa_ref, c_ref, cb_ref, ca_ref,
    xlo_ref, xhi_ref, ylo_ref, yhi_ref, zlo_ref, zhi_ref, source_ref, window,
):
    for j in range(3):
        fill_window(window, chunk, j, ab_ref[j, 0], lambda k: a_ref[j, k], aa_ref[j, 0], xlo_ref[3 + j], xhi_ref[3 + j])
    fill_window(window, chunk, 3, cb_ref[0], lambda k: c_ref[k], ca_ref[0], xlo_ref[6], xhi_ref[6])
    start = pl.program_id(0) * chunk

    def plane(k, carry):
        at = [
            Around(
                window.at[f], k, start + k,
                ylo_ref[3 + f, pl.ds(k, 1), :], yhi_ref[3 + f, pl.ds(k, 1), :], zlo_ref[3 + f], zhi_ref[3 + f],
            )
            for f in range(4)
        ]
        a, c = at[:3], at[3]
        flux = [c.more[i] * a[i].more[i] - c.less[i] * a[i].less[i] for i in range(3)]
        source_ref[:, k, :] = (-0.5 * time_step) * (flux[0] + flux[1] + flux[2])
        return carry

    lax.fori_loop(0, chunk, plane, 0)


def adjoint_cells_body(
    chunk, v_ref, vb_ref, va_ref, a_ref, ab_ref, aa_ref,
    xlo_ref, xhi_ref, ylo_ref, yhi_ref, zlo_ref, zhi_ref, out_ref, window,
):
    for j in range(3):
        fill_window(window, chunk, j, vb_ref[j, 0], lambda k: v_ref[j, k], va_ref[j, 0], xlo_ref[j], xhi_ref[j])
        fill_window(window, chunk, 3 + j, ab_ref[j, 0], lambda k: a_ref[j, k], aa_ref[j, 0], xlo_ref[3 + j], xhi_ref[3 + j])
    start = pl.program_id(0) * chunk

    def plane(k, carry):
        at = [
            Around(
                window.at[f], k, start + k,
                ylo_ref[f, pl.ds(k, 1), :], yhi_ref[f, pl.ds(k, 1), :], zlo_ref[f], zhi_ref[f],
            )
            for f in range(6)
        ]
        v, a = at[:3], at[3:]
        for j in range(3):
            shear = sum(a[i].mid * (v[i].more[j] - v[i].less[j]) for i in range(3))
            carried = sum(v[i].more[i] * a[j].more[i] - v[i].less[i] * a[j].less[i] for i in range(3))
            out_ref[j, k] = a[j].mid + time_step * (
                viscosity * a[j].laplace() + 0.5 * (carried - shear)
            )
        return carry

    lax.fori_loop(0, chunk, plane, 0)


def next_cells_body(
    chunk, v_ref, vb_ref, va_ref, e_ref, eb_ref, ea_ref, c_ref,
    xlo_ref, xhi_ref, ylo_ref, yhi_ref, zlo_ref, zhi_ref,
    exlo_ref, exhi_ref, eylo_ref, eyhi_ref, ezlo_ref, ezhi_ref, out_ref, window,
):
    for j in range(3):
        fill_window(window, chunk, j, vb_ref[j, 0], lambda k: v_ref[j, k], va_ref[j, 0], xlo_ref[j], xhi_ref[j])
    fill_window(window, chunk, 3, eb_ref[0], lambda k: e_ref[k], ea_ref[0], exlo_ref[...], exhi_ref[...])
    start = pl.program_id(0) * chunk

    def plane(k, carry):
        v = [
            Around(
                window.at[f], k, start + k,
                ylo_ref[f, pl.ds(k, 1), :], yhi_ref[f, pl.ds(k, 1), :], zlo_ref[f], zhi_ref[f],
            )
            for f in range(3)
        ]
        e = Around(
            window.at[3], k, start + k,
            eylo_ref[pl.ds(k, 1), :], eyhi_ref[pl.ds(k, 1), :], ezlo_ref[...], ezhi_ref[...],
        )
        for j in range(3):
            advect = sum(v[i].mid * (v[j].more[i] - v[j].less[i]) for i in range(3))
            pushed = c_ref[k] * (e.more[j] - e.less[j])
            out_ref[j, k] = v[j].mid + time_step * (
                viscosity * v[j].laplace() + 0.5 * (pushed - advect)
            )
        return carry

    lax.fori_loop(0, chunk, plane, 0)


def cell_specs(chunk, xl, yl, zl, lead):
    def at(block, place):
        if lead:
            return pl.BlockSpec((3, block, yl, zl), lambda i: (0, place(i), 0, 0))
        return pl.BlockSpec((block, yl, zl), lambda i: (place(i), 0, 0))

    return [
        at(chunk, lambda i: i),
        at(1, lambda i: jnp.maximum(i * chunk - 1, 0)),
        at(1, lambda i: jnp.minimum((i + 1) * chunk, xl - 1)),
    ]


def face_specs(chunk, yl, zl, width, fields):
    def spec(shape, index):
        return pl.BlockSpec((fields, *shape), lambda i: (0, *index(i)))

    x_spec = spec((yl, zl), lambda i: (0, 0))
    y_spec = spec((chunk, zl), lambda i: (i, 0))
    z_spec = spec((yl, width), lambda i: (0, 0))
    return [x_spec, x_spec, y_spec, y_spec, z_spec, z_spec]


def source_call(adjoint_seed, susceptibility, faces):
    xl, yl, zl = susceptibility.shape
    chunk = 8
    a, c = adjoint_seed, susceptibility
    return pl.pallas_call(
        functools.partial(source_body, chunk),
        grid=(xl // chunk,),
        in_specs=cell_specs(chunk, xl, yl, zl, True)
        + cell_specs(chunk, xl, yl, zl, False)
        + face_specs(chunk, yl, zl, lanes_of(max(xl, zl)), 7),
        out_specs=pl.BlockSpec((yl, chunk, zl), lambda i: (0, i, 0)),
        out_shape=jax.ShapeDtypeStruct((yl, xl, zl), jnp.float32),
        scratch_shapes=[pltpu.VMEM((4, chunk + 2, yl, zl), jnp.float32)],
        compiler_params=kernel_params,
    )(a, a, a, c, c, c, *faces)


def adjoint_cells_call(velocity, adjoint_seed, faces):
    _, xl, yl, zl = velocity.shape
    chunk = 8
    three = cell_specs(chunk, xl, yl, zl, True)
    v, a = velocity, adjoint_seed
    return pl.pallas_call(
        functools.partial(adjoint_cells_body, chunk),
        grid=(xl // chunk,),
        in_specs=three + three + face_specs(chunk, yl, zl, lanes_of(max(xl, zl)), 6),
        out_specs=three[0],
        out_shape=jax.ShapeDtypeStruct(v.shape, jnp.float32),
        scratch_shapes=[pltpu.VMEM((6, chunk + 2, yl, zl), jnp.float32)],
        compiler_params=kernel_params,
    )(v, v, v, a, a, a, *faces)


def next_cells_call(velocity, energy, susceptibility, faces, energy_faces):
    xl, yl, zl = susceptibility.shape
    chunk = 8
    three = cell_specs(chunk, xl, yl, zl, True)
    one = cell_specs(chunk, xl, yl, zl, False)
    width = lanes_of(max(xl, zl))
    energy_specs = [
        pl.BlockSpec((yl, zl), lambda i: (0, 0)),
        pl.BlockSpec((chunk, zl), lambda i: (i, 0)),
        pl.BlockSpec((yl, width), lambda i: (0, 0)),
    ]
    energy_specs = [spec for spec in energy_specs for _ in range(2)]
    v, e, c = velocity, energy, susceptibility
    return pl.pallas_call(
        functools.partial(next_cells_body, chunk),
        grid=(xl // chunk,),
        in_specs=three + one + one[:1] + face_specs(chunk, yl, zl, width, 3) + energy_specs,
        out_specs=three[0],
        out_shape=jax.ShapeDtypeStruct(v.shape, jnp.float32),
        scratch_shapes=[pltpu.VMEM((4, chunk + 2, yl, zl), jnp.float32)],
        compiler_params=kernel_params,
    )(v, v, v, e, e, e, c, *faces, *energy_faces)


def on_device(mesh, velocity, adjoint_seed, susceptibility, remanence, region_bounds, step_id):
    plan = Plan(mesh, susceptibility.shape)
    tables = make_tables(plan)
    places = [
        lax.axis_index(a) * n + jnp.arange(n, dtype=jnp.int32)
        for a, n in zip(axes, susceptibility.shape)
    ]
    inside = [
        (place >= region_bounds[0, d]) & (place < region_bounds[1, d])
        for d, place in enumerate(places)
    ]
    region_mask = (
        inside[0][:, None, None] & inside[1][None, :, None] & inside[2][None, None, :]
    ).astype(jnp.float32)
    def end_layers(done):
        ends = [
            jnp.concatenate([velocity[:, x], adjoint_seed[:, x], susceptibility[None, x]], axis=0)
            for x in (0, plan.xl - 1)
        ]
        return ends, faces_call(velocity, adjoint_seed, susceptibility)

    def neighbours(done):
        ends, (ylo, yhi, zlo, zhi) = done[0]
        faces = [
            *to_neighbours(*ends, "gx"), *to_neighbours(ylo, yhi, "gy"), *to_neighbours(zlo, zhi, "gz"),
        ]
        return faces, field_tables(plan, tables)

    def source_of(done):
        return source_call(adjoint_seed, susceptibility, done[1][0])

    def other_tables(done):
        angle = full_turn * (step_id[0] % field_period).astype(jnp.float32) / field_period
        applied = jnp.stack([jnp.cos(angle), jnp.sin(angle), jnp.zeros((), jnp.float32)])
        return applied, adjoint_tables(plan, tables)

    octant, done = gather_octant(
        plan,
        (remanence * region_mask).transpose(1, 0, 2),
        [end_layers, neighbours, source_of, other_tables],
    )
    _, (faces, there), source, (applied, back) = done
    own, other = field_call(plan, there, octant)
    field_adjoint, energy, ylo, yhi, zlo, zhi = combine_call(applied, own, swapped(other), source)
    energy_faces = [
        *to_neighbours(energy[0], energy[-1], "gx"), *to_neighbours(ylo, yhi, "gy"), *to_neighbours(zlo, zhi, "gz"),
    ]
    other, energy_faces = together(swapped(field_adjoint), energy_faces)
    sums = adjoint_call(plan, back, field_adjoint, other)
    sums, energy, faces = together(sums, energy, faces)

    def next_cells():
        return next_cells_call(velocity, energy, susceptibility, faces, energy_faces)

    def adjoint_cells():
        return adjoint_cells_call(velocity, adjoint_seed, faces)

    gradient, (next_velocity, velocity_adjoint) = owners_sum(plan, sums, [next_cells, adjoint_cells])
    design_gradient = region_mask * gradient.transpose(1, 0, 2)
    return (next_velocity, velocity_adjoint, design_gradient)


def solution(mesh):
    cells = P(*axes)
    vectors = P(None, *axes)
    return jax.shard_map(
        functools.partial(on_device, mesh),
        mesh=mesh,
        in_specs=(vectors, vectors, cells, cells, P(), P()),
        out_specs=(vectors, vectors, cells),
        check_vma=False,
    )
```

```python
import functools
import math

import jax
import jax.numpy as jnp
import ml_dtypes
import numpy as np
from jax import lax
from jax.experimental import pallas as pl
from jax.experimental.pallas import tpu as pltpu
from jax.sharding import PartitionSpec as P

time_step = 0.5
viscosity = 0.2
field_period = 24
full_turn = 2.0 * math.pi
bf16 = ml_dtypes.bfloat16
axes = ("gx", "gy", "gz")


def wave_tables(length):
    half = length // 2
    slot = np.arange(length)
    wave = np.where(slot <= half, slot, slot - half)
    angle = full_turn * (wave[:, None] * np.arange(length)[None, :] % length) / length
    weight = np.sqrt(np.where(slot % half == 0, 1.0, 2.0) / length)[:, None]
    odd = (slot > half)[:, None]
    kappa = full_turn * wave / length
    basis = np.where(odd, np.sin(angle), np.cos(angle)) * weight
    slope = np.where(odd, np.cos(angle), -np.sin(angle)) * weight * kappa[:, None]
    slope[half] = 0.0
    return basis, slope, kappa


def two_parts(table):
    high = table.astype(bf16)
    low = (table - high.astype(np.float64)).astype(bf16)
    return high, low


def split(value):
    high = value.astype(jnp.bfloat16)
    low = (value - high.astype(jnp.float32)).astype(jnp.bfloat16)
    return high, low


def dot(left, right):
    return jnp.dot(left, right, preferred_element_type=jnp.float32)


def twice_rows(table):
    high, low = two_parts(table)
    top = np.concatenate([high, high], axis=-1)
    return np.concatenate([top, np.concatenate([low, np.zeros_like(low)], axis=-1)], axis=-2)


def dot_rows(table, values):
    both = dot(table, jnp.concatenate(split(values), axis=0))
    half = both.shape[0] // 2
    return both[:half] + both[half:]


class Plan:
    def __init__(self, mesh, local):
        self.gx, self.gy, self.gz = (mesh.shape[a] for a in axes)
        self.xl, self.yl, self.zl = local
        self.nx, self.ny, self.nz = self.xl * self.gx, self.yl * self.gy, self.zl * self.gz
        self.x2, self.y2, self.z2 = self.nx // 2, self.ny // 2, self.nz // 2
        self.kx, self.kh = self.nx // 2, self.nx // 4
        self.yc = 2 * self.yl
        self.pitch = self.kx + 8
        self.px, self.py = self.xl // 4, self.yl // 2
        self.unroll = 2 if self.py % 4 == 0 else 1
        self.relay = (self.gx, self.gy, self.gz) == (2, 8, 2)
        self.arrays = 16 if self.relay else 1
        self.segments = self.relay_segments() if self.relay else self.gathered_segments()

    def gathered_segments(self):
        size = self.py * self.px
        return [
            [
                [
                    (0, ((first * self.gy + across) * self.gz + 2 * depth + side) * size)
                    for first in range(self.gx)
                    for side in range(2)
                ]
                for depth in range(self.gz // 2)
            ]
            for across in range(self.gy)
        ]

    def relay_segments(self):
        size = self.py * self.px
        segments = []
        for at in range(0, 16, 4):
            segments.append([[(at, 0), (at, size), (at + 1, 0), (at + 1, size)]])
            segments.append([[(at + 2, 0), (at + 3, 0), (at + 2, size), (at + 3, size)]])
        return segments

    def orders(self):
        x_orders = [
            np.concatenate([np.arange(self.px) + (column ^ r) * self.px for r in range(4)])
            for column in range(4)
        ]
        y_orders = []
        for side in range(2):
            for later in range(2):
                blocks = [2 * (half ^ later) + (side ^ far) for far in range(2) for half in range(2)]
                y_orders.append(np.concatenate([np.arange(self.yl) + block * self.yl for block in blocks]))
        return x_orders, y_orders


def make_tables(plan):
    bx, dx, wx = wave_tables(plan.nx)
    by, dy, wy = wave_tables(plan.ny)
    bz, dz, wz = wave_tables(plan.nz)
    hx, hy, hz = plan.nx // 2, plan.ny // 2, plan.nz // 2
    ez = bz.copy()
    ez[0] = bz[hz]
    z1 = dz.copy()
    z1[0] = 0.0
    z2 = dz.copy()
    z2[0] = -(np.pi**2) * bz[hz]
    z3 = -(wz**2)[:, None] * bz
    z3[0] = 0.0
    z1n = np.zeros_like(z1)
    z1n[hz] = -np.pi * bz[hz]
    xs = dx.copy()
    xs[hx] = np.pi * bx[hx]
    w3 = wz.copy()
    w3[0] = np.pi
    base = wy[:, None] ** 2 + w3[None, :] ** 2
    keep = np.ones_like(base, bool)
    keep[:, 0] = False
    keep[hy, 0] = True
    base = np.where(keep, base, 1e30).astype(np.float32)
    own = [np.arange(c * plan.kh, (c + 1) * plan.kh) for c in range(2)]
    own = [np.concatenate([cosines, hx + cosines]) for cosines in own]

    def by_side(table):
        return np.stack([table[slots] for slots in own])

    fx, fy = by_side(bx[:, : plan.x2]), by[None, :, : plan.y2]
    if plan.relay:
        x_orders, y_orders = plan.orders()
        fx = np.stack([part[:, order] for part in fx for order in x_orders])
        fy = np.stack([fy[0][:, order] for order in y_orders])
    return dict(
        fx=fx,
        fy=fy,
        xb=by_side(bx),
        xs=by_side(xs),
        w1=by_side((wx**2).astype(np.float32)),
        z1n=np.stack([z1n, z1]),
        ez=ez[:, : plan.z2],
        by=by,
        dy=dy,
        z1=z1,
        z2=z2,
        z3=z3,
        base=base,
    )


def pair_lanes(*arrays):
    return jnp.concatenate(arrays, axis=1)


def pair_rows(*arrays):
    return jnp.concatenate(arrays, axis=0)


def load_plane(refs, plan, segment, i):
    blocks = [
        pair_rows(*[refs[array][pl.ds(start + i * plan.px, plan.px), :] for array, start in runs])
        for runs in segment
    ]
    return blocks[0] if len(blocks) == 1 else pair_lanes(*blocks)


def store_plane(refs, plan, segment, i, value):
    for depth, runs in enumerate(segment):
        for place, (array, start) in enumerate(runs):
            refs[array][pl.ds(start + i * plan.px, plan.px), :] = value[
                place * plan.px : (place + 1) * plan.px, depth * plan.zl : (depth + 1) * plan.zl
            ]


def field_body(
    plan, group, places_ref, w1_ref,
    fx_ref, ez_ref, fy_ref, g_ref, z13_ref, z2_ref, z1n_ref, xs_ref, xb_ref, base_ref, *refs,
):
    kx, kh, pitch = plan.kx, plan.kh, plan.pitch
    w1_at = places_ref[8] * kx
    y2, z2, xl, yl, yc, zl = plan.y2, plan.z2, plan.xl, plan.yl, plan.yc, plan.zl
    span = yc * pitch
    m_refs, (own_ref, other_ref, s_ref, r_ref) = refs[: plan.arrays], refs[plan.arrays :]

    def along_x(number, segment):
        def body(step, carry):
            for pair in [plan.unroll * step + k for k in range(plan.unroll)]:
                planes = [load_plane(m_refs, plan, segment, 2 * pair + k) for k in range(2)]
                out = dot_rows(fx_ref[...], pair_lanes(*planes))
                row = (number * plan.py + 2 * pair) * pitch
                s_ref[pl.ds(row, kx), :] = out[:, :z2]
                s_ref[pl.ds(row + pitch, kx), :] = out[:, z2:]
            return carry

        lax.fori_loop(0, plan.py // 2 // plan.unroll, body, 0)

    for number, segment in enumerate(plan.segments):
        along_x(number, segment)

    def row_waves(slots):
        planes = pair_lanes(*[s_ref[pl.ds(slot, y2, stride=pitch), :] for slot in slots])
        out = dot_rows(fy_ref[...], planes)
        return [out[:, part * z2 : (part + 1) * z2] for part in range(len(slots))]

    def depth_waves(planes):
        high, low = split(pair_rows(*planes))
        return dot(pair_lanes(high, low, high), ez_ref[...])

    def one_slab(spectrum, kern):
        high, low = split(spectrum * kern)
        both = dot(g_ref[...], high)
        return both[: 2 * yc] + both[2 * yc :] + dot(g_ref[: 2 * yc], low)

    def two_products(high, low, table_ref):
        both = dot(high, table_ref[...])
        return both[:, :zl] + both[:, zl:] + dot(low, table_ref[:, :zl])

    def store(slots, cells, j):
        for place, slot in enumerate(slots):
            r_ref[pl.ds(j * span + slot, yc, stride=pitch), :] = cells[place * yc : (place + 1) * yc]

    def depth_cells(slots, slabs, edge):
        q1 = pair_rows(*[slab[:yc] for slab in slabs])
        q2 = pair_rows(*[slab[yc:] for slab in slabs])
        lane = lax.broadcasted_iota(jnp.int32, q1.shape, 1)
        q2 = jnp.where(lane == 0, q1, q2)
        high, low = split(q1)
        r13 = dot(pair_lanes(high, low, high), z13_ref[...])
        store(slots, two_products(high, low, z1n_ref) if edge else r13[:, :zl], 0)
        store(slots, r13[:, zl:], 2)
        store(slots, two_products(*split(q2), z2_ref), 1)

    def waves(step, carry):
        first = step * group
        slots = [first + k + part for k in range(group) for part in (0, kh)]
        planes = sum([row_waves(slots[2 * k : 2 * k + 2]) for k in range(group)], [])
        spectra = depth_waves(planes)
        slabs = []
        for k in range(group):
            kern = 1.0 / (base_ref[...] + w1_ref[w1_at + first + k])
            for part in range(2):
                at = (2 * k + part) * plan.ny
                slabs.append(one_slab(spectra[at : at + plan.ny], kern))
        depth_cells(slots, slabs, False)
        return carry

    lax.fori_loop(0, kh // group, waves, 0)

    spectrum = depth_waves(row_waves([kh]))
    depth_cells([kh], [one_slab(spectrum, 1.0 / (base_ref[...] + w1_ref[w1_at + kh]))], True)

    def back_x(mat_ref, values):
        return dot_rows(mat_ref[...], values)

    def cells(out_ref, shift):
        def body(pair, carry):
            here = [
                [pl.ds(j * span + (shift + 2 * pair + k) * pitch, kx) for k in range(2)]
                for j in range(3)
            ]
            h1 = back_x(xs_ref, pair_lanes(r_ref[here[0][0], :], r_ref[here[0][1], :]))
            for k in range(2):
                h23 = back_x(xb_ref, pair_lanes(r_ref[here[1][k], :], r_ref[here[2][k], :]))
                at = (2 * pair + k) * xl
                out_ref[pl.ds(at, xl), :] = h1[:, k * zl : (k + 1) * zl]
                out_ref[pl.ds(yl * xl + at, xl), :] = h23[:, :zl]
                out_ref[pl.ds(2 * yl * xl + at, xl), :] = h23[:, zl:]
            return carry

        lax.fori_loop(0, yl // 2, body, 0)

    cells(other_ref, yl)
    cells(own_ref, 0)


def adjoint_body(
    plan, group, places_ref, w1_ref,
    fx_ref, ez_ref, fy_ref, g_ref, z13_ref, z2_ref, z1n_ref, xs_ref, xb_ref, base_ref, own_ref, other_ref, *refs,
):
    kx, kh, pitch = plan.kx, plan.kh, plan.pitch
    w1_at = places_ref[8] * kx
    y2, z2, xl, yl, yc, zl = plan.y2, plan.z2, plan.xl, plan.yl, plan.yc, plan.zl
    span = yc * pitch
    m_refs, (s_ref, r_ref) = refs[: plan.arrays], refs[plan.arrays :]

    def along_x(mat_ref, values):
        return dot_rows(mat_ref[...], values)

    def cells(f_ref, shift):
        def body(pair, carry):
            here = [
                [pl.ds((j * yl + 2 * pair + k) * xl, xl) for k in range(2)] for j in range(3)
            ]
            u1 = along_x(xs_ref, pair_lanes(f_ref[here[0][0], :], f_ref[here[0][1], :]))
            for k in range(2):
                u23 = along_x(xb_ref, pair_lanes(f_ref[here[1][k], :], f_ref[here[2][k], :]))
                row = (shift + 2 * pair + k) * pitch
                r_ref[pl.ds(row, kx), :] = u1[:, k * zl : (k + 1) * zl]
                r_ref[pl.ds(span + row, kx), :] = u23[:, :zl]
                r_ref[pl.ds(2 * span + row, kx), :] = u23[:, zl:]
            return carry

        lax.fori_loop(0, yl // 2, body, 0)

    cells(own_ref, 0)
    cells(other_ref, yl)

    def depth_waves(slots, edge):
        u = [
            pair_rows(*[r_ref[pl.ds(j * span + slot, yc, stride=pitch), :] for slot in slots])
            for j in range(3)
        ]
        high1, low1 = split(u[0])
        high2, low2 = split(u[1])
        high3, low3 = split(u[2])
        high = pair_lanes(high1, high3)
        q1 = dot(pair_lanes(high, low1, low3, high), z13_ref[...])
        if edge:
            q1 = q1 + dot(pair_lanes(high1, low1, high1), z1n_ref[...])
        q2 = dot(pair_lanes(high2, low2, high2), z2_ref[...])
        first = lax.broadcasted_iota(jnp.int32, q1.shape, 1) == 0
        return jnp.where(first, q2, q1), jnp.where(first, 0.0, q2)

    def one_slab(q1, q2, kern):
        return dot_rows(g_ref[...], pair_rows(q1, q2)) * kern

    def depth_cells(spectra):
        high, low = split(pair_rows(*spectra))
        out = dot(high, ez_ref[...])
        return out[:, :z2] + out[:, z2:] + dot(low, ez_ref[:, :z2])

    def row_cells(slots, planes):
        high, low = split(pair_lanes(*planes))
        both = dot(fy_ref[...], high)
        out = both[:y2] + both[y2:] + dot(fy_ref[:y2], low)
        for part, slot in enumerate(slots):
            s_ref[pl.ds(slot, y2, stride=pitch), :] = out[:, part * z2 : (part + 1) * z2]

    def waves(step, carry):
        first = step * group
        slots = [first + k + part for k in range(group) for part in (0, kh)]
        q1, q2 = depth_waves(slots, False)
        spectra = []
        for k in range(group):
            kern = 1.0 / (base_ref[...] + w1_ref[w1_at + first + k])
            for part in range(2):
                take = slice((2 * k + part) * yc, (2 * k + part + 1) * yc)
                spectra.append(one_slab(q1[take], q2[take], kern))
        planes = depth_cells(spectra)
        planes = [planes[k * plan.ny : (k + 1) * plan.ny] for k in range(2 * group)]
        for k in range(group):
            row_cells(slots[2 * k : 2 * k + 2], planes[2 * k : 2 * k + 2])
        return carry

    lax.fori_loop(0, kh // group, waves, 0)

    q1, q2 = depth_waves([kh], True)
    row_cells([kh], [depth_cells([one_slab(q1, q2, 1.0 / (base_ref[...] + w1_ref[w1_at + kh]))])])

    def back_x(number, segment):
        def body(step, carry):
            for pair in [plan.unroll * step + k for k in range(plan.unroll)]:
                row = (number * plan.py + 2 * pair) * pitch
                planes = [s_ref[pl.ds(row + k * pitch, kx), :] for k in range(2)]
                out = dot_rows(fx_ref[...], pair_lanes(*planes))
                store_plane(m_refs, plan, segment, 2 * pair, out[:, :z2])
                store_plane(m_refs, plan, segment, 2 * pair + 1, out[:, z2:])
            return carry

        lax.fori_loop(0, plan.py // 2 // plan.unroll, body, 0)

    for number, segment in enumerate(plan.segments):
        back_x(number, segment)


vmem = pl.BlockSpec(memory_space=pltpu.VMEM)
smem = pl.BlockSpec(memory_space=pltpu.SMEM)
kernel_params = pltpu.CompilerParams(vmem_limit_bytes=60 * 2**20)


def scratch_of(plan):
    return [
        pltpu.VMEM((plan.y2 * plan.pitch, plan.z2), jnp.float32),
        pltpu.VMEM((3 * plan.yc * plan.pitch, plan.zl), jnp.float32),
    ]


def thrice_rows(table):
    high, low = two_parts(table)
    return np.concatenate([high, high, low], axis=-2)


def blocks_of(table, count, dim):
    return np.stack(np.split(table, table.shape[dim] // count, axis=dim))


def pair_blocks(table, count, dim):
    blocks = blocks_of(table, count, dim)
    order = np.arange(len(blocks))
    return np.concatenate([blocks, blocks[order + 1 - 2 * (order % 2)]], axis=dim + 1)


def by_side_blocks(tables, count, dim):
    return np.concatenate([blocks_of(table, count, dim) for table in tables])


def parts_over(table):
    return np.concatenate(two_parts(table), axis=-2)


def parts_beside(table):
    return np.concatenate(two_parts(table), axis=-1)


def places_of(plan):
    first, second, third = [lax.axis_index(a) for a in axes]
    side = lax.rem(second, 2)
    fx, fy = side, jnp.zeros_like(side)
    if plan.relay:
        fx = 4 * side + 2 * first + third
        fy = 2 * side + jnp.minimum(second // 2, 1)
    x_place = side * plan.gx + first
    return jnp.stack([fx, fy, second, third, third, side * plan.gz + third, x_place, x_place, side])


def field_tables(plan, t):
    xl, yl, zl = plan.xl, plan.yl, plan.zl
    z13 = np.concatenate([blocks_of(t[name], zl, 1) for name in ("z1", "z3")], axis=2)
    g = np.concatenate([pair_blocks(t[name].T, yl, 0) for name in ("by", "dy")], axis=1)
    return [
        twice_rows(t["fx"]), thrice_rows(t["ez"].T), twice_rows(t["fy"]), parts_over(g), thrice_rows(z13),
        parts_beside(blocks_of(t["z2"], zl, 1)), parts_beside(by_side_blocks(t["z1n"], zl, 1)),
        twice_rows(by_side_blocks([m.T for m in t["xs"]], xl, 0)),
        twice_rows(by_side_blocks([m.T for m in t["xb"]], xl, 0)), t["base"],
    ]


def adjoint_tables(plan, t):
    xl, yl, zl = plan.xl, plan.yl, plan.zl
    z13 = np.concatenate([blocks_of(t[name].T, zl, 0) for name in ("z1", "z3")], axis=1)
    g = np.concatenate([pair_blocks(t[name], yl, 1) for name in ("by", "dy")], axis=2)
    edge = [(table - t["z1"]).T for table in t["z1n"]]
    return [
        twice_rows(t["fx"].swapaxes(1, 2)), parts_beside(t["ez"]), parts_over(t["fy"].swapaxes(1, 2)), twice_rows(g),
        thrice_rows(z13), thrice_rows(blocks_of(t["z2"].T, zl, 0)), thrice_rows(by_side_blocks(edge, zl, 0)),
        twice_rows(by_side_blocks(t["xs"], xl, 1)), twice_rows(by_side_blocks(t["xb"], xl, 1)), t["base"],
    ]


table_places = (0, None, 1, 2, 3, 4, 5, 6, 7, None)


def spectral_call(plan, body, places, w1, tables, arrays, out_shape):
    def table_spec(table, place):
        if place is None:
            return vmem
        return pl.BlockSpec((None, *table.shape[1:]), lambda i, places_ref: (places_ref[place], 0, 0))

    return pl.pallas_call(
        functools.partial(body, plan, min(8, plan.kh)),
        out_shape=out_shape,
        grid_spec=pltpu.PrefetchScalarGridSpec(
            num_scalar_prefetch=1,
            grid=(1,),
            in_specs=[smem]
            + [table_spec(table, place) for table, place in zip(tables, table_places)]
            + [vmem] * len(arrays),
            out_specs=[vmem] * len(out_shape),
            scratch_shapes=scratch_of(plan),
        ),
        compiler_params=kernel_params,
    )(places, jnp.asarray(w1.reshape(-1)), *[jnp.asarray(table) for table in tables], *arrays)


def field_call(plan, tables, places, octant):
    xl, yl, zl = plan.xl, plan.yl, plan.zl
    shape = jax.ShapeDtypeStruct((3 * yl * xl, zl), jnp.float32)
    own, other = spectral_call(
        plan, field_body, places, tables["w1"], field_tables(plan, tables), octant, [shape, shape]
    )
    return own.reshape(3, yl, xl, zl), other.reshape(3, yl, xl, zl)


def adjoint_call(plan, tables, places, own, other):
    zl = plan.zl
    rows = plan.x2 * plan.y2 * plan.z2 // zl // plan.arrays
    fields = [own.reshape(-1, zl), other.reshape(-1, zl)]
    shape = jax.ShapeDtypeStruct((rows, zl), jnp.float32)
    return spectral_call(
        plan, adjoint_body, places, tables["w1"], adjoint_tables(plan, tables), fields, [shape] * plan.arrays
    )


def swapped(array):
    count = lax.axis_size("gy")
    return lax.ppermute(array, "gy", [(i, i + 1 - 2 * (i % 2)) for i in range(count)])


def spread(block, axis, dim):
    count = lax.axis_size(axis)
    halves = jnp.split(block, 2, axis=dim)
    moved = [
        lax.ppermute(half, axis, [(s, 2 * s + k) for s in range(count // 2)])
        for k, half in enumerate(halves)
    ]
    return moved[0] + moved[1]


def unspread(piece, axis, dim):
    count = lax.axis_size(axis)
    moved = [
        lax.ppermute(piece, axis, [(2 * s + k, s) for s in range(count // 2)]) for k in range(2)
    ]
    return jnp.concatenate(moved, axis=dim)


def gather_octant(plan, quarters, work):
    if plan.relay:
        return relay_octant(plan, quarters, work)
    done = []
    for step in work:
        done.append(step(done))
    piece = jnp.concatenate([q.reshape(plan.yl, plan.px, plan.zl) for q in quarters], axis=1)
    for axis, dim in (("gx", 1), ("gz", 1), ("gy", 0)):
        piece = spread(piece, axis, dim)
    return [lax.all_gather(piece.reshape(plan.py * plan.px, plan.zl), axes, tiled=True)], done


def owners_sum(plan, sums, work):
    if plan.relay:
        return relay_sums(plan, sums, work)
    done = []
    for step in work:
        done.append(step(done))
    piece = lax.psum_scatter(sums[0], axes, scatter_dimension=0, tiled=True)
    piece = piece.reshape(plan.py, plan.px, plan.zl)
    return unspread(unspread(unspread(piece, "gy", 0), "gz", 1), "gx", 1), done


flip = [(0, 1), (1, 0)]


def along(array, pairs):
    return lax.ppermute(array, "gy", [(2 * a + c, 2 * b + c) for a, b in pairs for c in range(2)])


def together(*values):
    return lax.optimization_barrier(values)


def relay_octant(plan, quarters, work):
    z = lax.axis_index("gy") // 2
    done = []
    moved = [lax.ppermute(quarters[r], ("gx", "gz"), [(0, r)]) for r in range(1, 4)]
    moved, result = together(moved, work[0](done))
    done.append(result)
    piece = quarters[0] + moved[0] + moved[1] + moved[2]
    up = along(piece, [(0, 1), (1, 2)])
    down = along(piece, [(1, 0)])
    up2 = along(up, [(1, 2), (2, 3)])
    up2, result = together(up2, work[1](done))
    up3 = along(up2, [(2, 3)])
    first = across_once(plan, jnp.where(z < 2, piece, jnp.where(z == 2, up, up2)))
    first, result = together(first, result)
    done.append(result)
    first = across_twice(first)
    up3, result = together(up3, [step(done) for step in work[2:]])
    done.extend(result)
    second = jnp.where(z == 0, down, jnp.where(z == 1, up, jnp.where(z == 2, up2, up3)))
    own = first + across_twice(across_once(plan, second))
    return own + [swapped(array) for array in own], done


def across_once(plan, piece):
    half = plan.py * plan.px
    low, high = piece[:half], piece[half:]
    return pair_rows(low, lax.ppermute(low, "gz", flip)), pair_rows(high, lax.ppermute(high, "gx", flip))


def across_twice(pairs):
    a, b = pairs
    return [a, lax.ppermute(a, "gx", flip), b, lax.ppermute(b, "gz", flip)]


def across_halves(arrays):
    a, ay, b, bx = arrays
    return lax.ppermute(ay, "gx", flip), lax.ppermute(bx, "gz", flip)


def across_sums(plan, arrays, halves):
    half = plan.py * plan.px
    a, b = arrays[0] + halves[0], arrays[2] + halves[1]
    low = a[:half] + lax.ppermute(a[half:], "gz", flip)
    high = b[:half] + lax.ppermute(b[half:], "gx", flip)
    return pair_rows(low, high)


def relay_sums(plan, sums, work):
    z = lax.axis_index("gy") // 2
    own = [sums[i] + swapped(sums[i + 8]) for i in (4, 5, 6, 7, 0, 1, 2, 3)]
    done = []
    halves, result = together(across_halves(own[:4]), work[0](done))
    done.append(result)
    second, *own[4:] = together(across_sums(plan, own[:4], halves), *own[4:])
    down = along(second, [(3, 2)])
    up = along(second, [(0, 1)])
    halves = across_halves(own[4:])
    down, halves, result = together(down, halves, work[1](done))
    done.append(result)
    second = second + down
    down = along(second, [(2, 1)])
    first = across_sums(plan, own[4:], halves)
    down, first, result = together(down, first, work[2](done))
    done.append(result)
    second = second + down
    down = along(second, [(1, 0)])
    down2 = along(first, [(3, 2)])
    down, down2, result = together(down, down2, work[3](done))
    done.append(result)
    first = first + down2
    first = first + up + down + along(first, [(2, 1)])
    quarters = [first] + [lax.ppermute(first, ("gx", "gz"), [(r, 0)]) for r in range(1, 4)]
    block = jnp.concatenate([q.reshape(plan.yl, plan.px, plan.zl) for q in quarters], axis=1)
    return block, done


def magnet_body(plan, from_ref, to_ref, rem_ref, *out_refs):
    yl, px, zl = plan.yl, plan.px, plan.zl
    lane = lax.broadcasted_iota(jnp.int32, (px, zl), 1)
    row = lax.broadcasted_iota(jnp.int32, (px, zl), 0)
    in_z = (lane >= from_ref[2]) & (lane < to_ref[2])
    for r, out_ref in enumerate(out_refs):
        inside = in_z & (row + r * px >= from_ref[0]) & (row + r * px < to_ref[0])

        def plane(y, carry, inside=inside, out_ref=out_ref, r=r):
            here = inside & (y >= from_ref[1]) & (y < to_ref[1])
            values = rem_ref[pl.ds(r * px * yl + y, px, stride=yl), :]
            out_ref[pl.ds(y * px, px), :] = jnp.where(here, values, 0.0)
            return carry

        lax.fori_loop(0, yl, plane, 0)


def magnet_call(plan, remanence, bounds):
    shape = jax.ShapeDtypeStruct((plan.yl * plan.px, plan.zl), jnp.float32)
    return pl.pallas_call(
        functools.partial(magnet_body, plan),
        out_shape=[shape] * 4,
        in_specs=[smem, smem, vmem],
        out_specs=[vmem] * 4,
        compiler_params=kernel_params,
    )(bounds[0], bounds[1], remanence.reshape(-1, plan.zl))


def lanes_of(count):
    return -(-count // 128) * 128


def faces_body(chunk, v_ref, a_ref, c_ref, ylo_ref, yhi_ref, zlo_ref, zhi_ref):
    yl, zl = v_ref.shape[2:]
    step = pl.program_id(0)

    @pl.when(step == 0)
    def _():
        zlo_ref[...] = jnp.zeros_like(zlo_ref)
        zhi_ref[...] = jnp.zeros_like(zhi_ref)

    lane = lax.broadcasted_iota(jnp.int32, zlo_ref.shape[1:], 1)
    for field in range(7):
        low, high = zlo_ref[field], zhi_ref[field]
        for k in range(chunk):
            plane = v_ref[field, k] if field < 3 else a_ref[field - 3, k] if field < 6 else c_ref[k]
            ylo_ref[field, k : k + 1, :] = plane[:1]
            yhi_ref[field, k : k + 1, :] = plane[yl - 1 :]
            here = lane == step * chunk + k
            low = jnp.where(here, plane[:, :1], low)
            high = jnp.where(here, plane[:, zl - 1 :], high)
        zlo_ref[field] = low
        zhi_ref[field] = high


def faces_call(velocity, adjoint_seed, susceptibility):
    xl, yl, zl = susceptibility.shape
    chunk = 8
    three = pl.BlockSpec((3, chunk, yl, zl), lambda i: (0, i, 0, 0))
    y_spec = pl.BlockSpec((7, chunk, zl), lambda i: (0, i, 0))
    z_spec = pl.BlockSpec((7, yl, lanes_of(max(xl, zl))), lambda i: (0, 0, 0))
    y_shape = jax.ShapeDtypeStruct((7, xl, zl), jnp.float32)
    z_shape = jax.ShapeDtypeStruct((7, yl, lanes_of(max(xl, zl))), jnp.float32)
    return pl.pallas_call(
        functools.partial(faces_body, chunk),
        grid=(xl // chunk,),
        in_specs=[three, three, pl.BlockSpec((chunk, yl, zl), lambda i: (i, 0, 0))],
        out_specs=[y_spec, y_spec, z_spec, z_spec],
        out_shape=[y_shape, y_shape, z_shape, z_shape],
        compiler_params=kernel_params,
    )(velocity, adjoint_seed, susceptibility)


def to_neighbours(low_face, high_face, axis):
    count = lax.axis_size(axis)
    if count == 2:
        lower = lax.axis_index(axis) == 0
        other = lax.ppermute(jnp.where(lower, high_face, low_face), axis, [(0, 1), (1, 0)])
        return jnp.where(lower, 0.0, other), jnp.where(lower, other, 0.0)
    below = lax.ppermute(high_face, axis, [(i, i + 1) for i in range(count - 1)])
    above = lax.ppermute(low_face, axis, [(i + 1, i) for i in range(count - 1)])
    return below, above


def combine_body(chunk, app_ref, own_ref, arrived_ref, source_ref, f_ref, e_ref, ylo_ref, yhi_ref, zlo_ref, zhi_ref):
    yl, _, zl = source_ref.shape
    step = pl.program_id(0)

    @pl.when(step == 0)
    def _():
        zlo_ref[...] = jnp.zeros_like(zlo_ref)
        zhi_ref[...] = jnp.zeros_like(zhi_ref)

    energy = 0.0
    for j in range(3):
        total = own_ref[j] + arrived_ref[j] + app_ref[j]
        f_ref[j] = source_ref[...] * total
        energy = energy + total * total
    energy = 0.5 * energy
    lane = lax.broadcasted_iota(jnp.int32, zlo_ref.shape, 1)
    low, high = zlo_ref[...], zhi_ref[...]
    for k in range(chunk):
        plane = energy[:, k, :]
        e_ref[k] = plane
        ylo_ref[k : k + 1, :] = plane[:1]
        yhi_ref[k : k + 1, :] = plane[yl - 1 :]
        here = lane == step * chunk + k
        low = jnp.where(here, plane[:, :1], low)
        high = jnp.where(here, plane[:, zl - 1 :], high)
    zlo_ref[...] = low
    zhi_ref[...] = high


def combine_call(applied, own, arrived, source):
    _, yl, xl, zl = own.shape
    chunk = 16
    width = lanes_of(max(xl, zl))
    three = pl.BlockSpec((3, yl, chunk, zl), lambda i: (0, 0, i, 0))
    y_spec = pl.BlockSpec((chunk, zl), lambda i: (i, 0))
    z_spec = pl.BlockSpec((yl, width), lambda i: (0, 0))
    shapes = [(3, yl, xl, zl), (xl, yl, zl), (xl, zl), (xl, zl), (yl, width), (yl, width)]
    return pl.pallas_call(
        functools.partial(combine_body, chunk),
        grid=(xl // chunk,),
        in_specs=[smem, three, three, pl.BlockSpec((yl, chunk, zl), lambda i: (0, i, 0))],
        out_specs=[
            three, pl.BlockSpec((chunk, yl, zl), lambda i: (i, 0, 0)), y_spec, y_spec, z_spec, z_spec,
        ],
        out_shape=[jax.ShapeDtypeStruct(shape, jnp.float32) for shape in shapes],
        compiler_params=kernel_params,
    )(applied, own, arrived, source)


class Around:
    def __init__(self, ref, k, x, y_below, y_above, z_below, z_above):
        mid = ref[k + 1]
        yl, zl = mid.shape
        row = lax.broadcasted_iota(jnp.int32, mid.shape, 0)
        lane = lax.broadcasted_iota(jnp.int32, mid.shape, 1)
        width = z_below.shape[1]
        left = pltpu.roll(z_below, lax.rem(width - x, width), 1)[:, :zl]
        right = pltpu.roll(z_above, lax.rem(width + zl - 1 - x, width), 1)[:, :zl]
        self.mid = mid
        self.less = [
            ref[k],
            jnp.where(row == 0, y_below, pltpu.roll(mid, 1, 0)),
            jnp.where(lane == 0, left, pltpu.roll(mid, 1, 1)),
        ]
        self.more = [
            ref[k + 2],
            jnp.where(row == yl - 1, y_above, pltpu.roll(mid, yl - 1, 0)),
            jnp.where(lane == zl - 1, right, pltpu.roll(mid, zl - 1, 1)),
        ]

    def slope(self, d):
        return (self.more[d] - self.less[d]) * 0.5

    def laplace(self):
        beside = self.more[0] + self.less[0] + self.more[1] + self.less[1]
        return beside + self.more[2] + self.less[2] - 6.0 * self.mid


def fill_window(window, chunk, field, before, block, after, x_below, x_above, step=None, last=None):
    step = pl.program_id(0) if step is None else step
    last = pl.num_programs(0) - 1 if last is None else last
    for k in range(chunk):
        window[field, k + 1] = block(k)
    window[field, 0] = jnp.where(step == 0, x_below, before)
    window[field, chunk + 1] = jnp.where(step == last, x_above, after)


def source_body(
    chunk, a_ref, ab_ref, aa_ref, c_ref, cb_ref, ca_ref,
    xlo_ref, xhi_ref, ylo_ref, yhi_ref, zlo_ref, zhi_ref, source_ref, window,
):
    for j in range(3):
        fill_window(window, chunk, j, ab_ref[j, 0], lambda k: a_ref[j, k], aa_ref[j, 0], xlo_ref[3 + j], xhi_ref[3 + j])
    fill_window(window, chunk, 3, cb_ref[0], lambda k: c_ref[k], ca_ref[0], xlo_ref[6], xhi_ref[6])
    start = pl.program_id(0) * chunk

    def plane(k, carry):
        at = [
            Around(
                window.at[f], k, start + k,
                ylo_ref[3 + f, pl.ds(k, 1), :], yhi_ref[3 + f, pl.ds(k, 1), :], zlo_ref[3 + f], zhi_ref[3 + f],
            )
            for f in range(4)
        ]
        a, c = at[:3], at[3]
        flux = [c.more[i] * a[i].more[i] - c.less[i] * a[i].less[i] for i in range(3)]
        source_ref[:, k, :] = (-0.5 * time_step) * (flux[0] + flux[1] + flux[2])
        return carry

    lax.fori_loop(0, chunk, plane, 0)


def adjoint_cells_body(
    chunk, begin, last, v_ref, vb_ref, va_ref, a_ref, ab_ref, aa_ref,
    xlo_ref, xhi_ref, ylo_ref, yhi_ref, zlo_ref, zhi_ref, *refs,
):
    out_ref, window = refs[-2:]
    step = pl.program_id(0) + begin
    for j in range(3):
        fill_window(window, chunk, j, vb_ref[j, 0], lambda k: v_ref[j, k], va_ref[j, 0], xlo_ref[j], xhi_ref[j], step, last)
        fill_window(window, chunk, 3 + j, ab_ref[j, 0], lambda k: a_ref[j, k], aa_ref[j, 0], xlo_ref[3 + j], xhi_ref[3 + j], step, last)
    start = step * chunk

    def plane(k, carry):
        at = [
            Around(
                window.at[f], k, start + k,
                ylo_ref[f, pl.ds(k, 1), :], yhi_ref[f, pl.ds(k, 1), :], zlo_ref[f], zhi_ref[f],
            )
            for f in range(6)
        ]
        v, a = at[:3], at[3:]
        for j in range(3):
            shear = sum(a[i].mid * (v[i].more[j] - v[i].less[j]) for i in range(3))
            carried = sum(v[i].more[i] * a[j].more[i] - v[i].less[i] * a[j].less[i] for i in range(3))
            out_ref[j, k] = a[j].mid + time_step * (
                viscosity * a[j].laplace() + 0.5 * (carried - shear)
            )
        return carry

    lax.fori_loop(0, chunk, plane, 0)


def next_cells_body(
    chunk, begin, last, v_ref, vb_ref, va_ref, e_ref, eb_ref, ea_ref, c_ref,
    xlo_ref, xhi_ref, ylo_ref, yhi_ref, zlo_ref, zhi_ref,
    exlo_ref, exhi_ref, eylo_ref, eyhi_ref, ezlo_ref, ezhi_ref, *refs,
):
    out_ref, window = refs[-2:]
    step = pl.program_id(0) + begin
    for j in range(3):
        fill_window(window, chunk, j, vb_ref[j, 0], lambda k: v_ref[j, k], va_ref[j, 0], xlo_ref[j], xhi_ref[j], step, last)
    fill_window(window, chunk, 3, eb_ref[0], lambda k: e_ref[k], ea_ref[0], exlo_ref[...], exhi_ref[...], step, last)
    start = step * chunk

    def plane(k, carry):
        v = [
            Around(
                window.at[f], k, start + k,
                ylo_ref[f, pl.ds(k, 1), :], yhi_ref[f, pl.ds(k, 1), :], zlo_ref[f], zhi_ref[f],
            )
            for f in range(3)
        ]
        e = Around(
            window.at[3], k, start + k,
            eylo_ref[pl.ds(k, 1), :], eyhi_ref[pl.ds(k, 1), :], ezlo_ref[...], ezhi_ref[...],
        )
        for j in range(3):
            advect = sum(v[i].mid * (v[j].more[i] - v[j].less[i]) for i in range(3))
            pushed = c_ref[k] * (e.more[j] - e.less[j])
            out_ref[j, k] = v[j].mid + time_step * (
                viscosity * v[j].laplace() + 0.5 * (pushed - advect)
            )
        return carry

    lax.fori_loop(0, chunk, plane, 0)


def cell_specs(chunk, xl, yl, zl, lead, begin=0):
    def at(block, place):
        if lead:
            return pl.BlockSpec((3, block, yl, zl), lambda i: (0, place(i + begin), 0, 0))
        return pl.BlockSpec((block, yl, zl), lambda i: (place(i + begin), 0, 0))

    return [
        at(chunk, lambda i: i),
        at(1, lambda i: jnp.maximum(i * chunk - 1, 0)),
        at(1, lambda i: jnp.minimum((i + 1) * chunk, xl - 1)),
    ]


def face_specs(chunk, yl, zl, width, fields, begin=0):
    def spec(shape, index):
        return pl.BlockSpec((fields, *shape), lambda i: (0, *index(i)))

    x_spec = spec((yl, zl), lambda i: (0, 0))
    y_spec = spec((chunk, zl), lambda i: (i + begin, 0))
    z_spec = spec((yl, width), lambda i: (0, 0))
    return [x_spec, x_spec, y_spec, y_spec, z_spec, z_spec]


def source_call(adjoint_seed, susceptibility, faces):
    xl, yl, zl = susceptibility.shape
    chunk = 8
    a, c = adjoint_seed, susceptibility
    return pl.pallas_call(
        functools.partial(source_body, chunk),
        grid=(xl // chunk,),
        in_specs=cell_specs(chunk, xl, yl, zl, True)
        + cell_specs(chunk, xl, yl, zl, False)
        + face_specs(chunk, yl, zl, lanes_of(max(xl, zl)), 7),
        out_specs=pl.BlockSpec((yl, chunk, zl), lambda i: (0, i, 0)),
        out_shape=jax.ShapeDtypeStruct((yl, xl, zl), jnp.float32),
        scratch_shapes=[pltpu.VMEM((4, chunk + 2, yl, zl), jnp.float32)],
        compiler_params=kernel_params,
    )(a, a, a, c, c, c, *faces)


def adjoint_cells_call(velocity, adjoint_seed, faces, part, earlier):
    _, xl, yl, zl = velocity.shape
    chunk = 8
    steps = xl // chunk // 2
    begin = part * steps
    specs = cell_specs(chunk, xl, yl, zl, True, begin)
    v, a = velocity, adjoint_seed
    return pl.pallas_call(
        functools.partial(adjoint_cells_body, chunk, begin, xl // chunk - 1),
        grid=(steps,),
        in_specs=specs
        + specs
        + face_specs(chunk, yl, zl, lanes_of(max(xl, zl)), 6, begin)
        + [pl.BlockSpec(memory_space=pl.ANY)] * part,
        out_specs=specs[0],
        out_shape=jax.ShapeDtypeStruct(v.shape, jnp.float32),
        scratch_shapes=[pltpu.VMEM((6, chunk + 2, yl, zl), jnp.float32)],
        input_output_aliases={12: 0} if part else {},
        compiler_params=kernel_params,
    )(v, v, v, a, a, a, *faces, *earlier)


def next_cells_call(velocity, energy, susceptibility, faces, energy_faces, part, earlier):
    xl, yl, zl = susceptibility.shape
    chunk = 8
    steps = xl // chunk // 2
    begin = part * steps
    three = cell_specs(chunk, xl, yl, zl, True, begin)
    one = cell_specs(chunk, xl, yl, zl, False, begin)
    width = lanes_of(max(xl, zl))
    energy_specs = [
        pl.BlockSpec((yl, zl), lambda i: (0, 0)),
        pl.BlockSpec((chunk, zl), lambda i: (i + begin, 0)),
        pl.BlockSpec((yl, width), lambda i: (0, 0)),
    ]
    energy_specs = [spec for spec in energy_specs for _ in range(2)]
    v, e, c = velocity, energy, susceptibility
    return pl.pallas_call(
        functools.partial(next_cells_body, chunk, begin, xl // chunk - 1),
        grid=(steps,),
        in_specs=three
        + one
        + one[:1]
        + face_specs(chunk, yl, zl, width, 3, begin)
        + energy_specs
        + [pl.BlockSpec(memory_space=pl.ANY)] * part,
        out_specs=three[0],
        out_shape=jax.ShapeDtypeStruct(v.shape, jnp.float32),
        scratch_shapes=[pltpu.VMEM((4, chunk + 2, yl, zl), jnp.float32)],
        input_output_aliases={19: 0} if part else {},
        compiler_params=kernel_params,
    )(v, v, v, e, e, e, c, *faces, *energy_faces, *earlier)


def on_device(mesh, velocity, adjoint_seed, susceptibility, remanence, region_bounds, step_id):
    plan = Plan(mesh, susceptibility.shape)
    tables = make_tables(plan)
    corner = jnp.stack([lax.axis_index(a) * n for a, n in zip(axes, susceptibility.shape)])
    bounds = region_bounds - corner[None, :]
    place = [jnp.arange(n, dtype=jnp.int32) for n in susceptibility.shape]
    inside = [(p >= bounds[0, d]) & (p < bounds[1, d]) for d, p in enumerate(place)]
    region_mask = inside[0][:, None, None] & inside[1][None, :, None] & inside[2][None, None, :]

    def end_layers(done):
        ends = [
            jnp.concatenate([velocity[:, x], adjoint_seed[:, x], susceptibility[None, x]], axis=0)
            for x in (0, plan.xl - 1)
        ]
        return ends, faces_call(velocity, adjoint_seed, susceptibility)

    def neighbours(done):
        ends, (ylo, yhi, zlo, zhi) = done[0]
        faces = [
            *to_neighbours(*ends, "gx"), *to_neighbours(ylo, yhi, "gy"), *to_neighbours(zlo, zhi, "gz"),
        ]
        return faces, places_of(plan)

    def source_of(done):
        return source_call(adjoint_seed, susceptibility, done[1][0])

    def applied_field(done):
        angle = full_turn * (step_id[0] % field_period).astype(jnp.float32) / field_period
        applied = jnp.stack([jnp.cos(angle), jnp.sin(angle), jnp.zeros((), jnp.float32)])
        return applied

    octant, done = gather_octant(
        plan,
        magnet_call(plan, remanence, bounds),
        [end_layers, neighbours, source_of, applied_field],
    )
    _, (faces, places), source, applied = done
    own, other = field_call(plan, tables, places, octant)
    field_adjoint, energy, ylo, yhi, zlo, zhi = combine_call(applied, own, swapped(other), source)
    energy_faces = [
        *to_neighbours(energy[0], energy[-1], "gx"), *to_neighbours(ylo, yhi, "gy"), *to_neighbours(zlo, zhi, "gz"),
    ]
    other, energy_faces = together(swapped(field_adjoint), energy_faces)
    sums = adjoint_call(plan, tables, places, field_adjoint, other)
    sums, energy, faces = together(sums, energy, faces)

    def next_cells(part):
        return lambda done: next_cells_call(
            velocity, energy, susceptibility, faces, energy_faces, part, done[:part]
        )

    def adjoint_cells(part):
        return lambda done: adjoint_cells_call(
            velocity, adjoint_seed, faces, part, done[2 : 2 + part]
        )

    gradient, (_, next_velocity, _, velocity_adjoint) = owners_sum(
        plan, sums, [next_cells(0), next_cells(1), adjoint_cells(0), adjoint_cells(1)]
    )
    design_gradient = jnp.where(region_mask, gradient.transpose(1, 0, 2), 0.0)
    return (next_velocity, velocity_adjoint, design_gradient)


def solution(mesh):
    cells = P(*axes)
    vectors = P(None, *axes)
    return jax.shard_map(
        functools.partial(on_device, mesh),
        mesh=mesh,
        in_specs=(vectors, vectors, cells, cells, P(), P()),
        out_specs=(vectors, vectors, cells),
        check_vma=False,
    )
```

```python
import functools
import math

import jax
import jax.numpy as jnp
import ml_dtypes
import numpy as np
from jax import lax
from jax.experimental import pallas as pl
from jax.experimental.pallas import tpu as pltpu
from jax.sharding import PartitionSpec as P

time_step = 0.5
viscosity = 0.2
field_period = 24
full_turn = 2.0 * math.pi
bf16 = ml_dtypes.bfloat16
axes = ("gx", "gy", "gz")


def wave_tables(length):
    half = length // 2
    slot = np.arange(length)
    wave = np.where(slot <= half, slot, slot - half)
    angle = full_turn * (wave[:, None] * np.arange(length)[None, :] % length) / length
    weight = np.sqrt(np.where(slot % half == 0, 1.0, 2.0) / length)[:, None]
    odd = (slot > half)[:, None]
    kappa = full_turn * wave / length
    basis = np.where(odd, np.sin(angle), np.cos(angle)) * weight
    slope = np.where(odd, np.cos(angle), -np.sin(angle)) * weight * kappa[:, None]
    slope[half] = 0.0
    return basis, slope, kappa


def two_parts(table):
    high = table.astype(bf16)
    low = (table - high.astype(np.float64)).astype(bf16)
    return high, low


def split(value):
    high = value.astype(jnp.bfloat16)
    low = (value - high.astype(jnp.float32)).astype(jnp.bfloat16)
    return high, low


def dot(left, right):
    return jnp.dot(left, right, preferred_element_type=jnp.float32)


def twice_rows(table):
    high, low = two_parts(table)
    top = np.concatenate([high, high], axis=-1)
    return np.concatenate([top, np.concatenate([low, np.zeros_like(low)], axis=-1)], axis=-2)


def dot_rows(table, values):
    both = dot(table, jnp.concatenate(split(values), axis=0))
    half = both.shape[0] // 2
    return both[:half] + both[half:]


class Plan:
    def __init__(self, mesh, local):
        self.gx, self.gy, self.gz = (mesh.shape[a] for a in axes)
        self.xl, self.yl, self.zl = local
        self.nx, self.ny, self.nz = self.xl * self.gx, self.yl * self.gy, self.zl * self.gz
        self.x2, self.y2, self.z2 = self.nx // 2, self.ny // 2, self.nz // 2
        self.kx, self.kh = self.nx // 2, self.nx // 4
        self.yc = 2 * self.yl
        self.pitch = self.kx + 8
        self.px, self.py = self.xl // 4, self.yl // 2
        self.unroll = 2 if self.py % 4 == 0 else 1
        self.relay = (self.gx, self.gy, self.gz) == (2, 8, 2)
        self.arrays = 16 if self.relay else 1
        self.segments = self.relay_segments() if self.relay else self.gathered_segments()

    def gathered_segments(self):
        size = self.py * self.px
        return [
            [
                [
                    (0, ((first * self.gy + across) * self.gz + 2 * depth + side) * size)
                    for first in range(self.gx)
                    for side in range(2)
                ]
                for depth in range(self.gz // 2)
            ]
            for across in range(self.gy)
        ]

    def relay_segments(self):
        size = self.py * self.px
        segments = []
        for at in range(0, 16, 4):
            segments.append([[(at, 0), (at, size), (at + 1, 0), (at + 1, size)]])
            segments.append([[(at + 2, 0), (at + 3, 0), (at + 2, size), (at + 3, size)]])
        return segments

    def orders(self):
        x_orders = [
            np.concatenate([np.arange(self.px) + (column ^ r) * self.px for r in range(4)])
            for column in range(4)
        ]
        y_orders = []
        for side in range(2):
            for later in range(2):
                blocks = [2 * (half ^ later) + (side ^ far) for far in range(2) for half in range(2)]
                y_orders.append(np.concatenate([np.arange(self.yl) + block * self.yl for block in blocks]))
        return x_orders, y_orders


def make_tables(plan):
    bx, dx, wx = wave_tables(plan.nx)
    by, dy, wy = wave_tables(plan.ny)
    bz, dz, wz = wave_tables(plan.nz)
    hx, hy, hz = plan.nx // 2, plan.ny // 2, plan.nz // 2
    ez = bz.copy()
    ez[0] = bz[hz]
    z1 = dz.copy()
    z1[0] = 0.0
    z2 = dz.copy()
    z2[0] = -(np.pi**2) * bz[hz]
    z3 = -(wz**2)[:, None] * bz
    z3[0] = 0.0
    z1n = np.zeros_like(z1)
    z1n[hz] = -np.pi * bz[hz]
    xs = dx.copy()
    xs[hx] = np.pi * bx[hx]
    w3 = wz.copy()
    w3[0] = np.pi
    base = wy[:, None] ** 2 + w3[None, :] ** 2
    keep = np.ones_like(base, bool)
    keep[:, 0] = False
    keep[hy, 0] = True
    base = np.where(keep, base, 1e30).astype(np.float32)
    own = [np.arange(c * plan.kh, (c + 1) * plan.kh) for c in range(2)]
    own = [np.concatenate([cosines, hx + cosines]) for cosines in own]

    def by_side(table):
        return np.stack([table[slots] for slots in own])

    fx, fy = by_side(bx[:, : plan.x2]), by[None, :, : plan.y2]
    if plan.relay:
        x_orders, y_orders = plan.orders()
        fx = np.stack([part[:, order] for part in fx for order in x_orders])
        fy = np.stack([fy[0][:, order] for order in y_orders])
    return dict(
        fx=fx,
        fy=fy,
        xb=by_side(bx),
        xs=by_side(xs),
        w1=by_side((wx**2).astype(np.float32)),
        z1n=np.stack([z1n, z1]),
        ez=ez[:, : plan.z2],
        by=by,
        dy=dy,
        z1=z1,
        z2=z2,
        z3=z3,
        base=base,
    )


def pair_lanes(*arrays):
    return jnp.concatenate(arrays, axis=1)


def pair_rows(*arrays):
    return jnp.concatenate(arrays, axis=0)


def load_plane(refs, plan, segment, i):
    blocks = [
        pair_rows(*[refs[array][pl.ds(start + i * plan.px, plan.px), :] for array, start in runs])
        for runs in segment
    ]
    return blocks[0] if len(blocks) == 1 else pair_lanes(*blocks)


def store_plane(refs, plan, segment, i, value):
    for depth, runs in enumerate(segment):
        for place, (array, start) in enumerate(runs):
            refs[array][pl.ds(start + i * plan.px, plan.px), :] = value[
                place * plan.px : (place + 1) * plan.px, depth * plan.zl : (depth + 1) * plan.zl
            ]


def field_body(
    plan, group, places_ref, w1_ref,
    fx_ref, ez_ref, fy_ref, g_ref, z13_ref, z2_ref, z1n_ref, xs_ref, xb_ref, base_ref, *refs,
):
    kx, kh, pitch = plan.kx, plan.kh, plan.pitch
    w1_at = places_ref[8] * kx
    y2, z2, xl, yl, yc, zl = plan.y2, plan.z2, plan.xl, plan.yl, plan.yc, plan.zl
    span = yc * pitch
    m_refs, (own_ref, other_ref, s_ref, r_ref) = refs[: plan.arrays], refs[plan.arrays :]

    def along_x(number, segment):
        def body(step, carry):
            for pair in [plan.unroll * step + k for k in range(plan.unroll)]:
                planes = [load_plane(m_refs, plan, segment, 2 * pair + k) for k in range(2)]
                out = dot_rows(fx_ref[...], pair_lanes(*planes))
                row = (number * plan.py + 2 * pair) * pitch
                s_ref[pl.ds(row, kx), :] = out[:, :z2]
                s_ref[pl.ds(row + pitch, kx), :] = out[:, z2:]
            return carry

        lax.fori_loop(0, plan.py // 2 // plan.unroll, body, 0)

    for number, segment in enumerate(plan.segments):
        along_x(number, segment)

    def row_waves(slots):
        planes = pair_lanes(*[s_ref[pl.ds(slot, y2, stride=pitch), :] for slot in slots])
        out = dot_rows(fy_ref[...], planes)
        return [out[:, part * z2 : (part + 1) * z2] for part in range(len(slots))]

    def depth_waves(planes):
        high, low = split(pair_rows(*planes))
        return dot(pair_lanes(high, low, high), ez_ref[...])

    def one_slab(spectrum, kern):
        high, low = split(spectrum * kern)
        both = dot(g_ref[...], high)
        return both[: 2 * yc] + both[2 * yc :] + dot(g_ref[: 2 * yc], low)

    def two_products(high, low, table_ref):
        both = dot(high, table_ref[...])
        return both[:, :zl] + both[:, zl:] + dot(low, table_ref[:, :zl])

    def store(slots, cells, j):
        for place, slot in enumerate(slots):
            r_ref[pl.ds(j * span + slot, yc, stride=pitch), :] = cells[place * yc : (place + 1) * yc]

    def depth_cells(slots, slabs, edge):
        q1 = pair_rows(*[slab[:yc] for slab in slabs])
        q2 = pair_rows(*[slab[yc:] for slab in slabs])
        lane = lax.broadcasted_iota(jnp.int32, q1.shape, 1)
        q2 = jnp.where(lane == 0, q1, q2)
        high, low = split(q1)
        r13 = dot(pair_lanes(high, low, high), z13_ref[...])
        store(slots, two_products(high, low, z1n_ref) if edge else r13[:, :zl], 0)
        store(slots, r13[:, zl:], 2)
        store(slots, two_products(*split(q2), z2_ref), 1)

    def waves(step, carry):
        first = step * group
        slots = [first + k + part for k in range(group) for part in (0, kh)]
        planes = sum([row_waves(slots[2 * k : 2 * k + 2]) for k in range(group)], [])
        spectra = depth_waves(planes)
        slabs = []
        for k in range(group):
            kern = 1.0 / (base_ref[...] + w1_ref[w1_at + first + k])
            for part in range(2):
                at = (2 * k + part) * plan.ny
                slabs.append(one_slab(spectra[at : at + plan.ny], kern))
        depth_cells(slots, slabs, False)
        return carry

    lax.fori_loop(0, kh // group, waves, 0)

    spectrum = depth_waves(row_waves([kh]))
    depth_cells([kh], [one_slab(spectrum, 1.0 / (base_ref[...] + w1_ref[w1_at + kh]))], True)

    def back_x(mat_ref, values):
        return dot_rows(mat_ref[...], values)

    def cells(out_ref, shift):
        def body(pair, carry):
            here = [
                [pl.ds(j * span + (shift + 2 * pair + k) * pitch, kx) for k in range(2)]
                for j in range(3)
            ]
            h1 = back_x(xs_ref, pair_lanes(r_ref[here[0][0], :], r_ref[here[0][1], :]))
            for k in range(2):
                h23 = back_x(xb_ref, pair_lanes(r_ref[here[1][k], :], r_ref[here[2][k], :]))
                at = (2 * pair + k) * xl
                out_ref[pl.ds(at, xl), :] = h1[:, k * zl : (k + 1) * zl]
                out_ref[pl.ds(yl * xl + at, xl), :] = h23[:, :zl]
                out_ref[pl.ds(2 * yl * xl + at, xl), :] = h23[:, zl:]
            return carry

        lax.fori_loop(0, yl // 2, body, 0)

    cells(other_ref, yl)
    cells(own_ref, 0)


def adjoint_body(
    plan, group, places_ref, w1_ref,
    fx_ref, ez_ref, fy_ref, g_ref, z13_ref, z2_ref, z1n_ref, xs_ref, xb_ref, base_ref, own_ref, other_ref, *refs,
):
    kx, kh, pitch = plan.kx, plan.kh, plan.pitch
    w1_at = places_ref[8] * kx
    y2, z2, xl, yl, yc, zl = plan.y2, plan.z2, plan.xl, plan.yl, plan.yc, plan.zl
    span = yc * pitch
    m_refs, (s_ref, r_ref) = refs[: plan.arrays], refs[plan.arrays :]

    def along_x(mat_ref, values):
        return dot_rows(mat_ref[...], values)

    def cells(f_ref, shift):
        def body(pair, carry):
            here = [
                [pl.ds((j * yl + 2 * pair + k) * xl, xl) for k in range(2)] for j in range(3)
            ]
            u1 = along_x(xs_ref, pair_lanes(f_ref[here[0][0], :], f_ref[here[0][1], :]))
            for k in range(2):
                u23 = along_x(xb_ref, pair_lanes(f_ref[here[1][k], :], f_ref[here[2][k], :]))
                row = (shift + 2 * pair + k) * pitch
                r_ref[pl.ds(row, kx), :] = u1[:, k * zl : (k + 1) * zl]
                r_ref[pl.ds(span + row, kx), :] = u23[:, :zl]
                r_ref[pl.ds(2 * span + row, kx), :] = u23[:, zl:]
            return carry

        lax.fori_loop(0, yl // 2, body, 0)

    cells(own_ref, 0)
    cells(other_ref, yl)

    def depth_waves(slots, edge):
        u = [
            pair_rows(*[r_ref[pl.ds(j * span + slot, yc, stride=pitch), :] for slot in slots])
            for j in range(3)
        ]
        high1, low1 = split(u[0])
        high2, low2 = split(u[1])
        high3, low3 = split(u[2])
        high = pair_lanes(high1, high3)
        q1 = dot(pair_lanes(high, low1, low3, high), z13_ref[...])
        if edge:
            q1 = q1 + dot(pair_lanes(high1, low1, high1), z1n_ref[...])
        q2 = dot(pair_lanes(high2, low2, high2), z2_ref[...])
        first = lax.broadcasted_iota(jnp.int32, q1.shape, 1) == 0
        return jnp.where(first, q2, q1), jnp.where(first, 0.0, q2)

    def one_slab(q1, q2, kern):
        return dot_rows(g_ref[...], pair_rows(q1, q2)) * kern

    def depth_cells(spectra):
        high, low = split(pair_rows(*spectra))
        out = dot(high, ez_ref[...])
        return out[:, :z2] + out[:, z2:] + dot(low, ez_ref[:, :z2])

    def row_cells(slots, planes):
        high, low = split(pair_lanes(*planes))
        both = dot(fy_ref[...], high)
        out = both[:y2] + both[y2:] + dot(fy_ref[:y2], low)
        for part, slot in enumerate(slots):
            s_ref[pl.ds(slot, y2, stride=pitch), :] = out[:, part * z2 : (part + 1) * z2]

    def waves(step, carry):
        first = step * group
        slots = [first + k + part for k in range(group) for part in (0, kh)]
        q1, q2 = depth_waves(slots, False)
        spectra = []
        for k in range(group):
            kern = 1.0 / (base_ref[...] + w1_ref[w1_at + first + k])
            for part in range(2):
                take = slice((2 * k + part) * yc, (2 * k + part + 1) * yc)
                spectra.append(one_slab(q1[take], q2[take], kern))
        planes = depth_cells(spectra)
        planes = [planes[k * plan.ny : (k + 1) * plan.ny] for k in range(2 * group)]
        for k in range(group):
            row_cells(slots[2 * k : 2 * k + 2], planes[2 * k : 2 * k + 2])
        return carry

    lax.fori_loop(0, kh // group, waves, 0)

    q1, q2 = depth_waves([kh], True)
    row_cells([kh], [depth_cells([one_slab(q1, q2, 1.0 / (base_ref[...] + w1_ref[w1_at + kh]))])])

    def back_x(number, segment):
        def body(step, carry):
            for pair in [plan.unroll * step + k for k in range(plan.unroll)]:
                row = (number * plan.py + 2 * pair) * pitch
                planes = [s_ref[pl.ds(row + k * pitch, kx), :] for k in range(2)]
                out = dot_rows(fx_ref[...], pair_lanes(*planes))
                store_plane(m_refs, plan, segment, 2 * pair, out[:, :z2])
                store_plane(m_refs, plan, segment, 2 * pair + 1, out[:, z2:])
            return carry

        lax.fori_loop(0, plan.py // 2 // plan.unroll, body, 0)

    for number, segment in enumerate(plan.segments):
        back_x(number, segment)


vmem = pl.BlockSpec(memory_space=pltpu.VMEM)
smem = pl.BlockSpec(memory_space=pltpu.SMEM)
kernel_params = pltpu.CompilerParams(vmem_limit_bytes=60 * 2**20)


def scratch_of(plan):
    return [
        pltpu.VMEM((plan.y2 * plan.pitch, plan.z2), jnp.float32),
        pltpu.VMEM((3 * plan.yc * plan.pitch, plan.zl), jnp.float32),
    ]


def thrice_rows(table):
    high, low = two_parts(table)
    return np.concatenate([high, high, low], axis=-2)


def blocks_of(table, count, dim):
    return np.stack(np.split(table, table.shape[dim] // count, axis=dim))


def pair_blocks(table, count, dim):
    blocks = blocks_of(table, count, dim)
    order = np.arange(len(blocks))
    return np.concatenate([blocks, blocks[order + 1 - 2 * (order % 2)]], axis=dim + 1)


def by_side_blocks(tables, count, dim):
    return np.concatenate([blocks_of(table, count, dim) for table in tables])


def parts_over(table):
    return np.concatenate(two_parts(table), axis=-2)


def parts_beside(table):
    return np.concatenate(two_parts(table), axis=-1)


def places_of(plan):
    first, second, third = [lax.axis_index(a) for a in axes]
    side = lax.rem(second, 2)
    fx, fy = side, jnp.zeros_like(side)
    if plan.relay:
        fx = 4 * side + 2 * first + third
        fy = 2 * side + jnp.minimum(second // 2, 1)
    x_place = side * plan.gx + first
    return jnp.stack([fx, fy, second, third, third, side * plan.gz + third, x_place, x_place, side])


def field_tables(plan, t):
    xl, yl, zl = plan.xl, plan.yl, plan.zl
    z13 = np.concatenate([blocks_of(t[name], zl, 1) for name in ("z1", "z3")], axis=2)
    g = np.concatenate([pair_blocks(t[name].T, yl, 0) for name in ("by", "dy")], axis=1)
    return [
        twice_rows(t["fx"]), thrice_rows(t["ez"].T), twice_rows(t["fy"]), parts_over(g), thrice_rows(z13),
        parts_beside(blocks_of(t["z2"], zl, 1)), parts_beside(by_side_blocks(t["z1n"], zl, 1)),
        twice_rows(by_side_blocks([m.T for m in t["xs"]], xl, 0)),
        twice_rows(by_side_blocks([m.T for m in t["xb"]], xl, 0)), t["base"],
    ]


def adjoint_tables(plan, t):
    xl, yl, zl = plan.xl, plan.yl, plan.zl
    z13 = np.concatenate([blocks_of(t[name].T, zl, 0) for name in ("z1", "z3")], axis=1)
    g = np.concatenate([pair_blocks(t[name], yl, 1) for name in ("by", "dy")], axis=2)
    edge = [(table - t["z1"]).T for table in t["z1n"]]
    return [
        twice_rows(t["fx"].swapaxes(1, 2)), parts_beside(t["ez"]), parts_over(t["fy"].swapaxes(1, 2)), twice_rows(g),
        thrice_rows(z13), thrice_rows(blocks_of(t["z2"].T, zl, 0)), thrice_rows(by_side_blocks(edge, zl, 0)),
        twice_rows(by_side_blocks(t["xs"], xl, 1)), twice_rows(by_side_blocks(t["xb"], xl, 1)), t["base"],
    ]


table_places = (0, None, 1, 2, 3, 4, 5, 6, 7, None)


def spectral_call(plan, body, places, w1, tables, arrays, out_shape):
    def table_spec(table, place):
        if place is None:
            return vmem
        return pl.BlockSpec((None, *table.shape[1:]), lambda i, places_ref: (places_ref[place], 0, 0))

    return pl.pallas_call(
        functools.partial(body, plan, min(8, plan.kh)),
        out_shape=out_shape,
        grid_spec=pltpu.PrefetchScalarGridSpec(
            num_scalar_prefetch=1,
            grid=(1,),
            in_specs=[smem]
            + [table_spec(table, place) for table, place in zip(tables, table_places)]
            + [vmem] * len(arrays),
            out_specs=[vmem] * len(out_shape),
            scratch_shapes=scratch_of(plan),
        ),
        compiler_params=kernel_params,
    )(places, jnp.asarray(w1.reshape(-1)), *[jnp.asarray(table) for table in tables], *arrays)


def field_call(plan, tables, places, octant):
    xl, yl, zl = plan.xl, plan.yl, plan.zl
    shape = jax.ShapeDtypeStruct((3 * yl * xl, zl), jnp.float32)
    own, other = spectral_call(
        plan, field_body, places, tables["w1"], field_tables(plan, tables), octant, [shape, shape]
    )
    return own.reshape(3, yl, xl, zl), other.reshape(3, yl, xl, zl)


def adjoint_call(plan, tables, places, own, other):
    zl = plan.zl
    rows = plan.x2 * plan.y2 * plan.z2 // zl // plan.arrays
    fields = [own.reshape(-1, zl), other.reshape(-1, zl)]
    shape = jax.ShapeDtypeStruct((rows, zl), jnp.float32)
    return spectral_call(
        plan, adjoint_body, places, tables["w1"], adjoint_tables(plan, tables), fields, [shape] * plan.arrays
    )


def swapped(array):
    count = lax.axis_size("gy")
    return lax.ppermute(array, "gy", [(i, i + 1 - 2 * (i % 2)) for i in range(count)])


def spread(block, axis, dim):
    count = lax.axis_size(axis)
    halves = jnp.split(block, 2, axis=dim)
    moved = [
        lax.ppermute(half, axis, [(s, 2 * s + k) for s in range(count // 2)])
        for k, half in enumerate(halves)
    ]
    return moved[0] + moved[1]


def unspread(piece, axis, dim):
    count = lax.axis_size(axis)
    moved = [
        lax.ppermute(piece, axis, [(2 * s + k, s) for s in range(count // 2)]) for k in range(2)
    ]
    return jnp.concatenate(moved, axis=dim)


def gather_octant(plan, quarters, work):
    if plan.relay:
        return relay_octant(plan, quarters, work)
    done = []
    for step in work:
        done.append(step(done))
    piece = jnp.concatenate([q.reshape(plan.yl, plan.px, plan.zl) for q in quarters], axis=1)
    for axis, dim in (("gx", 1), ("gz", 1), ("gy", 0)):
        piece = spread(piece, axis, dim)
    return [lax.all_gather(piece.reshape(plan.py * plan.px, plan.zl), axes, tiled=True)], done


def owners_sum(plan, sums, work, late):
    if plan.relay:
        return relay_sums(plan, sums, work, late)
    done = [work[0]([])]
    done += [work[1](done), work[2](late)]
    piece = lax.psum_scatter(sums[0], axes, scatter_dimension=0, tiled=True)
    piece = piece.reshape(plan.py, plan.px, plan.zl)
    return unspread(unspread(unspread(piece, "gy", 0), "gz", 1), "gx", 1), done


flip = [(0, 1), (1, 0)]


def along(array, pairs):
    return lax.ppermute(array, "gy", [(2 * a + c, 2 * b + c) for a, b in pairs for c in range(2)])


def together(*values):
    return lax.optimization_barrier(values)


def to_column(array, start, end):
    return lax.ppermute(array, ("gx", "gz"), [(start, end)])


def relay_octant(plan, quarters, work):
    z = lax.axis_index("gy") // 2
    done = []
    half = plan.py * plan.px
    near = [to_column(quarters[r], 0, r) for r in (1, 2)]
    via = [to_column(quarters[3][:half], 0, 1), to_column(quarters[3][half:], 0, 2)]
    via = [to_column(via[0], 1, 3), to_column(via[1], 2, 3)]
    piece = quarters[0] + near[0] + near[1] + pair_rows(*via)
    up = along(piece, [(0, 1), (1, 2)])
    down = along(piece, [(1, 0)])
    up, result = together(up, work[0](done))
    done.append(result)
    up2 = along(up, [(1, 2), (2, 3)])
    up3 = along(up2, [(2, 3)])
    first = across_once(plan, jnp.where(z < 2, piece, jnp.where(z == 2, up, up2)))
    first, result = together(first, work[1](done))
    done.append(result)
    first = across_twice(first)
    second = jnp.where(z == 0, down, jnp.where(z == 1, up, jnp.where(z == 2, up2, up3)))
    second, done[1] = together(across_once(plan, second), done[1])
    second, result = together(across_twice(second), [step(done) for step in work[2:]])
    done.extend(result)
    own = first + second
    return own + [swapped(array) for array in own], done


def across_once(plan, piece):
    half = plan.py * plan.px
    low, high = piece[:half], piece[half:]
    return pair_rows(low, lax.ppermute(low, "gz", flip)), pair_rows(high, lax.ppermute(high, "gx", flip))


def across_twice(pairs):
    a, b = pairs
    return [a, lax.ppermute(a, "gx", flip), b, lax.ppermute(b, "gz", flip)]


def across_halves(arrays):
    a, ay, b, bx = arrays
    return lax.ppermute(ay, "gx", flip), lax.ppermute(bx, "gz", flip)


def across_sums(plan, arrays, halves):
    half = plan.py * plan.px
    a, b = arrays[0] + halves[0], arrays[2] + halves[1]
    low = a[:half] + lax.ppermute(a[half:], "gz", flip)
    high = b[:half] + lax.ppermute(b[half:], "gx", flip)
    return pair_rows(low, high)


def relay_sums(plan, sums, work, late):
    z = lax.axis_index("gy") // 2
    own = [sums[i] + swapped(sums[i + 8]) for i in (4, 5, 6, 7, 0, 1, 2, 3)]
    done = []
    halves, result = together(across_halves(own[:4]), work[0](done))
    done.append(result)
    second, *own[4:] = together(across_sums(plan, own[:4], halves), *own[4:])
    down = along(second, [(3, 2)])
    up = along(second, [(0, 1)])
    halves = across_halves(own[4:])
    down, halves, result = together(down, halves, work[1](done))
    done.append(result)
    second = second + down
    down = along(second, [(2, 1)])
    first = across_sums(plan, own[4:], halves)
    down2 = along(first, [(3, 2)])
    second = second + down
    down = along(second, [(1, 0)])
    first = first + down2
    first = first + up + down + along(first, [(2, 1)])
    half = plan.py * plan.px
    first, late = together(first, late)
    near = [to_column(first, r, 0) for r in (1, 2)]
    via = [to_column(first[:half], 3, 1), to_column(first[half:], 3, 2)]
    via = [to_column(via[0], 1, 0), to_column(via[1], 2, 0)]
    near, via, result = together(near, via, work[2](late))
    done.append(result)
    quarters = [first, *near, pair_rows(*via)]
    block = jnp.concatenate([q.reshape(plan.yl, plan.px, plan.zl) for q in quarters], axis=1)
    return block, done


def magnet_body(plan, from_ref, to_ref, rem_ref, *out_refs):
    yl, px, zl = plan.yl, plan.px, plan.zl
    lane = lax.broadcasted_iota(jnp.int32, (px, zl), 1)
    row = lax.broadcasted_iota(jnp.int32, (px, zl), 0)
    in_z = (lane >= from_ref[2]) & (lane < to_ref[2])
    for r, out_ref in enumerate(out_refs):
        inside = in_z & (row + r * px >= from_ref[0]) & (row + r * px < to_ref[0])

        def plane(y, carry, inside=inside, out_ref=out_ref, r=r):
            here = inside & (y >= from_ref[1]) & (y < to_ref[1])
            values = rem_ref[pl.ds(r * px * yl + y, px, stride=yl), :]
            out_ref[pl.ds(y * px, px), :] = jnp.where(here, values, 0.0)
            return carry

        lax.fori_loop(0, yl, plane, 0, unroll=4)


def magnet_call(plan, remanence, bounds):
    shape = jax.ShapeDtypeStruct((plan.yl * plan.px, plan.zl), jnp.float32)
    return pl.pallas_call(
        functools.partial(magnet_body, plan),
        out_shape=[shape] * 4,
        in_specs=[smem, smem, vmem],
        out_specs=[vmem] * 4,
        compiler_params=kernel_params,
    )(bounds[0], bounds[1], remanence.reshape(-1, plan.zl))


def lanes_of(count):
    return -(-count // 128) * 128


def faces_body(chunk, v_ref, a_ref, c_ref, ylo_ref, yhi_ref, zlo_ref, zhi_ref):
    yl, zl = v_ref.shape[2:]
    step = pl.program_id(0)

    @pl.when(step == 0)
    def _():
        zlo_ref[...] = jnp.zeros_like(zlo_ref)
        zhi_ref[...] = jnp.zeros_like(zhi_ref)

    lane = lax.broadcasted_iota(jnp.int32, zlo_ref.shape[1:], 1)
    for field in range(7):
        low, high = zlo_ref[field], zhi_ref[field]
        for k in range(chunk):
            plane = v_ref[field, k] if field < 3 else a_ref[field - 3, k] if field < 6 else c_ref[k]
            ylo_ref[field, k : k + 1, :] = plane[:1]
            yhi_ref[field, k : k + 1, :] = plane[yl - 1 :]
            here = lane == step * chunk + k
            low = jnp.where(here, plane[:, :1], low)
            high = jnp.where(here, plane[:, zl - 1 :], high)
        zlo_ref[field] = low
        zhi_ref[field] = high


def faces_call(velocity, adjoint_seed, susceptibility):
    xl, yl, zl = susceptibility.shape
    chunk = 16
    three = pl.BlockSpec((3, chunk, yl, zl), lambda i: (0, i, 0, 0))
    y_spec = pl.BlockSpec((7, chunk, zl), lambda i: (0, i, 0))
    z_spec = pl.BlockSpec((7, yl, lanes_of(max(xl, zl))), lambda i: (0, 0, 0))
    y_shape = jax.ShapeDtypeStruct((7, xl, zl), jnp.float32)
    z_shape = jax.ShapeDtypeStruct((7, yl, lanes_of(max(xl, zl))), jnp.float32)
    return pl.pallas_call(
        functools.partial(faces_body, chunk),
        grid=(xl // chunk,),
        in_specs=[three, three, pl.BlockSpec((chunk, yl, zl), lambda i: (i, 0, 0))],
        out_specs=[y_spec, y_spec, z_spec, z_spec],
        out_shape=[y_shape, y_shape, z_shape, z_shape],
        compiler_params=kernel_params,
    )(velocity, adjoint_seed, susceptibility)


def to_neighbours(low_face, high_face, axis):
    count = lax.axis_size(axis)
    if count == 2:
        lower = lax.axis_index(axis) == 0
        other = lax.ppermute(jnp.where(lower, high_face, low_face), axis, [(0, 1), (1, 0)])
        return jnp.where(lower, 0.0, other), jnp.where(lower, other, 0.0)
    below = lax.ppermute(high_face, axis, [(i, i + 1) for i in range(count - 1)])
    above = lax.ppermute(low_face, axis, [(i + 1, i) for i in range(count - 1)])
    return below, above


def combine_body(chunk, app_ref, own_ref, arrived_ref, source_ref, f_ref, e_ref, ylo_ref, yhi_ref, zlo_ref, zhi_ref):
    yl, _, zl = source_ref.shape
    step = pl.program_id(0)

    @pl.when(step == 0)
    def _():
        zlo_ref[...] = jnp.zeros_like(zlo_ref)
        zhi_ref[...] = jnp.zeros_like(zhi_ref)

    energy = 0.0
    for j in range(3):
        total = own_ref[j] + arrived_ref[j] + app_ref[j]
        f_ref[j] = source_ref[...] * total
        energy = energy + total * total
    energy = 0.5 * energy
    lane = lax.broadcasted_iota(jnp.int32, zlo_ref.shape, 1)
    low, high = zlo_ref[...], zhi_ref[...]
    for k in range(chunk):
        plane = energy[:, k, :]
        e_ref[k] = plane
        ylo_ref[k : k + 1, :] = plane[:1]
        yhi_ref[k : k + 1, :] = plane[yl - 1 :]
        here = lane == step * chunk + k
        low = jnp.where(here, plane[:, :1], low)
        high = jnp.where(here, plane[:, zl - 1 :], high)
    zlo_ref[...] = low
    zhi_ref[...] = high


def combine_call(applied, own, arrived, source):
    _, yl, xl, zl = own.shape
    chunk = 32
    width = lanes_of(max(xl, zl))
    three = pl.BlockSpec((3, yl, chunk, zl), lambda i: (0, 0, i, 0))
    y_spec = pl.BlockSpec((chunk, zl), lambda i: (i, 0))
    z_spec = pl.BlockSpec((yl, width), lambda i: (0, 0))
    shapes = [(3, yl, xl, zl), (xl, yl, zl), (xl, zl), (xl, zl), (yl, width), (yl, width)]
    return pl.pallas_call(
        functools.partial(combine_body, chunk),
        grid=(xl // chunk,),
        in_specs=[smem, three, three, pl.BlockSpec((yl, chunk, zl), lambda i: (0, i, 0))],
        out_specs=[
            three, pl.BlockSpec((chunk, yl, zl), lambda i: (i, 0, 0)), y_spec, y_spec, z_spec, z_spec,
        ],
        out_shape=[jax.ShapeDtypeStruct(shape, jnp.float32) for shape in shapes],
        compiler_params=kernel_params,
    )(applied, own, arrived, source)


class Around:
    def __init__(self, ref, k, x, y_below, y_above, z_below, z_above):
        mid = ref[k + 1]
        yl, zl = mid.shape
        row = lax.broadcasted_iota(jnp.int32, mid.shape, 0)
        lane = lax.broadcasted_iota(jnp.int32, mid.shape, 1)
        width = z_below.shape[1]
        left = pltpu.roll(z_below, lax.rem(width - x, width), 1)[:, :zl]
        right = pltpu.roll(z_above, lax.rem(width + zl - 1 - x, width), 1)[:, :zl]
        self.mid = mid
        self.less = [
            ref[k],
            jnp.where(row == 0, y_below, pltpu.roll(mid, 1, 0)),
            jnp.where(lane == 0, left, pltpu.roll(mid, 1, 1)),
        ]
        self.more = [
            ref[k + 2],
            jnp.where(row == yl - 1, y_above, pltpu.roll(mid, yl - 1, 0)),
            jnp.where(lane == zl - 1, right, pltpu.roll(mid, zl - 1, 1)),
        ]

    def slope(self, d):
        return (self.more[d] - self.less[d]) * 0.5

    def laplace(self):
        beside = self.more[0] + self.less[0] + self.more[1] + self.less[1]
        return beside + self.more[2] + self.less[2] - 6.0 * self.mid


def fill_window(window, chunk, field, before, block, after, x_below, x_above, step=None, last=None):
    step = pl.program_id(0) if step is None else step
    last = pl.num_programs(0) - 1 if last is None else last
    for k in range(chunk):
        window[field, k + 1] = block(k)
    window[field, 0] = jnp.where(step == 0, x_below, before)
    window[field, chunk + 1] = jnp.where(step == last, x_above, after)


def source_body(
    chunk, a_ref, ab_ref, aa_ref, c_ref, cb_ref, ca_ref,
    xlo_ref, xhi_ref, ylo_ref, yhi_ref, zlo_ref, zhi_ref, source_ref, window,
):
    for j in range(3):
        fill_window(window, chunk, j, ab_ref[j, 0], lambda k: a_ref[j, k], aa_ref[j, 0], xlo_ref[3 + j], xhi_ref[3 + j])
    fill_window(window, chunk, 3, cb_ref[0], lambda k: c_ref[k], ca_ref[0], xlo_ref[6], xhi_ref[6])
    start = pl.program_id(0) * chunk

    def plane(k, carry):
        at = [
            Around(
                window.at[f], k, start + k,
                ylo_ref[3 + f, pl.ds(k, 1), :], yhi_ref[3 + f, pl.ds(k, 1), :], zlo_ref[3 + f], zhi_ref[3 + f],
            )
            for f in range(4)
        ]
        a, c = at[:3], at[3]
        flux = [c.more[i] * a[i].more[i] - c.less[i] * a[i].less[i] for i in range(3)]
        source_ref[:, k, :] = (-0.5 * time_step) * (flux[0] + flux[1] + flux[2])
        return carry

    lax.fori_loop(0, chunk, plane, 0, unroll=4)


def adjoint_cells_body(
    chunk, begin, last, v_ref, vb_ref, va_ref, a_ref, ab_ref, aa_ref,
    xlo_ref, xhi_ref, ylo_ref, yhi_ref, zlo_ref, zhi_ref, *refs,
):
    out_ref, window = refs[-2:]
    step = pl.program_id(0) + begin
    for j in range(3):
        fill_window(window, chunk, j, vb_ref[j, 0], lambda k: v_ref[j, k], va_ref[j, 0], xlo_ref[j], xhi_ref[j], step, last)
        fill_window(window, chunk, 3 + j, ab_ref[j, 0], lambda k: a_ref[j, k], aa_ref[j, 0], xlo_ref[3 + j], xhi_ref[3 + j], step, last)
    start = step * chunk

    def plane(k, carry):
        at = [
            Around(
                window.at[f], k, start + k,
                ylo_ref[f, pl.ds(k, 1), :], yhi_ref[f, pl.ds(k, 1), :], zlo_ref[f], zhi_ref[f],
            )
            for f in range(6)
        ]
        v, a = at[:3], at[3:]
        for j in range(3):
            shear = sum(a[i].mid * (v[i].more[j] - v[i].less[j]) for i in range(3))
            carried = sum(v[i].more[i] * a[j].more[i] - v[i].less[i] * a[j].less[i] for i in range(3))
            out_ref[j, k] = a[j].mid + time_step * (
                viscosity * a[j].laplace() + 0.5 * (carried - shear)
            )
        return carry

    lax.fori_loop(0, chunk, plane, 0, unroll=4)


def next_cells_body(
    chunk, begin, last, v_ref, vb_ref, va_ref, e_ref, eb_ref, ea_ref, c_ref,
    xlo_ref, xhi_ref, ylo_ref, yhi_ref, zlo_ref, zhi_ref,
    exlo_ref, exhi_ref, eylo_ref, eyhi_ref, ezlo_ref, ezhi_ref, *refs,
):
    out_ref, window = refs[-2:]
    step = pl.program_id(0) + begin
    for j in range(3):
        fill_window(window, chunk, j, vb_ref[j, 0], lambda k: v_ref[j, k], va_ref[j, 0], xlo_ref[j], xhi_ref[j], step, last)
    fill_window(window, chunk, 3, eb_ref[0], lambda k: e_ref[k], ea_ref[0], exlo_ref[...], exhi_ref[...], step, last)
    start = step * chunk

    def plane(k, carry):
        v = [
            Around(
                window.at[f], k, start + k,
                ylo_ref[f, pl.ds(k, 1), :], yhi_ref[f, pl.ds(k, 1), :], zlo_ref[f], zhi_ref[f],
            )
            for f in range(3)
        ]
        e = Around(
            window.at[3], k, start + k,
            eylo_ref[pl.ds(k, 1), :], eyhi_ref[pl.ds(k, 1), :], ezlo_ref[...], ezhi_ref[...],
        )
        for j in range(3):
            advect = sum(v[i].mid * (v[j].more[i] - v[j].less[i]) for i in range(3))
            pushed = c_ref[k] * (e.more[j] - e.less[j])
            out_ref[j, k] = v[j].mid + time_step * (
                viscosity * v[j].laplace() + 0.5 * (pushed - advect)
            )
        return carry

    lax.fori_loop(0, chunk, plane, 0, unroll=2)


def cell_specs(chunk, xl, yl, zl, lead, begin=0):
    def at(block, place):
        if lead:
            return pl.BlockSpec((3, block, yl, zl), lambda i: (0, place(i + begin), 0, 0))
        return pl.BlockSpec((block, yl, zl), lambda i: (place(i + begin), 0, 0))

    return [
        at(chunk, lambda i: i),
        at(1, lambda i: jnp.maximum(i * chunk - 1, 0)),
        at(1, lambda i: jnp.minimum((i + 1) * chunk, xl - 1)),
    ]


def face_specs(chunk, yl, zl, width, fields, begin=0):
    def spec(shape, index):
        return pl.BlockSpec((fields, *shape), lambda i: (0, *index(i)))

    x_spec = spec((yl, zl), lambda i: (0, 0))
    y_spec = spec((chunk, zl), lambda i: (i + begin, 0))
    z_spec = spec((yl, width), lambda i: (0, 0))
    return [x_spec, x_spec, y_spec, y_spec, z_spec, z_spec]


def source_call(adjoint_seed, susceptibility, faces):
    xl, yl, zl = susceptibility.shape
    chunk = 16
    a, c = adjoint_seed, susceptibility
    return pl.pallas_call(
        functools.partial(source_body, chunk),
        grid=(xl // chunk,),
        in_specs=cell_specs(chunk, xl, yl, zl, True)
        + cell_specs(chunk, xl, yl, zl, False)
        + face_specs(chunk, yl, zl, lanes_of(max(xl, zl)), 7),
        out_specs=pl.BlockSpec((yl, chunk, zl), lambda i: (0, i, 0)),
        out_shape=jax.ShapeDtypeStruct((yl, xl, zl), jnp.float32),
        scratch_shapes=[pltpu.VMEM((4, chunk + 2, yl, zl), jnp.float32)],
        compiler_params=kernel_params,
    )(a, a, a, c, c, c, *faces)


def adjoint_cells_call(velocity, adjoint_seed, faces, part, earlier):
    _, xl, yl, zl = velocity.shape
    chunk = 8
    steps = xl // chunk // 2
    begin = part * steps
    specs = cell_specs(chunk, xl, yl, zl, True, begin)
    v, a = velocity, adjoint_seed
    return pl.pallas_call(
        functools.partial(adjoint_cells_body, chunk, begin, xl // chunk - 1),
        grid=(steps,),
        in_specs=specs
        + specs
        + face_specs(chunk, yl, zl, lanes_of(max(xl, zl)), 6, begin)
        + [pl.BlockSpec(memory_space=pl.ANY)] * part,
        out_specs=specs[0],
        out_shape=jax.ShapeDtypeStruct(v.shape, jnp.float32),
        scratch_shapes=[pltpu.VMEM((6, chunk + 2, yl, zl), jnp.float32)],
        input_output_aliases={12: 0} if part else {},
        compiler_params=kernel_params,
    )(v, v, v, a, a, a, *faces, *earlier)


def next_cells_call(velocity, energy, susceptibility, faces, energy_faces, part, earlier):
    xl, yl, zl = susceptibility.shape
    chunk = 8
    steps = xl // chunk // 2
    begin = part * steps
    three = cell_specs(chunk, xl, yl, zl, True, begin)
    one = cell_specs(chunk, xl, yl, zl, False, begin)
    width = lanes_of(max(xl, zl))
    energy_specs = [
        pl.BlockSpec((yl, zl), lambda i: (0, 0)),
        pl.BlockSpec((chunk, zl), lambda i: (i + begin, 0)),
        pl.BlockSpec((yl, width), lambda i: (0, 0)),
    ]
    energy_specs = [spec for spec in energy_specs for _ in range(2)]
    v, e, c = velocity, energy, susceptibility
    return pl.pallas_call(
        functools.partial(next_cells_body, chunk, begin, xl // chunk - 1),
        grid=(steps,),
        in_specs=three
        + one
        + one[:1]
        + face_specs(chunk, yl, zl, width, 3, begin)
        + energy_specs
        + [pl.BlockSpec(memory_space=pl.ANY)] * part,
        out_specs=three[0],
        out_shape=jax.ShapeDtypeStruct(v.shape, jnp.float32),
        scratch_shapes=[pltpu.VMEM((4, chunk + 2, yl, zl), jnp.float32)],
        input_output_aliases={19: 0} if part else {},
        compiler_params=kernel_params,
    )(v, v, v, e, e, e, c, *faces, *energy_faces, *earlier)


def on_device(mesh, velocity, adjoint_seed, susceptibility, remanence, region_bounds, step_id):
    plan = Plan(mesh, susceptibility.shape)
    tables = make_tables(plan)
    corner = jnp.stack([lax.axis_index(a) * n for a, n in zip(axes, susceptibility.shape)])
    bounds = region_bounds - corner[None, :]
    place = [jnp.arange(n, dtype=jnp.int32) for n in susceptibility.shape]
    inside = [(p >= bounds[0, d]) & (p < bounds[1, d]) for d, p in enumerate(place)]
    region_mask = inside[0][:, None, None] & inside[1][None, :, None] & inside[2][None, None, :]

    def end_layers(done):
        ends = [
            jnp.concatenate([velocity[:, x], adjoint_seed[:, x], susceptibility[None, x]], axis=0)
            for x in (0, plan.xl - 1)
        ]
        return ends, faces_call(velocity, adjoint_seed, susceptibility)

    def neighbours(done):
        ends, (ylo, yhi, zlo, zhi) = done[0]
        faces = [
            *to_neighbours(*ends, "gx"), *to_neighbours(ylo, yhi, "gy"), *to_neighbours(zlo, zhi, "gz"),
        ]
        return faces, places_of(plan)

    def source_of(done):
        return source_call(adjoint_seed, susceptibility, done[1][0])

    def applied_field(done):
        angle = full_turn * (step_id[0] % field_period).astype(jnp.float32) / field_period
        return jnp.stack([jnp.cos(angle), jnp.sin(angle), jnp.zeros((), jnp.float32)])

    octant, done = gather_octant(
        plan,
        magnet_call(plan, remanence, bounds),
        [end_layers, neighbours, source_of, applied_field],
    )
    _, (faces, places), source, applied = done
    own, other = field_call(plan, tables, places, octant)
    field_adjoint, energy, ylo, yhi, zlo, zhi = combine_call(applied, own, swapped(other), source)
    energy_faces = [
        *to_neighbours(energy[0], energy[-1], "gx"), *to_neighbours(ylo, yhi, "gy"), *to_neighbours(zlo, zhi, "gz"),
    ]
    field_adjoint, faces = together(field_adjoint, faces)
    half_adjoint = adjoint_cells_call(velocity, adjoint_seed, faces, 0, [])
    other, energy_faces, half_adjoint = together(swapped(field_adjoint), energy_faces, half_adjoint)
    sums = adjoint_call(plan, tables, places, field_adjoint, other)
    sums, energy, faces = together(sums, energy, faces)

    def next_cells(part):
        return lambda done: next_cells_call(
            velocity, energy, susceptibility, faces, energy_faces, part, done[:part]
        )

    def adjoint_rest(late):
        return adjoint_cells_call(velocity, adjoint_seed, late[0], 1, late[1:])

    gradient, (_, next_velocity, velocity_adjoint) = owners_sum(
        plan, sums, [next_cells(0), next_cells(1), adjoint_rest], [faces, half_adjoint]
    )
    design_gradient = jnp.where(region_mask, gradient.transpose(1, 0, 2), 0.0)
    return (next_velocity, velocity_adjoint, design_gradient)


def solution(mesh):
    cells = P(*axes)
    vectors = P(None, *axes)
    return jax.shard_map(
        functools.partial(on_device, mesh),
        mesh=mesh,
        in_specs=(vectors, vectors, cells, cells, P(), P()),
        out_specs=(vectors, vectors, cells),
        check_vma=False,
    )
```

```python
import functools
import math

import jax
import jax.numpy as jnp
import ml_dtypes
import numpy as np
from jax import lax
from jax.experimental import pallas as pl
from jax.experimental.pallas import tpu as pltpu
from jax.sharding import PartitionSpec as P

time_step = 0.5
viscosity = 0.2
field_period = 24
full_turn = 2.0 * math.pi
bf16 = ml_dtypes.bfloat16
axes = ("gx", "gy", "gz")


def wave_tables(length):
    half = length // 2
    slot = np.arange(length)
    wave = np.where(slot <= half, slot, slot - half)
    angle = full_turn * (wave[:, None] * np.arange(length)[None, :] % length) / length
    weight = np.sqrt(np.where(slot % half == 0, 1.0, 2.0) / length)[:, None]
    odd = (slot > half)[:, None]
    kappa = full_turn * wave / length
    basis = np.where(odd, np.sin(angle), np.cos(angle)) * weight
    slope = np.where(odd, np.cos(angle), -np.sin(angle)) * weight * kappa[:, None]
    slope[half] = 0.0
    return basis, slope, kappa


def two_parts(table):
    high = table.astype(bf16)
    low = (table - high.astype(np.float64)).astype(bf16)
    return high, low


def split(value):
    high = value.astype(jnp.bfloat16)
    low = (value - high.astype(jnp.float32)).astype(jnp.bfloat16)
    return high, low


def dot(left, right):
    return jnp.dot(left, right, preferred_element_type=jnp.float32)


def twice_rows(table):
    high, low = two_parts(table)
    top = np.concatenate([high, high], axis=-1)
    return np.concatenate([top, np.concatenate([low, np.zeros_like(low)], axis=-1)], axis=-2)


def dot_rows(table, values):
    both = dot(table, jnp.concatenate(split(values), axis=0))
    half = both.shape[0] // 2
    return both[:half] + both[half:]


class Plan:
    def __init__(self, mesh, local):
        self.gx, self.gy, self.gz = (mesh.shape[a] for a in axes)
        self.xl, self.yl, self.zl = local
        self.nx, self.ny, self.nz = self.xl * self.gx, self.yl * self.gy, self.zl * self.gz
        self.x2, self.y2, self.z2 = self.nx // 2, self.ny // 2, self.nz // 2
        self.kx, self.kh = self.nx // 2, self.nx // 4
        self.yc = 2 * self.yl
        self.pitch = self.kx + 8
        self.px, self.py = self.xl // 4, self.yl // 2
        self.unroll = 2 if self.py % 4 == 0 else 1
        self.relay = (self.gx, self.gy, self.gz) == (2, 8, 2)
        self.arrays = 16 if self.relay else 1
        self.segments = self.relay_segments() if self.relay else self.gathered_segments()

    def gathered_segments(self):
        size = self.py * self.px
        return [
            [
                [
                    (0, ((first * self.gy + across) * self.gz + 2 * depth + side) * size)
                    for first in range(self.gx)
                    for side in range(2)
                ]
                for depth in range(self.gz // 2)
            ]
            for across in range(self.gy)
        ]

    def relay_segments(self):
        size = self.py * self.px
        segments = []
        for at in range(0, 16, 4):
            segments.append([[(at, 0), (at, size), (at + 1, 0), (at + 1, size)]])
            segments.append([[(at + 2, 0), (at + 3, 0), (at + 2, size), (at + 3, size)]])
        return segments

    def orders(self):
        x_orders = [
            np.concatenate([np.arange(self.px) + (column ^ r) * self.px for r in range(4)])
            for column in range(4)
        ]
        y_orders = []
        for side in range(2):
            for later in range(2):
                blocks = [2 * (half ^ later) + (side ^ far) for far in range(2) for half in range(2)]
                y_orders.append(np.concatenate([np.arange(self.yl) + block * self.yl for block in blocks]))
        return x_orders, y_orders


def make_tables(plan):
    bx, dx, wx = wave_tables(plan.nx)
    by, dy, wy = wave_tables(plan.ny)
    bz, dz, wz = wave_tables(plan.nz)
    hx, hy, hz = plan.nx // 2, plan.ny // 2, plan.nz // 2
    ez = bz.copy()
    ez[0] = bz[hz]
    z1 = dz.copy()
    z1[0] = 0.0
    z2 = dz.copy()
    z2[0] = -(np.pi**2) * bz[hz]
    z3 = -(wz**2)[:, None] * bz
    z3[0] = 0.0
    z1n = np.zeros_like(z1)
    z1n[hz] = -np.pi * bz[hz]
    xs = dx.copy()
    xs[hx] = np.pi * bx[hx]
    w3 = wz.copy()
    w3[0] = np.pi
    base = wy[:, None] ** 2 + w3[None, :] ** 2
    keep = np.ones_like(base, bool)
    keep[:, 0] = False
    keep[hy, 0] = True
    base = np.where(keep, base, 1e30).astype(np.float32)
    own = [np.arange(c * plan.kh, (c + 1) * plan.kh) for c in range(2)]
    own = [np.concatenate([cosines, hx + cosines]) for cosines in own]

    def by_side(table):
        return np.stack([table[slots] for slots in own])

    fx, fy = by_side(bx[:, : plan.x2]), by[None, :, : plan.y2]
    if plan.relay:
        x_orders, y_orders = plan.orders()
        fx = np.stack([part[:, order] for part in fx for order in x_orders])
        fy = np.stack([fy[0][:, order] for order in y_orders])
    return dict(
        fx=fx,
        fy=fy,
        xb=by_side(bx),
        xs=by_side(xs),
        w1=by_side((wx**2).astype(np.float32)),
        z1n=np.stack([z1n, z1]),
        ez=ez[:, : plan.z2],
        by=by,
        dy=dy,
        z1=z1,
        z2=z2,
        z3=z3,
        base=base,
    )


def pair_lanes(*arrays):
    return jnp.concatenate(arrays, axis=1)


def pair_rows(*arrays):
    return jnp.concatenate(arrays, axis=0)


def load_plane(refs, plan, segment, i):
    blocks = [
        pair_rows(*[refs[array][pl.ds(start + i * plan.px, plan.px), :] for array, start in runs])
        for runs in segment
    ]
    return blocks[0] if len(blocks) == 1 else pair_lanes(*blocks)


def store_plane(refs, plan, segment, i, value):
    for depth, runs in enumerate(segment):
        for place, (array, start) in enumerate(runs):
            refs[array][pl.ds(start + i * plan.px, plan.px), :] = value[
                place * plan.px : (place + 1) * plan.px, depth * plan.zl : (depth + 1) * plan.zl
            ]


def field_body(
    plan, group, places_ref, w1_ref,
    fx_ref, ez_ref, fy_ref, g_ref, z13_ref, z2_ref, z1n_ref, xs_ref, xb_ref, base_ref, *refs,
):
    kx, kh, pitch = plan.kx, plan.kh, plan.pitch
    w1_at = places_ref[8] * kx
    y2, z2, xl, yl, yc, zl = plan.y2, plan.z2, plan.xl, plan.yl, plan.yc, plan.zl
    span = yc * pitch
    m_refs, (own_out, other_out, s_ref, r_ref, own_ref, other_ref, sem) = refs[: plan.arrays], refs[plan.arrays :]

    def along_x(number, segment):
        def body(step, carry):
            for pair in [plan.unroll * step + k for k in range(plan.unroll)]:
                planes = [load_plane(m_refs, plan, segment, 2 * pair + k) for k in range(2)]
                out = dot_rows(fx_ref[...], pair_lanes(*planes))
                row = (number * plan.py + 2 * pair) * pitch
                s_ref[pl.ds(row, kx), :] = out[:, :z2]
                s_ref[pl.ds(row + pitch, kx), :] = out[:, z2:]
            return carry

        lax.fori_loop(0, plan.py // 2 // plan.unroll, body, 0)

    for number, segment in enumerate(plan.segments):
        along_x(number, segment)

    def row_waves(slots):
        planes = pair_lanes(*[s_ref[pl.ds(slot, y2, stride=pitch), :] for slot in slots])
        out = dot_rows(fy_ref[...], planes)
        return [out[:, part * z2 : (part + 1) * z2] for part in range(len(slots))]

    def depth_waves(planes):
        high, low = split(pair_rows(*planes))
        return dot(pair_lanes(high, low, high), ez_ref[...])

    def one_slab(spectrum, kern):
        high, low = split(spectrum * kern)
        both = dot(g_ref[...], high)
        return both[: 2 * yc] + both[2 * yc :] + dot(g_ref[: 2 * yc], low)

    def two_products(high, low, table_ref):
        both = dot(high, table_ref[...])
        return both[:, :zl] + both[:, zl:] + dot(low, table_ref[:, :zl])

    def store(slots, cells, j):
        for place, slot in enumerate(slots):
            r_ref[pl.ds(j * span + slot, yc, stride=pitch), :] = cells[place * yc : (place + 1) * yc]

    def depth_cells(slots, slabs, edge):
        q1 = pair_rows(*[slab[:yc] for slab in slabs])
        q2 = pair_rows(*[slab[yc:] for slab in slabs])
        lane = lax.broadcasted_iota(jnp.int32, q1.shape, 1)
        q2 = jnp.where(lane == 0, q1, q2)
        high, low = split(q1)
        r13 = dot(pair_lanes(high, low, high), z13_ref[...])
        store(slots, two_products(high, low, z1n_ref) if edge else r13[:, :zl], 0)
        store(slots, r13[:, zl:], 2)
        store(slots, two_products(*split(q2), z2_ref), 1)

    def waves(step, carry):
        first = step * group
        slots = [first + k + part for k in range(group) for part in (0, kh)]
        planes = sum([row_waves(slots[2 * k : 2 * k + 2]) for k in range(group)], [])
        spectra = depth_waves(planes)
        slabs = []
        for k in range(group):
            kern = 1.0 / (base_ref[...] + w1_ref[w1_at + first + k])
            for part in range(2):
                at = (2 * k + part) * plan.ny
                slabs.append(one_slab(spectra[at : at + plan.ny], kern))
        depth_cells(slots, slabs, False)
        return carry

    lax.fori_loop(0, kh // group, waves, 0)

    spectrum = depth_waves(row_waves([kh]))
    depth_cells([kh], [one_slab(spectrum, 1.0 / (base_ref[...] + w1_ref[w1_at + kh]))], True)

    def back_x(mat_ref, values):
        return dot_rows(mat_ref[...], values)

    def cells(out_ref, shift):
        def body(pair, carry):
            here = [
                [pl.ds(j * span + (shift + 2 * pair + k) * pitch, kx) for k in range(2)]
                for j in range(3)
            ]
            h1 = back_x(xs_ref, pair_lanes(r_ref[here[0][0], :], r_ref[here[0][1], :]))
            for k in range(2):
                h23 = back_x(xb_ref, pair_lanes(r_ref[here[1][k], :], r_ref[here[2][k], :]))
                at = (2 * pair + k) * xl
                out_ref[pl.ds(at, xl), :] = h1[:, k * zl : (k + 1) * zl]
                out_ref[pl.ds(yl * xl + at, xl), :] = h23[:, :zl]
                out_ref[pl.ds(2 * yl * xl + at, xl), :] = h23[:, zl:]
            return carry

        lax.fori_loop(0, yl // 2, body, 0)

    cells(other_ref, yl)
    away = pltpu.make_async_copy(other_ref, other_out, sem.at[0])
    away.start()
    cells(own_ref, 0)
    kept = pltpu.make_async_copy(own_ref, own_out, sem.at[1])
    kept.start()
    away.wait()
    kept.wait()


def adjoint_body(
    plan, group, places_ref, w1_ref,
    fx_ref, ez_ref, fy_ref, g_ref, z13_ref, z2_ref, z1n_ref, xs_ref, xb_ref, base_ref, own_in, other_in, *refs,
):
    kx, kh, pitch = plan.kx, plan.kh, plan.pitch
    w1_at = places_ref[8] * kx
    y2, z2, xl, yl, yc, zl = plan.y2, plan.z2, plan.xl, plan.yl, plan.yc, plan.zl
    span = yc * pitch
    m_outs, (s_ref, r_ref, own_ref, other_ref, sem) = refs[: plan.arrays], refs[plan.arrays : plan.arrays + 5]
    m_refs, out_sem = refs[plan.arrays + 5 : -1], refs[-1]
    here = pltpu.make_async_copy(own_in, own_ref, sem.at[0])
    there = pltpu.make_async_copy(other_in, other_ref, sem.at[1])
    here.start()
    there.start()

    def along_x(mat_ref, values):
        return dot_rows(mat_ref[...], values)

    def cells(f_ref, shift):
        def body(pair, carry):
            here = [
                [pl.ds((j * yl + 2 * pair + k) * xl, xl) for k in range(2)] for j in range(3)
            ]
            u1 = along_x(xs_ref, pair_lanes(f_ref[here[0][0], :], f_ref[here[0][1], :]))
            for k in range(2):
                u23 = along_x(xb_ref, pair_lanes(f_ref[here[1][k], :], f_ref[here[2][k], :]))
                row = (shift + 2 * pair + k) * pitch
                r_ref[pl.ds(row, kx), :] = u1[:, k * zl : (k + 1) * zl]
                r_ref[pl.ds(span + row, kx), :] = u23[:, :zl]
                r_ref[pl.ds(2 * span + row, kx), :] = u23[:, zl:]
            return carry

        lax.fori_loop(0, yl // 2, body, 0)

    here.wait()
    cells(own_ref, 0)
    there.wait()
    cells(other_ref, yl)

    def depth_waves(slots, edge):
        u = [
            pair_rows(*[r_ref[pl.ds(j * span + slot, yc, stride=pitch), :] for slot in slots])
            for j in range(3)
        ]
        high1, low1 = split(u[0])
        high2, low2 = split(u[1])
        high3, low3 = split(u[2])
        high = pair_lanes(high1, high3)
        q1 = dot(pair_lanes(high, low1, low3, high), z13_ref[...])
        if edge:
            q1 = q1 + dot(pair_lanes(high1, low1, high1), z1n_ref[...])
        q2 = dot(pair_lanes(high2, low2, high2), z2_ref[...])
        first = lax.broadcasted_iota(jnp.int32, q1.shape, 1) == 0
        return jnp.where(first, q2, q1), jnp.where(first, 0.0, q2)

    def one_slab(q1, q2, kern):
        return dot_rows(g_ref[...], pair_rows(q1, q2)) * kern

    def depth_cells(spectra):
        high, low = split(pair_rows(*spectra))
        out = dot(high, ez_ref[...])
        return out[:, :z2] + out[:, z2:] + dot(low, ez_ref[:, :z2])

    def row_cells(slots, planes):
        high, low = split(pair_lanes(*planes))
        both = dot(fy_ref[...], high)
        out = both[:y2] + both[y2:] + dot(fy_ref[:y2], low)
        for part, slot in enumerate(slots):
            s_ref[pl.ds(slot, y2, stride=pitch), :] = out[:, part * z2 : (part + 1) * z2]

    def waves(step, carry):
        first = step * group
        slots = [first + k + part for k in range(group) for part in (0, kh)]
        q1, q2 = depth_waves(slots, False)
        spectra = []
        for k in range(group):
            kern = 1.0 / (base_ref[...] + w1_ref[w1_at + first + k])
            for part in range(2):
                take = slice((2 * k + part) * yc, (2 * k + part + 1) * yc)
                spectra.append(one_slab(q1[take], q2[take], kern))
        planes = depth_cells(spectra)
        planes = [planes[k * plan.ny : (k + 1) * plan.ny] for k in range(2 * group)]
        for k in range(group):
            row_cells(slots[2 * k : 2 * k + 2], planes[2 * k : 2 * k + 2])
        return carry

    lax.fori_loop(0, kh // group, waves, 0)

    q1, q2 = depth_waves([kh], True)
    row_cells([kh], [depth_cells([one_slab(q1, q2, 1.0 / (base_ref[...] + w1_ref[w1_at + kh]))])])

    def back_x(number, segment):
        def body(step, carry):
            for pair in [plan.unroll * step + k for k in range(plan.unroll)]:
                row = (number * plan.py + 2 * pair) * pitch
                planes = [s_ref[pl.ds(row + k * pitch, kx), :] for k in range(2)]
                out = dot_rows(fx_ref[...], pair_lanes(*planes))
                store_plane(m_refs, plan, segment, 2 * pair, out[:, :z2])
                store_plane(m_refs, plan, segment, 2 * pair + 1, out[:, z2:])
            return carry

        lax.fori_loop(0, plan.py // 2 // plan.unroll, body, 0)

    copies = [
        pltpu.make_async_copy(m_refs[k], m_outs[k], out_sem.at[k]) for k in range(plan.arrays)
    ]
    last = {array: n for n, runs in enumerate(plan.segments) for array, _ in sum(runs, [])}
    for number, segment in enumerate(plan.segments):
        back_x(number, segment)
        for array in range(plan.arrays):
            if last[array] == number:
                copies[array].start()
    for copy in copies:
        copy.wait()


vmem = pl.BlockSpec(memory_space=pltpu.VMEM)
smem = pl.BlockSpec(memory_space=pltpu.SMEM)
kernel_params = pltpu.CompilerParams(vmem_limit_bytes=60 * 2**20)


def scratch_of(plan):
    return [
        pltpu.VMEM(((plan.y2 + 1) * plan.pitch, plan.z2), jnp.float32),
        pltpu.VMEM(((3 * plan.yc + 1) * plan.pitch, plan.zl), jnp.float32),
        pltpu.VMEM((3 * plan.yl * plan.xl, plan.zl), jnp.float32),
        pltpu.VMEM((3 * plan.yl * plan.xl, plan.zl), jnp.float32),
        pltpu.SemaphoreType.DMA((2,)),
    ]


def thrice_rows(table):
    high, low = two_parts(table)
    return np.concatenate([high, high, low], axis=-2)


def blocks_of(table, count, dim):
    return np.stack(np.split(table, table.shape[dim] // count, axis=dim))


def pair_blocks(table, count, dim):
    blocks = blocks_of(table, count, dim)
    order = np.arange(len(blocks))
    return np.concatenate([blocks, blocks[order + 1 - 2 * (order % 2)]], axis=dim + 1)


def by_side_blocks(tables, count, dim):
    return np.concatenate([blocks_of(table, count, dim) for table in tables])


def parts_over(table):
    return np.concatenate(two_parts(table), axis=-2)


def parts_beside(table):
    return np.concatenate(two_parts(table), axis=-1)


def places_of(plan):
    first, second, third = [lax.axis_index(a) for a in axes]
    side = lax.rem(second, 2)
    fx, fy = side, jnp.zeros_like(side)
    if plan.relay:
        fx = 4 * side + 2 * first + third
        fy = 2 * side + jnp.minimum(second // 2, 1)
    x_place = side * plan.gx + first
    return jnp.stack([fx, fy, second, third, third, side * plan.gz + third, x_place, x_place, side])


def field_tables(plan, t):
    xl, yl, zl = plan.xl, plan.yl, plan.zl
    z13 = np.concatenate([blocks_of(t[name], zl, 1) for name in ("z1", "z3")], axis=2)
    g = np.concatenate([pair_blocks(t[name].T, yl, 0) for name in ("by", "dy")], axis=1)
    return [
        twice_rows(t["fx"]), thrice_rows(t["ez"].T), twice_rows(t["fy"]), parts_over(g), thrice_rows(z13),
        parts_beside(blocks_of(t["z2"], zl, 1)), parts_beside(by_side_blocks(t["z1n"], zl, 1)),
        twice_rows(by_side_blocks([m.T for m in t["xs"]], xl, 0)),
        twice_rows(by_side_blocks([m.T for m in t["xb"]], xl, 0)), t["base"],
    ]


def adjoint_tables(plan, t):
    xl, yl, zl = plan.xl, plan.yl, plan.zl
    z13 = np.concatenate([blocks_of(t[name].T, zl, 0) for name in ("z1", "z3")], axis=1)
    g = np.concatenate([pair_blocks(t[name], yl, 1) for name in ("by", "dy")], axis=2)
    edge = [(table - t["z1"]).T for table in t["z1n"]]
    return [
        twice_rows(t["fx"].swapaxes(1, 2)), parts_beside(t["ez"]), parts_over(t["fy"].swapaxes(1, 2)), twice_rows(g),
        thrice_rows(z13), thrice_rows(blocks_of(t["z2"].T, zl, 0)), thrice_rows(by_side_blocks(edge, zl, 0)),
        twice_rows(by_side_blocks(t["xs"], xl, 1)), twice_rows(by_side_blocks(t["xb"], xl, 1)), t["base"],
    ]


table_places = (0, None, 1, 2, 3, 4, 5, 6, 7, None)


def spectral_call(plan, body, places, w1, tables, arrays, out_shape, in_space, scratch):
    def table_spec(table, place):
        if place is None:
            return vmem
        return pl.BlockSpec((None, *table.shape[1:]), lambda i, places_ref: (places_ref[place], 0, 0))

    return pl.pallas_call(
        functools.partial(body, plan, min(8, plan.kh)),
        out_shape=out_shape,
        grid_spec=pltpu.PrefetchScalarGridSpec(
            num_scalar_prefetch=1,
            grid=(1,),
            in_specs=[smem]
            + [table_spec(table, place) for table, place in zip(tables, table_places)]
            + [pl.BlockSpec(memory_space=in_space)] * len(arrays),
            out_specs=[pl.BlockSpec(memory_space=pl.ANY)] * len(out_shape),
            scratch_shapes=scratch_of(plan) + scratch,
        ),
        compiler_params=kernel_params,
    )(places, jnp.asarray(w1.reshape(-1)), *[jnp.asarray(table) for table in tables], *arrays)


def field_call(plan, tables, places, octant):
    xl, yl, zl = plan.xl, plan.yl, plan.zl
    shape = jax.ShapeDtypeStruct((3 * yl * xl, zl), jnp.float32)
    own, other = spectral_call(
        plan, field_body, places, tables["w1"], field_tables(plan, tables), octant, [shape, shape],
        pltpu.VMEM, [],
    )
    return own.reshape(3, yl, xl, zl), other.reshape(3, yl, xl, zl)


def adjoint_call(plan, tables, places, own, other):
    zl = plan.zl
    rows = plan.x2 * plan.y2 * plan.z2 // zl // plan.arrays
    fields = [own.reshape(-1, zl), other.reshape(-1, zl)]
    shape = jax.ShapeDtypeStruct((rows, zl), jnp.float32)
    return spectral_call(
        plan, adjoint_body, places, tables["w1"], adjoint_tables(plan, tables), fields, [shape] * plan.arrays,
        pl.ANY, [pltpu.VMEM((rows, zl), jnp.float32)] * plan.arrays + [pltpu.SemaphoreType.DMA((plan.arrays,))],
    )


def swapped(array):
    count = lax.axis_size("gy")
    return lax.ppermute(array, "gy", [(i, i + 1 - 2 * (i % 2)) for i in range(count)])


def spread(block, axis, dim):
    count = lax.axis_size(axis)
    halves = jnp.split(block, 2, axis=dim)
    moved = [
        lax.ppermute(half, axis, [(s, 2 * s + k) for s in range(count // 2)])
        for k, half in enumerate(halves)
    ]
    return moved[0] + moved[1]


def unspread(piece, axis, dim):
    count = lax.axis_size(axis)
    moved = [
        lax.ppermute(piece, axis, [(2 * s + k, s) for s in range(count // 2)]) for k in range(2)
    ]
    return jnp.concatenate(moved, axis=dim)


def gather_octant(plan, quarters, work):
    if plan.relay:
        return relay_octant(plan, quarters, work)
    done = []
    for step in work:
        done.append(step(done))
    piece = jnp.concatenate([q.reshape(plan.yl, plan.px, plan.zl) for q in quarters], axis=1)
    for axis, dim in (("gx", 1), ("gz", 1), ("gy", 0)):
        piece = spread(piece, axis, dim)
    return [lax.all_gather(piece.reshape(plan.py * plan.px, plan.zl), axes, tiled=True)], done


def owners_sum(plan, sums, work, late):
    if plan.relay:
        return relay_sums(plan, sums, work, late)
    done = [work[0]([])]
    done += [work[1](done), work[2](late)]
    piece = lax.psum_scatter(sums[0], axes, scatter_dimension=0, tiled=True)
    piece = piece.reshape(plan.py, plan.px, plan.zl)
    return unspread(unspread(unspread(piece, "gy", 0), "gz", 1), "gx", 1), done


flip = [(0, 1), (1, 0)]


def along(array, pairs):
    return lax.ppermute(array, "gy", [(2 * a + c, 2 * b + c) for a, b in pairs for c in range(2)])


def together(*values):
    return lax.optimization_barrier(values)


def to_column(array, start, end):
    return lax.ppermute(array, ("gx", "gz"), [(start, end)])


def relay_octant(plan, quarters, work):
    z = lax.axis_index("gy") // 2
    done = []
    half = plan.py * plan.px
    near = [to_column(quarters[r], 0, r) for r in (1, 2)]
    via = [to_column(quarters[3][:half], 0, 1), to_column(quarters[3][half:], 0, 2)]
    via = [to_column(via[0], 1, 3), to_column(via[1], 2, 3)]
    piece = quarters[0] + near[0] + near[1] + pair_rows(*via)
    up = along(piece, [(0, 1), (1, 2)])
    down = along(piece, [(1, 0)])
    up, result = together(up, work[0](done))
    done.append(result)
    up2 = along(up, [(1, 2), (2, 3)])
    up3 = along(up2, [(2, 3)])
    first = across_once(plan, jnp.where(z < 2, piece, jnp.where(z == 2, up, up2)))
    first, result = together(first, work[1](done))
    done.append(result)
    first = across_twice(first)
    second = jnp.where(z == 0, down, jnp.where(z == 1, up, jnp.where(z == 2, up2, up3)))
    second, done[1] = together(across_once(plan, second), done[1])
    second, result = together(across_twice(second), [step(done) for step in work[2:]])
    done.extend(result)
    own = first + second
    return own + [swapped(array) for array in own], done


def across_once(plan, piece):
    half = plan.py * plan.px
    low, high = piece[:half], piece[half:]
    return pair_rows(low, lax.ppermute(low, "gz", flip)), pair_rows(high, lax.ppermute(high, "gx", flip))


def across_twice(pairs):
    a, b = pairs
    return [a, lax.ppermute(a, "gx", flip), b, lax.ppermute(b, "gz", flip)]


def across_halves(arrays):
    a, ay, b, bx = arrays
    return lax.ppermute(ay, "gx", flip), lax.ppermute(bx, "gz", flip)


def across_sums(plan, arrays, halves):
    half = plan.py * plan.px
    a, b = arrays[0] + halves[0], arrays[2] + halves[1]
    low = a[:half] + lax.ppermute(a[half:], "gz", flip)
    high = b[:half] + lax.ppermute(b[half:], "gx", flip)
    return pair_rows(low, high)


def relay_sums(plan, sums, work, late):
    z = lax.axis_index("gy") // 2
    own = [sums[i] + swapped(sums[i + 8]) for i in (4, 5, 6, 7, 0, 1, 2, 3)]
    done = []
    halves, result = together(across_halves(own[:4]), work[0](done))
    done.append(result)
    second, *own[4:] = together(across_sums(plan, own[:4], halves), *own[4:])
    down = along(second, [(3, 2)])
    up = along(second, [(0, 1)])
    halves = across_halves(own[4:])
    down, halves, result = together(down, halves, work[1](done))
    done.append(result)
    second = second + down
    down = along(second, [(2, 1)])
    first = across_sums(plan, own[4:], halves)
    down2 = along(first, [(3, 2)])
    second = second + down
    down = along(second, [(1, 0)])
    first = first + down2
    first = first + up + down + along(first, [(2, 1)])
    half = plan.py * plan.px
    first, late = together(first, late)
    near = [to_column(first, r, 0) for r in (1, 2)]
    via = [to_column(first[:half], 3, 1), to_column(first[half:], 3, 2)]
    via = [to_column(via[0], 1, 0), to_column(via[1], 2, 0)]
    near, via, result = together(near, via, work[2](late))
    done.append(result)
    quarters = [first, *near, pair_rows(*via)]
    block = jnp.concatenate([q.reshape(plan.yl, plan.px, plan.zl) for q in quarters], axis=1)
    return block, done


def magnet_body(plan, from_ref, to_ref, rem_ref, *out_refs):
    yl, px, zl = plan.yl, plan.px, plan.zl
    lane = lax.broadcasted_iota(jnp.int32, (px, zl), 1)
    row = lax.broadcasted_iota(jnp.int32, (px, zl), 0)
    in_z = (lane >= from_ref[2]) & (lane < to_ref[2])
    for r, out_ref in enumerate(out_refs):
        inside = in_z & (row + r * px >= from_ref[0]) & (row + r * px < to_ref[0])

        def plane(y, carry, inside=inside, out_ref=out_ref, r=r):
            here = inside & (y >= from_ref[1]) & (y < to_ref[1])
            values = rem_ref[pl.ds(r * px * yl + y, px, stride=yl), :]
            out_ref[pl.ds(y * px, px), :] = jnp.where(here, values, 0.0)
            return carry

        lax.fori_loop(0, yl, plane, 0, unroll=4)


def magnet_call(plan, remanence, bounds):
    shape = jax.ShapeDtypeStruct((plan.yl * plan.px, plan.zl), jnp.float32)
    return pl.pallas_call(
        functools.partial(magnet_body, plan),
        out_shape=[shape] * 4,
        in_specs=[smem, smem, vmem],
        out_specs=[vmem] * 4,
        compiler_params=kernel_params,
    )(bounds[0], bounds[1], remanence.reshape(-1, plan.zl))


def lanes_of(count):
    return -(-count // 128) * 128


def faces_body(chunk, v_ref, a_ref, c_ref, ylo_ref, yhi_ref, zlo_ref, zhi_ref):
    yl, zl = v_ref.shape[2:]
    step = pl.program_id(0)

    @pl.when(step == 0)
    def _():
        zlo_ref[...] = jnp.zeros_like(zlo_ref)
        zhi_ref[...] = jnp.zeros_like(zhi_ref)

    lane = lax.broadcasted_iota(jnp.int32, zlo_ref.shape[1:], 1)
    for field in range(7):
        low, high = zlo_ref[field], zhi_ref[field]
        for k in range(chunk):
            plane = v_ref[field, k] if field < 3 else a_ref[field - 3, k] if field < 6 else c_ref[k]
            ylo_ref[field, k : k + 1, :] = plane[:1]
            yhi_ref[field, k : k + 1, :] = plane[yl - 1 :]
            here = lane == step * chunk + k
            low = jnp.where(here, plane[:, :1], low)
            high = jnp.where(here, plane[:, zl - 1 :], high)
        zlo_ref[field] = low
        zhi_ref[field] = high


def faces_call(velocity, adjoint_seed, susceptibility):
    xl, yl, zl = susceptibility.shape
    chunk = 16
    three = pl.BlockSpec((3, chunk, yl, zl), lambda i: (0, i, 0, 0))
    y_spec = pl.BlockSpec((7, chunk, zl), lambda i: (0, i, 0))
    z_spec = pl.BlockSpec((7, yl, lanes_of(max(xl, zl))), lambda i: (0, 0, 0))
    y_shape = jax.ShapeDtypeStruct((7, xl, zl), jnp.float32)
    z_shape = jax.ShapeDtypeStruct((7, yl, lanes_of(max(xl, zl))), jnp.float32)
    return pl.pallas_call(
        functools.partial(faces_body, chunk),
        grid=(xl // chunk,),
        in_specs=[three, three, pl.BlockSpec((chunk, yl, zl), lambda i: (i, 0, 0))],
        out_specs=[y_spec, y_spec, z_spec, z_spec],
        out_shape=[y_shape, y_shape, z_shape, z_shape],
        compiler_params=kernel_params,
    )(velocity, adjoint_seed, susceptibility)


def to_neighbours(low_face, high_face, axis):
    count = lax.axis_size(axis)
    if count == 2:
        lower = lax.axis_index(axis) == 0
        other = lax.ppermute(jnp.where(lower, high_face, low_face), axis, [(0, 1), (1, 0)])
        return jnp.where(lower, 0.0, other), jnp.where(lower, other, 0.0)
    below = lax.ppermute(high_face, axis, [(i, i + 1) for i in range(count - 1)])
    above = lax.ppermute(low_face, axis, [(i + 1, i) for i in range(count - 1)])
    return below, above


def combine_body(chunk, app_ref, own_ref, arrived_ref, source_ref, f_ref, e_ref, ylo_ref, yhi_ref, zlo_ref, zhi_ref):
    yl, _, zl = source_ref.shape
    step = pl.program_id(0)

    @pl.when(step == 0)
    def _():
        zlo_ref[...] = jnp.zeros_like(zlo_ref)
        zhi_ref[...] = jnp.zeros_like(zhi_ref)

    energy = 0.0
    for j in range(3):
        total = own_ref[j] + arrived_ref[j] + app_ref[j]
        f_ref[j] = source_ref[...] * total
        energy = energy + total * total
    energy = 0.5 * energy
    lane = lax.broadcasted_iota(jnp.int32, zlo_ref.shape, 1)
    low, high = zlo_ref[...], zhi_ref[...]
    for k in range(chunk):
        plane = energy[:, k, :]
        e_ref[k] = plane
        ylo_ref[k : k + 1, :] = plane[:1]
        yhi_ref[k : k + 1, :] = plane[yl - 1 :]
        here = lane == step * chunk + k
        low = jnp.where(here, plane[:, :1], low)
        high = jnp.where(here, plane[:, zl - 1 :], high)
    zlo_ref[...] = low
    zhi_ref[...] = high


def combine_call(applied, own, arrived, source):
    _, yl, xl, zl = own.shape
    chunk = 32
    width = lanes_of(max(xl, zl))
    three = pl.BlockSpec((3, yl, chunk, zl), lambda i: (0, 0, i, 0))
    y_spec = pl.BlockSpec((chunk, zl), lambda i: (i, 0))
    z_spec = pl.BlockSpec((yl, width), lambda i: (0, 0))
    shapes = [(3, yl, xl, zl), (xl, yl, zl), (xl, zl), (xl, zl), (yl, width), (yl, width)]
    return pl.pallas_call(
        functools.partial(combine_body, chunk),
        grid=(xl // chunk,),
        in_specs=[smem, three, three, pl.BlockSpec((yl, chunk, zl), lambda i: (0, i, 0))],
        out_specs=[
            three, pl.BlockSpec((chunk, yl, zl), lambda i: (i, 0, 0)), y_spec, y_spec, z_spec, z_spec,
        ],
        out_shape=[jax.ShapeDtypeStruct(shape, jnp.float32) for shape in shapes],
        compiler_params=kernel_params,
    )(applied, own, arrived, source)


class Around:
    def __init__(self, ref, k, x, y_below, y_above, z_below, z_above):
        mid = ref[k + 1]
        yl, zl = mid.shape
        row = lax.broadcasted_iota(jnp.int32, mid.shape, 0)
        lane = lax.broadcasted_iota(jnp.int32, mid.shape, 1)
        width = z_below.shape[1]
        left = pltpu.roll(z_below, lax.rem(width - x, width), 1)[:, :zl]
        right = pltpu.roll(z_above, lax.rem(width + zl - 1 - x, width), 1)[:, :zl]
        self.mid = mid
        self.less = [
            ref[k],
            jnp.where(row == 0, y_below, pltpu.roll(mid, 1, 0)),
            jnp.where(lane == 0, left, pltpu.roll(mid, 1, 1)),
        ]
        self.more = [
            ref[k + 2],
            jnp.where(row == yl - 1, y_above, pltpu.roll(mid, yl - 1, 0)),
            jnp.where(lane == zl - 1, right, pltpu.roll(mid, zl - 1, 1)),
        ]

    def slope(self, d):
        return (self.more[d] - self.less[d]) * 0.5

    def laplace(self):
        beside = self.more[0] + self.less[0] + self.more[1] + self.less[1]
        return beside + self.more[2] + self.less[2] - 6.0 * self.mid


def fill_window(window, chunk, field, before, block, after, x_below, x_above, step=None, last=None):
    step = pl.program_id(0) if step is None else step
    last = pl.num_programs(0) - 1 if last is None else last
    for k in range(chunk):
        window[field, k + 1] = block(k)
    window[field, 0] = jnp.where(step == 0, x_below, before)
    window[field, chunk + 1] = jnp.where(step == last, x_above, after)


def source_body(
    chunk, a_ref, ab_ref, aa_ref, c_ref, cb_ref, ca_ref,
    xlo_ref, xhi_ref, ylo_ref, yhi_ref, zlo_ref, zhi_ref, source_ref, window,
):
    for j in range(3):
        fill_window(window, chunk, j, ab_ref[j, 0], lambda k: a_ref[j, k], aa_ref[j, 0], xlo_ref[3 + j], xhi_ref[3 + j])
    fill_window(window, chunk, 3, cb_ref[0], lambda k: c_ref[k], ca_ref[0], xlo_ref[6], xhi_ref[6])
    start = pl.program_id(0) * chunk

    def plane(k, carry):
        at = [
            Around(
                window.at[f], k, start + k,
                ylo_ref[3 + f, pl.ds(k, 1), :], yhi_ref[3 + f, pl.ds(k, 1), :], zlo_ref[3 + f], zhi_ref[3 + f],
            )
            for f in range(4)
        ]
        a, c = at[:3], at[3]
        flux = [c.more[i] * a[i].more[i] - c.less[i] * a[i].less[i] for i in range(3)]
        source_ref[:, k, :] = (-0.5 * time_step) * (flux[0] + flux[1] + flux[2])
        return carry

    lax.fori_loop(0, chunk, plane, 0, unroll=4)


def adjoint_cells_body(
    chunk, begin, last, v_ref, vb_ref, va_ref, a_ref, ab_ref, aa_ref,
    xlo_ref, xhi_ref, ylo_ref, yhi_ref, zlo_ref, zhi_ref, *refs,
):
    out_ref, window = refs[-2:]
    step = pl.program_id(0) + begin
    for j in range(3):
        fill_window(window, chunk, j, vb_ref[j, 0], lambda k: v_ref[j, k], va_ref[j, 0], xlo_ref[j], xhi_ref[j], step, last)
        fill_window(window, chunk, 3 + j, ab_ref[j, 0], lambda k: a_ref[j, k], aa_ref[j, 0], xlo_ref[3 + j], xhi_ref[3 + j], step, last)
    start = step * chunk

    def plane(k, carry):
        at = [
            Around(
                window.at[f], k, start + k,
                ylo_ref[f, pl.ds(k, 1), :], yhi_ref[f, pl.ds(k, 1), :], zlo_ref[f], zhi_ref[f],
            )
            for f in range(6)
        ]
        v, a = at[:3], at[3:]
        for j in range(3):
            shear = sum(a[i].mid * (v[i].more[j] - v[i].less[j]) for i in range(3))
            carried = sum(v[i].more[i] * a[j].more[i] - v[i].less[i] * a[j].less[i] for i in range(3))
            out_ref[j, k] = a[j].mid + time_step * (
                viscosity * a[j].laplace() + 0.5 * (carried - shear)
            )
        return carry

    lax.fori_loop(0, chunk, plane, 0, unroll=4)


def next_cells_body(
    chunk, begin, last, v_ref, vb_ref, va_ref, e_ref, eb_ref, ea_ref, c_ref,
    xlo_ref, xhi_ref, ylo_ref, yhi_ref, zlo_ref, zhi_ref,
    exlo_ref, exhi_ref, eylo_ref, eyhi_ref, ezlo_ref, ezhi_ref, *refs,
):
    out_ref, window = refs[-2:]
    step = pl.program_id(0) + begin
    for j in range(3):
        fill_window(window, chunk, j, vb_ref[j, 0], lambda k: v_ref[j, k], va_ref[j, 0], xlo_ref[j], xhi_ref[j], step, last)
    fill_window(window, chunk, 3, eb_ref[0], lambda k: e_ref[k], ea_ref[0], exlo_ref[...], exhi_ref[...], step, last)
    start = step * chunk

    def plane(k, carry):
        v = [
            Around(
                window.at[f], k, start + k,
                ylo_ref[f, pl.ds(k, 1), :], yhi_ref[f, pl.ds(k, 1), :], zlo_ref[f], zhi_ref[f],
            )
            for f in range(3)
        ]
        e = Around(
            window.at[3], k, start + k,
            eylo_ref[pl.ds(k, 1), :], eyhi_ref[pl.ds(k, 1), :], ezlo_ref[...], ezhi_ref[...],
        )
        for j in range(3):
            advect = sum(v[i].mid * (v[j].more[i] - v[j].less[i]) for i in range(3))
            pushed = c_ref[k] * (e.more[j] - e.less[j])
            out_ref[j, k] = v[j].mid + time_step * (
                viscosity * v[j].laplace() + 0.5 * (pushed - advect)
            )
        return carry

    lax.fori_loop(0, chunk, plane, 0, unroll=2)


def cell_specs(chunk, xl, yl, zl, lead, begin=0):
    def at(block, place):
        if lead:
            return pl.BlockSpec((3, block, yl, zl), lambda i: (0, place(i + begin), 0, 0))
        return pl.BlockSpec((block, yl, zl), lambda i: (place(i + begin), 0, 0))

    return [
        at(chunk, lambda i: i),
        at(1, lambda i: jnp.maximum(i * chunk - 1, 0)),
        at(1, lambda i: jnp.minimum((i + 1) * chunk, xl - 1)),
    ]


def face_specs(chunk, yl, zl, width, fields, begin=0):
    def spec(shape, index):
        return pl.BlockSpec((fields, *shape), lambda i: (0, *index(i)))

    x_spec = spec((yl, zl), lambda i: (0, 0))
    y_spec = spec((chunk, zl), lambda i: (i + begin, 0))
    z_spec = spec((yl, width), lambda i: (0, 0))
    return [x_spec, x_spec, y_spec, y_spec, z_spec, z_spec]


def source_call(adjoint_seed, susceptibility, faces):
    xl, yl, zl = susceptibility.shape
    chunk = 16
    a, c = adjoint_seed, susceptibility
    return pl.pallas_call(
        functools.partial(source_body, chunk),
        grid=(xl // chunk,),
        in_specs=cell_specs(chunk, xl, yl, zl, True)
        + cell_specs(chunk, xl, yl, zl, False)
        + face_specs(chunk, yl, zl, lanes_of(max(xl, zl)), 7),
        out_specs=pl.BlockSpec((yl, chunk, zl), lambda i: (0, i, 0)),
        out_shape=jax.ShapeDtypeStruct((yl, xl, zl), jnp.float32),
        scratch_shapes=[pltpu.VMEM((4, chunk + 2, yl, zl), jnp.float32)],
        compiler_params=kernel_params,
    )(a, a, a, c, c, c, *faces)


def adjoint_cells_call(velocity, adjoint_seed, faces, part, earlier):
    _, xl, yl, zl = velocity.shape
    chunk = 8
    steps = xl // chunk // 2
    begin = part * steps
    specs = cell_specs(chunk, xl, yl, zl, True, begin)
    v, a = velocity, adjoint_seed
    return pl.pallas_call(
        functools.partial(adjoint_cells_body, chunk, begin, xl // chunk - 1),
        grid=(steps,),
        in_specs=specs
        + specs
        + face_specs(chunk, yl, zl, lanes_of(max(xl, zl)), 6, begin)
        + [pl.BlockSpec(memory_space=pl.ANY)] * part,
        out_specs=specs[0],
        out_shape=jax.ShapeDtypeStruct(v.shape, jnp.float32),
        scratch_shapes=[pltpu.VMEM((6, chunk + 2, yl, zl), jnp.float32)],
        input_output_aliases={12: 0} if part else {},
        compiler_params=kernel_params,
    )(v, v, v, a, a, a, *faces, *earlier)


def next_cells_call(velocity, energy, susceptibility, faces, energy_faces, part, earlier):
    xl, yl, zl = susceptibility.shape
    chunk = 8
    steps = xl // chunk // 2
    begin = part * steps
    three = cell_specs(chunk, xl, yl, zl, True, begin)
    one = cell_specs(chunk, xl, yl, zl, False, begin)
    width = lanes_of(max(xl, zl))
    energy_specs = [
        pl.BlockSpec((yl, zl), lambda i: (0, 0)),
        pl.BlockSpec((chunk, zl), lambda i: (i + begin, 0)),
        pl.BlockSpec((yl, width), lambda i: (0, 0)),
    ]
    energy_specs = [spec for spec in energy_specs for _ in range(2)]
    v, e, c = velocity, energy, susceptibility
    return pl.pallas_call(
        functools.partial(next_cells_body, chunk, begin, xl // chunk - 1),
        grid=(steps,),
        in_specs=three
        + one
        + one[:1]
        + face_specs(chunk, yl, zl, width, 3, begin)
        + energy_specs
        + [pl.BlockSpec(memory_space=pl.ANY)] * part,
        out_specs=three[0],
        out_shape=jax.ShapeDtypeStruct(v.shape, jnp.float32),
        scratch_shapes=[pltpu.VMEM((4, chunk + 2, yl, zl), jnp.float32)],
        input_output_aliases={19: 0} if part else {},
        compiler_params=kernel_params,
    )(v, v, v, e, e, e, c, *faces, *energy_faces, *earlier)


def on_device(mesh, velocity, adjoint_seed, susceptibility, remanence, region_bounds, step_id):
    plan = Plan(mesh, susceptibility.shape)
    tables = make_tables(plan)
    corner = jnp.stack([lax.axis_index(a) * n for a, n in zip(axes, susceptibility.shape)])
    bounds = region_bounds - corner[None, :]
    place = [jnp.arange(n, dtype=jnp.int32) for n in susceptibility.shape]
    inside = [(p >= bounds[0, d]) & (p < bounds[1, d]) for d, p in enumerate(place)]
    region_mask = inside[0][:, None, None] & inside[1][None, :, None] & inside[2][None, None, :]

    def end_layers(done):
        ends = [
            jnp.concatenate([velocity[:, x], adjoint_seed[:, x], susceptibility[None, x]], axis=0)
            for x in (0, plan.xl - 1)
        ]
        return ends, faces_call(velocity, adjoint_seed, susceptibility)

    def neighbours(done):
        ends, (ylo, yhi, zlo, zhi) = done[0]
        faces = [
            *to_neighbours(*ends, "gx"), *to_neighbours(ylo, yhi, "gy"), *to_neighbours(zlo, zhi, "gz"),
        ]
        return faces, places_of(plan)

    def source_of(done):
        return source_call(adjoint_seed, susceptibility, done[1][0])

    def applied_field(done):
        angle = full_turn * (step_id[0] % field_period).astype(jnp.float32) / field_period
        return jnp.stack([jnp.cos(angle), jnp.sin(angle), jnp.zeros((), jnp.float32)])

    octant, done = gather_octant(
        plan,
        magnet_call(plan, remanence, bounds),
        [end_layers, neighbours, source_of, applied_field],
    )
    _, (faces, places), source, applied = done
    own, other = field_call(plan, tables, places, octant)
    field_adjoint, energy, ylo, yhi, zlo, zhi = combine_call(applied, own, swapped(other), source)
    energy_faces = [
        *to_neighbours(energy[0], energy[-1], "gx"), *to_neighbours(ylo, yhi, "gy"), *to_neighbours(zlo, zhi, "gz"),
    ]
    field_adjoint, faces = together(field_adjoint, faces)
    half_adjoint = adjoint_cells_call(velocity, adjoint_seed, faces, 0, [])
    other, energy_faces, half_adjoint = together(swapped(field_adjoint), energy_faces, half_adjoint)
    sums = adjoint_call(plan, tables, places, field_adjoint, other)
    sums, energy, faces = together(sums, energy, faces)

    def next_cells(part):
        return lambda done: next_cells_call(
            velocity, energy, susceptibility, faces, energy_faces, part, done[:part]
        )

    def adjoint_rest(late):
        return adjoint_cells_call(velocity, adjoint_seed, late[0], 1, late[1:])

    gradient, (_, next_velocity, velocity_adjoint) = owners_sum(
        plan, sums, [next_cells(0), next_cells(1), adjoint_rest], [faces, half_adjoint]
    )
    design_gradient = jnp.where(region_mask, gradient.transpose(1, 0, 2), 0.0)
    return (next_velocity, velocity_adjoint, design_gradient)


def solution(mesh):
    cells = P(*axes)
    vectors = P(None, *axes)
    return jax.shard_map(
        functools.partial(on_device, mesh),
        mesh=mesh,
        in_specs=(vectors, vectors, cells, cells, P(), P()),
        out_specs=(vectors, vectors, cells),
        check_vma=False,
    )
```
